256 devices in a mesh: seq: 64 (over x_hi, z, y), head: 4 (over x_lo, core).
Axes of the slice: x: 4 (x_hi: 2, x_lo: 2; x = x_hi * 2 + x_lo), y: 4, z: 8, core: 2. Of those that a mesh axis runs over, the one named last changes fastest.
Arguments:
- queries: bfloat16 [8192, 2560], P('seq', 'head'), may hold values from -240 to 240
- keys: bfloat16 [8192, 2560], P('seq', 'head'), may hold values from -6 to 6
- values: bfloat16 [8192, 2560], P('seq', 'head'), may hold values from -6 to 6
- frame_mask: int32 [64, 64], replicated, may hold values from 0 to 1, as said below
- w_out: bfloat16 [2560, 5120], P('head'), may hold values from -0.125 to 0.125
Outputs:
- projected: bfloat16 [8192, 5120], P('seq', 'head')
The draws below stay inside these ranges and needn't reach their ends.
Inputs may be any that keep to these rules, and one draw needn't show every extreme that they name: `frame_mask`: every frame block may attend to itself and to the blocks one away; blocks 0 and 32 may attend to each other; no block attends to a block more than 32 blocks away.
All inputs are finite; a program needn't handle non-finite values.
Results may differ from the reference program's by a relative error of at most 0.015.
Values may be sent and summed in bfloat16 or wider, within the bound.
No kernel may reach another device: no remote copies, remote signals or barrier semaphores. Data moves between devices by JAX's collectives and lax.ppermute only.
A program may use at most 128 MiB of HBM per device.

```python
import jax
import jax.numpy as jnp
from jax import lax

D = 5120
HEAD_DIM = 128
HEADS = 20
TOK_DEV = 128
NBLK = 64
REACH = 32
TOKENS = 8192


def base_keys(key):
    drawn = jax.random.normal(key, (TOKENS, HEADS * HEAD_DIM), jnp.float32)
    return jnp.clip(drawn, -6.0, 6.0)


def draw_keys(key, part):
    shared = base_keys(key)
    return shared.astype(jnp.bfloat16)


def draw_queries(key, part):
    key = jax.random.fold_in(key, 11)
    fresh = jnp.clip(jax.random.normal(key, (TOKENS, HEADS * HEAD_DIM), jnp.float32), -6.0, 6.0)
    return fresh.astype(jnp.bfloat16)


def draw_frame_mask(key, part):
    key = jax.random.fold_in(key, 5)
    rows = jnp.arange(NBLK, dtype=jnp.int32)[:, None]
    cols = jnp.arange(NBLK, dtype=jnp.int32)[None, :]
    distance = jnp.abs(rows - cols)
    ticket = jax.random.randint(key, (NBLK, NBLK), 0, 1024, dtype=jnp.int32)
    far_pair = (rows == 0) & (cols == REACH) | (rows == REACH) & (cols == 0)
    chosen = (distance <= 1) | far_pair | (distance <= REACH) & (ticket * distance < 1024)
    return jnp.where(chosen, 1, 0).astype(jnp.int32)


def levels(own_key, extent, pieces, low, high):
    gain = 1.0
    for dim, shards_of in pieces:
        draws = jax.random.uniform(jax.random.fold_in(jax.random.fold_in(own_key, 6), dim), (shards_of,), jnp.float32, low / len(pieces), high / len(pieces))
        gain = gain * jnp.repeat(jnp.exp(draws), extent[dim] // shards_of).reshape((-1,) + (1,) * (len(extent) - 1 - dim))
    return gain


def normal_values(key, shape, width, reach, shards=(), held_as=jnp.bfloat16):
    loudness = levels(key, shape, shards, -0.22, 0.18) if shards else 1.0
    array = jax.random.normal(key, shape, jnp.float32) * width * loudness
    return jnp.minimum(jnp.maximum(array, -reach), reach).astype(held_as)


def setup_inputs(seed: int = 0) -> dict:
    splits = jax.random.split(jax.random.key(seed), 6)
    return {
        "queries": draw_queries(jax.random.fold_in(splits[5], 71), 0),
        "keys": draw_keys(jax.random.fold_in(splits[5], 71), 0),
        "values": normal_values(splits[2], (TOKENS, HEADS * HEAD_DIM), 1.0, 6.0, ((0, 64), (1, 4))),
        "frame_mask": draw_frame_mask(jax.random.fold_in(splits[5], 71), 0),
        "w_out": normal_values(splits[4], (HEADS * HEAD_DIM, D), (HEADS * HEAD_DIM) ** -0.5, 0.125, ((0, 4),)),
    }


def reference(queries, keys, values, frame_mask, w_out):
    scale = HEAD_DIM ** -0.5
    query_blocks = queries.reshape(NBLK, TOK_DEV, HEADS, HEAD_DIM)
    key_heads = keys.reshape(TOKENS, HEADS, HEAD_DIM).astype(jnp.float32)
    value_heads = values.reshape(TOKENS, HEADS, HEAD_DIM).astype(jnp.float32)
    owner = (jnp.arange(TOKENS) // TOK_DEV).astype(jnp.int32)

    def one_block(inputs):
        query_block, mask_row = inputs
        live = mask_row[owner] > 0
        scores = jnp.einsum('thd,uhd->htu', query_block.astype(jnp.float32), key_heads) * scale
        scores = jnp.where(live[None, None, :], scores, -jnp.inf)
        top = jnp.max(scores, axis=-1, keepdims=True)
        expo = jnp.exp(scores - top)
        total = jnp.sum(expo, axis=-1, keepdims=True)
        rounded = lax.optimization_barrier(expo.astype(jnp.bfloat16))
        mixed = jnp.einsum('htu,uhd->htd', rounded.astype(jnp.float32), value_heads) / total
        mixed = jnp.transpose(mixed, (1, 0, 2)).astype(jnp.bfloat16)
        return mixed.reshape(TOK_DEV, HEADS * HEAD_DIM)

    attended = lax.map(one_block, (query_blocks, frame_mask)).reshape(TOKENS, HEADS * HEAD_DIM)
    return jnp.dot(attended, w_out, preferred_element_type=jnp.float32).astype(jnp.bfloat16)
```

```python
import jax
import jax.numpy as jnp
from jax import lax
from jax.experimental import pallas as pl
from jax.experimental.pallas import tpu as pltpu
from jax.sharding import Mesh
from jax.sharding import PartitionSpec as P

HEAD_DIM = 128
BLOCK = 128
HEADS = 5
XH, NZ, NY, XL, NC = 2, 8, 4, 2, 2
ROW = NZ
KEYS = XH * NZ * NY
CHUNK = 4
LOW = -1e30
EXP2_SCALE = HEAD_DIM ** (-0.5) * 1.4426950408889634


def shift(size, by):
    return [(i, (i + by) % size) for i in range(size)]


def swap_planes(x):
    pairs = [((0, 0), (0, 0)), ((1, 1), (1, 1)), ((0, 1), (1, 0)), ((1, 0), (0, 1))]
    return lax.ppermute(x, ("xh", "c"), [(a * 2 + b, d * 2 + e) for (a, b), (d, e) in pairs])


def attend_kernel(count_ref, list_ref, q_ref, *refs):
    sources, out_ref, kv_ref, s_ref, sems = refs[:8], refs[8], refs[9], refs[10], refs[11]
    copies = [
        pltpu.make_async_copy(sources[i], kv_ref.at[pl.ds(i * NZ, NZ)], sems.at[i])
        for i in range(8)
    ]
    for copy in copies:
        copy.start()
    for copy in copies:
        copy.wait()

    def one_query_block(index, carry):
        query = q_ref[index]
        live = count_ref[index]
        steps = (live + (CHUNK - 1)) // CHUNK

        def score(step, top):
            for u in range(CHUNK):
                i = step * CHUNK + u
                key = kv_ref[list_ref[index, i], 0:BLOCK, :]
                s = lax.dot_general(
                    query, key, (((1,), (1,)), ((), ())), preferred_element_type=jnp.float32
                )
                s = jnp.where(i < live, s, LOW)
                s_ref[i] = s
                top = jnp.maximum(top, s)
            return top

        top = lax.fori_loop(0, steps, score, jnp.full((BLOCK, BLOCK), LOW, jnp.float32))
        top = jnp.max(top, axis=1, keepdims=True)

        def mix(step, state):
            total, accum = state
            for u in range(CHUNK):
                i = step * CHUNK + u
                value = kv_ref[list_ref[index, i], BLOCK : 2 * BLOCK, :]
                weight = jnp.exp2((s_ref[i] - top) * EXP2_SCALE)
                total = total + weight
                accum = accum + jnp.dot(
                    weight.astype(jnp.bfloat16), value, preferred_element_type=jnp.float32
                )
            return total, accum

        zero = jnp.zeros((BLOCK, BLOCK), jnp.float32)
        total, accum = lax.fori_loop(0, steps, mix, (zero, zero))
        total = jnp.sum(total, axis=1, keepdims=True)
        out_ref[index] = (accum / total).astype(jnp.bfloat16)
        return carry

    lax.fori_loop(0, ROW, one_query_block, 0)


def attend(count, live_list, query, parts):
    return pl.pallas_call(
        attend_kernel,
        out_shape=jax.ShapeDtypeStruct((ROW, BLOCK, HEAD_DIM), jnp.bfloat16),
        in_specs=[
            pl.BlockSpec(memory_space=pltpu.SMEM),
            pl.BlockSpec(memory_space=pltpu.SMEM),
            pl.BlockSpec(memory_space=pltpu.VMEM),
        ]
        + [pl.BlockSpec(memory_space=pl.ANY)] * 8,
        out_specs=pl.BlockSpec(memory_space=pltpu.VMEM),
        scratch_shapes=[
            pltpu.VMEM((KEYS, 2 * BLOCK, HEAD_DIM), jnp.bfloat16),
            pltpu.VMEM((KEYS, BLOCK, BLOCK), jnp.float32),
            pltpu.SemaphoreType.DMA((8,)),
        ],
        compiler_params=pltpu.CompilerParams(vmem_limit_bytes=24 * 1024 * 1024),
    )(count, live_list, query, *parts)


def live_lists(frame_mask):
    y, c = lax.axis_index("y"), lax.axis_index("c")
    z = jnp.arange(NZ, dtype=jnp.int32)
    own = 32 * c + 4 * z + y
    order = []
    for back in range(NY):
        for plane in (c, 1 - c):
            order.append(32 * plane + 4 * z + (y - back) % NY)
    order = jnp.concatenate(order)
    ids = jnp.arange(KEYS, dtype=jnp.int32)
    rows = jnp.sum(jnp.where(own[:, None, None] == ids[None, :, None], frame_mask[None], 0), axis=1)
    hit = jnp.sum(jnp.where(order[:, None] == ids[None, :], 1, 0)[None] * rows[:, None, :], axis=2)
    hit = jnp.where(hit > 0, 1, 0)
    before = jnp.sum(
        jnp.where(ids[None, None, :] < ids[None, :, None], 1, 0) * hit[:, None, :], axis=2
    )
    place = (before[:, None, :] == ids[None, :, None]) & (hit[:, None, :] > 0)
    lists = jnp.sum(jnp.where(place, ids[None, None, :], 0), axis=2)
    return jnp.sum(hit, axis=1).astype(jnp.int32), lists.astype(jnp.int32)


def heads_first(x):
    return jnp.transpose(x.reshape(BLOCK, HEADS, HEAD_DIM), (1, 0, 2))


def local(queries, keys, values, frame_mask, w_out):
    xl, c = lax.axis_index("xl"), lax.axis_index("c")
    count, lists = live_lists(frame_mask)
    qkv = jnp.concatenate([heads_first(queries), heads_first(keys), heads_first(values)], axis=1)
    qkv = swap_planes(qkv)
    qkv = jnp.concatenate([qkv, jnp.zeros((NZ - HEADS,) + qkv.shape[1:], qkv.dtype)], axis=0)
    qkv = lax.all_to_all(qkv, "z", 0, 0, tiled=True)
    query, kv = qkv[:, :BLOCK], qkv[:, BLOCK:]
    columns = [kv] + [lax.ppermute(kv, "y", shift(NY, by)) for by in (1, 2, 3)]
    parts = []
    for column in columns:
        parts += [column, lax.ppermute(column, "c", shift(NC, 1))]
    attended = attend(count, lists, query, parts)
    attended = lax.all_to_all(attended, "z", 0, 0, tiled=True)[:HEADS]
    attended = swap_planes(attended)
    attended = jnp.transpose(attended, (1, 0, 2)).reshape(BLOCK, HEADS * HEAD_DIM)

    width = w_out.shape[1] // 4

    def project(to_xl, to_c):
        w = lax.dynamic_slice(
            w_out, (0, (to_xl * 2 + to_c) * width), (HEADS * HEAD_DIM, width)
        )
        return jnp.dot(attended, w, preferred_element_type=jnp.float32)

    def over_cores(to_xl):
        sent = lax.ppermute(project(to_xl, 1 - c).astype(jnp.bfloat16), "c", shift(NC, 1))
        return project(to_xl, c) + sent.astype(jnp.float32)

    far = lax.ppermute(over_cores(1 - xl).astype(jnp.bfloat16), "xl", shift(XL, 1))
    near = over_cores(xl)
    return (near + far.astype(jnp.float32)).astype(jnp.bfloat16)


def solution(mesh):
    fine = Mesh(mesh.devices.reshape(XH, NZ, NY, XL, NC), ("xh", "z", "y", "xl", "c"))
    seq, head = ("xh", "z", "y"), ("xl", "c")
    in_specs = (P(seq, head), P(seq, head), P(seq, head), P(), P(head, None))
    return jax.shard_map(
        local, mesh=fine, in_specs=in_specs, out_specs=P(seq, head), check_vma=False
    )
```

```python
import jax
import jax.numpy as jnp
from jax import lax
from jax.experimental import pallas as pl
from jax.experimental.pallas import tpu as pltpu
from jax.sharding import Mesh
from jax.sharding import PartitionSpec as P

HEAD_DIM = 128
BLOCK = 128
HALF = 64
HEADS = 5
XH, NZ, NY, XL, NC = 2, 8, 4, 2, 2
ROWS = XH * NZ
TILES = ROWS * ROWS // 2
UNROLL = 4
TILE_N = 256
LOW = -1e30
EXP2_SCALE = HEAD_DIM ** (-0.5) * 1.4426950408889634
MIB = 1024 * 1024


def shift(size, by):
    return [(i, (i + by) % size) for i in range(size)]


def in_vmem(count):
    return [pl.BlockSpec(memory_space=pltpu.VMEM)] * count


def in_smem(count):
    return [pl.BlockSpec(memory_space=pltpu.SMEM)] * count


def split_kernel(core_ref, q_ref, k_ref, v_ref, keep_ref, send_ref):
    core = core_ref[0]
    mine = pl.ds(pl.multiple_of(core * HALF, HALF), HALF)
    other = pl.ds(pl.multiple_of((1 - core) * HALF, HALF), HALF)
    keep_ref[...] = jnp.zeros_like(keep_ref)
    for head in range(HEADS):
        lanes = slice(head * HEAD_DIM, (head + 1) * HEAD_DIM)
        for t, ref in enumerate((q_ref, k_ref, v_ref)):
            rows = slice(t * HALF, (t + 1) * HALF)
            keep_ref[core * NZ + head, rows, :] = ref[mine, lanes]
            send_ref[head, rows, :] = ref[other, lanes]


def split(core, queries, keys, values):
    return pl.pallas_call(
        split_kernel,
        out_shape=(
            jax.ShapeDtypeStruct((ROWS, 3 * HALF, HEAD_DIM), jnp.bfloat16),
            jax.ShapeDtypeStruct((HEADS, 3 * HALF, HEAD_DIM), jnp.bfloat16),
        ),
        in_specs=in_smem(1) + in_vmem(3),
        out_specs=tuple(in_vmem(2)),
    )(core, queries, keys, values)


def column_kernel(first, count_ref, table_ref, q_ref, kv_ref, *refs):
    if first:
        m_ref, l_ref, a_ref, s_ref, top_ref = refs
    else:
        m_in, l_in, a_in, m_ref, l_ref, a_ref, s_ref, top_ref = refs
    steps = (count_ref[0] + (UNROLL - 1)) // UNROLL
    lane = lax.broadcasted_iota(jnp.int32, (BLOCK, BLOCK), 1)
    top_ref[...] = jnp.full(top_ref.shape, LOW, jnp.float32)

    def score(step, carry):
        tiles = []
        for u in range(UNROLL):
            e = step * UNROLL + u
            key = jnp.concatenate(
                [kv_ref[table_ref[1, e], :HALF, :], kv_ref[table_ref[2, e], :HALF, :]], axis=0
            )
            s = lax.dot_general(
                q_ref[table_ref[0, e]],
                key,
                (((1,), (1,)), ((), ())),
                preferred_element_type=jnp.float32,
            )
            s = jnp.where(lane < table_ref[3, e], s, LOW)
            s_ref[e] = s
            tiles.append(s)
        for u in range(UNROLL):
            block = table_ref[0, step * UNROLL + u]
            top_ref[block] = jnp.maximum(top_ref[block], tiles[u])
        return carry

    lax.fori_loop(0, steps, score, 0)

    for block in range(ROWS):
        top = jnp.max(top_ref[block], axis=1, keepdims=True)
        if first:
            m_ref[block] = jnp.broadcast_to(top, (BLOCK, BLOCK))
            l_ref[block] = jnp.zeros((BLOCK, BLOCK), jnp.float32)
            a_ref[block] = jnp.zeros((BLOCK, HEAD_DIM), jnp.float32)
        else:
            new = jnp.maximum(m_in[block], top)
            fade = jnp.exp2((m_in[block] - new) * EXP2_SCALE)
            m_ref[block] = new
            l_ref[block] = l_in[block] * fade
            a_ref[block] = a_in[block] * fade

    def mix(step, carry):
        weights, products = [], []
        for u in range(UNROLL):
            e = step * UNROLL + u
            value = jnp.concatenate(
                [kv_ref[table_ref[1, e], HALF:, :], kv_ref[table_ref[2, e], HALF:, :]], axis=0
            )
            weight = jnp.exp2((s_ref[e] - m_ref[table_ref[0, e]]) * EXP2_SCALE)
            weights.append(weight)
            products.append(
                jnp.dot(weight.astype(jnp.bfloat16), value, preferred_element_type=jnp.float32)
            )
        for u in range(UNROLL):
            block = table_ref[0, step * UNROLL + u]
            l_ref[block] = l_ref[block] + weights[u]
            a_ref[block] = a_ref[block] + products[u]
        return carry

    lax.fori_loop(0, steps, mix, 0)


def attend_column(count, table, query, kv, state):
    first = state is None
    shape = jax.ShapeDtypeStruct((ROWS, BLOCK, BLOCK), jnp.float32)

    def kernel(*refs):
        column_kernel(first, *refs)

    return pl.pallas_call(
        kernel,
        out_shape=(shape, shape, shape),
        in_specs=in_smem(2) + in_vmem(2 if first else 5),
        out_specs=tuple(in_vmem(3)),
        scratch_shapes=[
            pltpu.VMEM((TILES, BLOCK, BLOCK), jnp.float32),
            pltpu.VMEM((ROWS, BLOCK, BLOCK), jnp.float32),
        ],
        compiler_params=pltpu.CompilerParams(vmem_limit_bytes=24 * MIB),
        cost_estimate=pl.CostEstimate(
            flops=2 * 20 * 2 * 128**3, bytes_accessed=6 * MIB, transcendentals=20 * 128 * 128
        ),
    )(count, table, query, kv, *(() if first else state))


def parcel_kernel(m_ref, l_ref, a_ref, keep_ref, send_ref):
    lane = lax.broadcasted_iota(jnp.int32, (BLOCK, BLOCK), 1)
    stats = jnp.zeros((BLOCK, BLOCK), jnp.float32)
    for block in range(ROWS):
        total = jnp.sum(l_ref[block], axis=1, keepdims=True)
        stats = jnp.where(lane == block, m_ref[block], stats)
        stats = jnp.where(lane == ROWS + block, total, stats)
        keep_ref[block] = a_ref[block, :HALF, :]
        send_ref[block] = a_ref[block, HALF:, :]
    keep_ref[ROWS] = stats[:HALF]
    send_ref[ROWS] = stats[HALF:]


def parcel(state):
    shape = jax.ShapeDtypeStruct((ROWS + 1, HALF, HEAD_DIM), jnp.float32)
    return pl.pallas_call(
        parcel_kernel,
        out_shape=(shape, shape),
        in_specs=in_vmem(3),
        out_specs=tuple(in_vmem(2)),
    )(*state)


def merge_kernel(here_ref, there_ref, out_ref):
    here, there = here_ref[ROWS], there_ref[ROWS]
    for block in range(ROWS):
        m0, m1 = here[:, block : block + 1], there[:, block : block + 1]
        l0 = here[:, ROWS + block : ROWS + block + 1]
        l1 = there[:, ROWS + block : ROWS + block + 1]
        m = jnp.maximum(m0, m1)
        f0 = jnp.exp2((m0 - m) * EXP2_SCALE)
        f1 = jnp.exp2((m1 - m) * EXP2_SCALE)
        mixed = here_ref[block] * f0 + there_ref[block] * f1
        out_ref[block] = (mixed / (l0 * f0 + l1 * f1)).astype(jnp.bfloat16)


def merge(here, there):
    return pl.pallas_call(
        merge_kernel,
        out_shape=jax.ShapeDtypeStruct((ROWS, HALF, HEAD_DIM), jnp.bfloat16),
        in_specs=in_vmem(2),
        out_specs=in_vmem(1)[0],
    )(here, there)


def project_kernel(place_ref, a_ref, b_ref, w_ref, w2_ref, out_ref, rows_ref):
    core = place_ref[0]

    @pl.when(pl.program_id(0) == 0)
    def _():
        mine = pl.ds(pl.multiple_of(core * HALF, HALF), HALF)
        other = pl.ds(pl.multiple_of((1 - core) * HALF, HALF), HALF)
        for which, head_set in enumerate((core, 1 - core)):
            for head in range(HEADS):
                at = (which * HEADS + head) * HEAD_DIM
                rows_ref[mine, at : at + HEAD_DIM] = a_ref[head_set * NZ + head]
                rows_ref[other, at : at + HEAD_DIM] = b_ref[head_set * NZ + head]

    width = HEADS * HEAD_DIM
    out = jnp.dot(rows_ref[:, :width], w_ref[...], preferred_element_type=jnp.float32)
    out = out + jnp.dot(rows_ref[:, width:], w2_ref[0], preferred_element_type=jnp.float32)
    out_ref[...] = out.astype(out_ref.dtype)


def project(place, a, b, w_own, w_other, dtype):
    width = w_own.shape[1] // (XL * NC)
    tiles = width // TILE_N
    deep = HEADS * HEAD_DIM
    whole = pl.BlockSpec((ROWS, HALF, HEAD_DIM), lambda i, place: (0, 0, 0))
    return pl.pallas_call(
        project_kernel,
        out_shape=jax.ShapeDtypeStruct((BLOCK, width), dtype),
        grid_spec=pltpu.PrefetchScalarGridSpec(
            num_scalar_prefetch=1,
            grid=(tiles,),
            in_specs=[
                whole,
                whole,
                pl.BlockSpec(
                    (deep, TILE_N), lambda i, place: (0, (place[1] * NC + place[0]) * tiles + i)
                ),
                pl.BlockSpec((1, deep, TILE_N), lambda i, place: (place[1], 0, i)),
            ],
            out_specs=pl.BlockSpec((BLOCK, TILE_N), lambda i, place: (0, i)),
            scratch_shapes=[pltpu.VMEM((BLOCK, 2 * deep), jnp.bfloat16)],
        ),
        cost_estimate=pl.CostEstimate(
            flops=2 * BLOCK * 2 * deep * width, bytes_accessed=4 * MIB, transcendentals=0
        ),
    )(place, a, b, w_own, w_other)


def live_tiles(frame_mask):
    y = lax.axis_index("y")
    ids = jnp.arange(ROWS, dtype=jnp.int32)
    blocks = jnp.arange(ROWS * NY, dtype=jnp.int32)
    mine = ids * NY + y
    back = jnp.arange(NY, dtype=jnp.int32)
    theirs = ids[None, :] * NY + ((y - back) % NY)[:, None]
    rows = jnp.sum(
        jnp.where(mine[:, None, None] == blocks[None, :, None], frame_mask[None], 0), axis=1
    )
    hit = jnp.sum(
        jnp.where(theirs[:, None, :, None] == blocks, rows[None, :, None, :], 0), axis=3
    )
    hit = jnp.where(hit != 0, 1, 0)
    rank = jnp.sum(jnp.where(ids[None, :] < ids[:, None], hit[:, :, None, :], 0), axis=3)
    count = jnp.sum(hit, axis=2)
    tiles = (count + 1) // 2
    start = jnp.sum(jnp.where(ids[None, :] < ids[:, None], tiles[:, None, :], 0), axis=2)
    e = jnp.arange(TILES, dtype=jnp.int32)
    chosen = (start[:, :, None] <= e) & (e < (start + tiles)[:, :, None])
    pick = lambda x: jnp.sum(jnp.where(chosen, x, 0), axis=1)
    at = 2 * (e[None, :] - pick(start[:, :, None]))
    live = jnp.clip(pick(count[:, :, None]) - at, 0, 2) * HALF
    live = jnp.where(jnp.any(chosen, axis=1), live, 0)

    def key_at(place):
        found = chosen[:, :, None, :] & (hit[:, :, :, None] > 0)
        found = found & (rank[:, :, :, None] == place[:, None, None, :])
        return jnp.sum(jnp.where(found, ids[None, None, :, None], 0), axis=(1, 2))

    table = jnp.stack([pick(ids[None, :, None]), key_at(at), key_at(at + 1), live], axis=1)
    return jnp.sum(tiles, axis=1).astype(jnp.int32), table.astype(jnp.int32)


def local(queries, keys, values, frame_mask, w_out):
    xl, c = lax.axis_index("xl"), lax.axis_index("c")
    core = jnp.stack([c]).astype(jnp.int32)

    slots, sent = split(core, queries, keys, values)
    got = lax.ppermute(sent, "c", shift(NC, 1))
    slots = lax.dynamic_update_slice(slots, got, ((1 - c) * NZ, 0, 0))
    slots, w_out, frame_mask = lax.optimization_barrier((slots, w_out, frame_mask))

    counts, tables = live_tiles(frame_mask)
    width = w_out.shape[1] // (XL * NC)
    traded = jnp.stack(
        [
            lax.dynamic_slice(
                w_out, (0, (part * NC + 1 - c) * width), (HEADS * HEAD_DIM, width)
            )
            for part in range(XL)
        ]
    )
    w_other = lax.ppermute(traded, "c", shift(NC, 1))

    slots = lax.all_to_all(slots, ("xh", "z"), 0, 0, tiled=True)
    own_query, kv = slots[:, :HALF], slots[:, HALF:]
    query = jnp.concatenate([own_query, lax.ppermute(own_query, "c", shift(NC, 1))], axis=1)
    state = None
    for by in (0, 1, 3, 2):
        column = kv if by == 0 else lax.ppermute(kv, "y", shift(NY, by))
        state = attend_column(counts[by : by + 1], tables[by], query, column, state)
    here, sent = parcel(state)
    there = lax.ppermute(sent, "c", shift(NC, 1))
    attended = lax.all_to_all(merge(here, there), ("xh", "z"), 0, 0, tiled=True)
    other_rows = lax.ppermute(attended, "c", shift(NC, 1))

    def columns_of(to_xl, dtype):
        place = jnp.stack([c, to_xl]).astype(jnp.int32)
        return project(place, attended, other_rows, w_out, w_other, dtype)

    far = lax.ppermute(columns_of(1 - xl, jnp.bfloat16), "xl", shift(XL, 1))
    near = columns_of(xl, jnp.float32)
    return (near + far.astype(jnp.float32)).astype(jnp.bfloat16)


def solution(mesh):
    fine = Mesh(mesh.devices.reshape(XH, NZ, NY, XL, NC), ("xh", "z", "y", "xl", "c"))
    seq, head = ("xh", "z", "y"), ("xl", "c")
    in_specs = (P(seq, head), P(seq, head), P(seq, head), P(), P(head, None))
    return jax.shard_map(
        local, mesh=fine, in_specs=in_specs, out_specs=P(seq, head), check_vma=False
    )
```

```python
import jax
import jax.numpy as jnp
from jax import lax
from jax.experimental import pallas as pl
from jax.experimental.pallas import tpu as pltpu
from jax.sharding import Mesh
from jax.sharding import PartitionSpec as P

HEAD_DIM = 128
BLOCK = 128
HALF = 64
HEADS = 5
XH, NZ, NY, XL, NC = 2, 8, 4, 2, 2
ROWS = XH * NZ
UNROLL = 4
TILE_N = 256
LOW = -1e30
EXP2_SCALE = HEAD_DIM ** (-0.5) * 1.4426950408889634
MIB = 1024 * 1024


def shift(size, by):
    return [(i, (i + by) % size) for i in range(size)]


def in_vmem(count):
    return [pl.BlockSpec(memory_space=pltpu.VMEM)] * count


def in_smem(count):
    return [pl.BlockSpec(memory_space=pltpu.SMEM)] * count


def split_kernel(core_ref, q_ref, k_ref, v_ref, keep_ref, send_ref):
    core = core_ref[0]
    mine = pl.ds(pl.multiple_of(core * HALF, HALF), HALF)
    other = pl.ds(pl.multiple_of((1 - core) * HALF, HALF), HALF)
    keep_ref[...] = jnp.zeros_like(keep_ref)
    for head in range(HEADS):
        lanes = slice(head * HEAD_DIM, (head + 1) * HEAD_DIM)
        for t, ref in enumerate((q_ref, k_ref, v_ref)):
            rows = slice(t * HALF, (t + 1) * HALF)
            keep_ref[core * NZ + head, rows, :] = ref[mine, lanes]
            send_ref[head, rows, :] = ref[other, lanes]


def split(core, queries, keys, values):
    return pl.pallas_call(
        split_kernel,
        out_shape=(
            jax.ShapeDtypeStruct((ROWS, 3 * HALF, HEAD_DIM), jnp.bfloat16),
            jax.ShapeDtypeStruct((HEADS, 3 * HALF, HEAD_DIM), jnp.bfloat16),
        ),
        in_specs=in_smem(1) + in_vmem(3),
        out_specs=tuple(in_vmem(2)),
        compiler_params=pltpu.CompilerParams(vmem_limit_bytes=4 * MIB),
    )(core, queries, keys, values)


def score_tiles(steps, table_ref, q_ref, kv_ref, s_ref, top_ref):
    lane = lax.broadcasted_iota(jnp.int32, (BLOCK, BLOCK), 1)

    def score(step, carry):
        tiles = []
        for u in range(UNROLL):
            e = step * UNROLL + u
            key = jnp.concatenate(
                [kv_ref[table_ref[1, e], :HALF, :], kv_ref[table_ref[2, e], :HALF, :]], axis=0
            )
            s = lax.dot_general(
                q_ref[table_ref[0, e]],
                key,
                (((1,), (1,)), ((), ())),
                preferred_element_type=jnp.float32,
            )
            s = jnp.where(lane < table_ref[3, e], s, LOW)
            s_ref[e] = s
            tiles.append(s)
        for u in range(UNROLL):
            block = table_ref[0, step * UNROLL + u]
            top_ref[block] = jnp.maximum(top_ref[block], tiles[u])
        return carry

    lax.fori_loop(0, steps, score, 0)


def mix_tiles(steps, table_ref, kv_ref, s_ref, m_ref, l_ref, a_ref):
    def mix(step, carry):
        weights, products = [], []
        for u in range(UNROLL):
            e = step * UNROLL + u
            value = jnp.concatenate(
                [kv_ref[table_ref[1, e], HALF:, :], kv_ref[table_ref[2, e], HALF:, :]], axis=0
            )
            weight = jnp.exp2((s_ref[e] - m_ref[table_ref[0, e]]) * EXP2_SCALE)
            weights.append(weight)
            products.append(
                jnp.dot(weight.astype(jnp.bfloat16), value, preferred_element_type=jnp.float32)
            )
        for u in range(UNROLL):
            block = table_ref[0, step * UNROLL + u]
            l_ref[block] = l_ref[block] + weights[u]
            a_ref[block] = a_ref[block] + products[u]
        return carry

    lax.fori_loop(0, steps, mix, 0)


def write_parcels(m_ref, l_ref, a_ref, keep_ref, send_ref):
    lane = lax.broadcasted_iota(jnp.int32, (BLOCK, BLOCK), 1)
    stats = jnp.zeros((BLOCK, BLOCK), jnp.float32)
    for block in range(ROWS):
        total = jnp.sum(l_ref[block], axis=1, keepdims=True)
        stats = jnp.where(lane == block, m_ref[block], stats)
        stats = jnp.where(lane == ROWS + block, total, stats)
        keep_ref[block] = a_ref[block, :HALF, :]
        send_ref[block] = a_ref[block, HALF:, :]
    keep_ref[ROWS] = stats[:HALF]
    send_ref[ROWS] = stats[HALF:]


def attend(count, table, query, parts, state, last):
    first = state is None
    slots = sum(part.shape[0] for part in parts)
    most = ROWS * slots // 2
    whole = jax.ShapeDtypeStruct((ROWS, BLOCK, BLOCK), jnp.float32)
    parcel = jax.ShapeDtypeStruct((ROWS + 1, HALF, HEAD_DIM), jnp.float32)

    def kernel(count_ref, table_ref, q_ref, *refs):
        part_refs, refs = refs[: len(parts)], refs[len(parts) :]
        if not first:
            (m_in, l_in, a_in), refs = refs[:3], refs[3:]
        if last:
            keep_ref, send_ref, kv_ref, s_ref, top_ref, m_ref, l_ref, a_ref = refs
        else:
            m_ref, l_ref, a_ref, kv_ref, s_ref, top_ref = refs
        at = 0
        for part in part_refs:
            kv_ref[at : at + part.shape[0]] = part[...]
            at += part.shape[0]
        steps = (count_ref[0] + (UNROLL - 1)) // UNROLL
        top_ref[...] = jnp.full(top_ref.shape, LOW, jnp.float32)
        score_tiles(steps, table_ref, q_ref, kv_ref, s_ref, top_ref)
        for block in range(ROWS):
            top = jnp.max(top_ref[block], axis=1, keepdims=True)
            if first:
                m_ref[block] = jnp.broadcast_to(top, (BLOCK, BLOCK))
                l_ref[block] = jnp.zeros((BLOCK, BLOCK), jnp.float32)
                a_ref[block] = jnp.zeros((BLOCK, HEAD_DIM), jnp.float32)
            else:
                new = jnp.maximum(m_in[block], top)
                fade = jnp.exp2((m_in[block] - new) * EXP2_SCALE)
                m_ref[block] = new
                l_ref[block] = l_in[block] * fade
                a_ref[block] = a_in[block] * fade
        mix_tiles(steps, table_ref, kv_ref, s_ref, m_ref, l_ref, a_ref)
        if last:
            write_parcels(m_ref, l_ref, a_ref, keep_ref, send_ref)

    scratch = [
        pltpu.VMEM((slots, 2 * HALF, HEAD_DIM), jnp.bfloat16),
        pltpu.VMEM((most, BLOCK, BLOCK), jnp.float32),
        pltpu.VMEM((ROWS, BLOCK, BLOCK), jnp.float32),
    ]
    if last:
        scratch += [pltpu.VMEM((ROWS, BLOCK, BLOCK), jnp.float32)] * 3
    return pl.pallas_call(
        kernel,
        out_shape=(parcel, parcel) if last else (whole, whole, whole),
        in_specs=in_smem(2) + in_vmem(1 + len(parts) + (0 if first else 3)),
        out_specs=tuple(in_vmem(2 if last else 3)),
        scratch_shapes=scratch,
        compiler_params=pltpu.CompilerParams(vmem_limit_bytes=28 * MIB),
        cost_estimate=pl.CostEstimate(
            flops=len(parts) * 40 * 2 * 128**3,
            bytes_accessed=6 * MIB,
            transcendentals=20 * 128 * 128,
        ),
    )(count, table, query, *parts, *(() if first else state))


def merge_kernel(here_ref, there_ref, out_ref):
    here, there = here_ref[ROWS], there_ref[ROWS]
    for block in range(ROWS):
        m0, m1 = here[:, block : block + 1], there[:, block : block + 1]
        l0 = here[:, ROWS + block : ROWS + block + 1]
        l1 = there[:, ROWS + block : ROWS + block + 1]
        m = jnp.maximum(m0, m1)
        f0 = jnp.exp2((m0 - m) * EXP2_SCALE)
        f1 = jnp.exp2((m1 - m) * EXP2_SCALE)
        mixed = here_ref[block] * f0 + there_ref[block] * f1
        out_ref[block] = (mixed / (l0 * f0 + l1 * f1)).astype(jnp.bfloat16)


def merge(here, there):
    return pl.pallas_call(
        merge_kernel,
        out_shape=jax.ShapeDtypeStruct((ROWS, HALF, HEAD_DIM), jnp.bfloat16),
        in_specs=in_vmem(2),
        out_specs=in_vmem(1)[0],
        compiler_params=pltpu.CompilerParams(vmem_limit_bytes=4 * MIB),
    )(here, there)


def project_kernel(core_ref, a_ref, b_ref, w_ref, w2_ref, out_ref, rows_ref):
    core = core_ref[0]
    mine = pl.ds(pl.multiple_of(core * HALF, HALF), HALF)
    other = pl.ds(pl.multiple_of((1 - core) * HALF, HALF), HALF)
    for which, head_set in enumerate((core, 1 - core)):
        for head in range(HEADS):
            at = (which * HEADS + head) * HEAD_DIM
            rows_ref[mine, at : at + HEAD_DIM] = a_ref[head_set * NZ + head]
            rows_ref[other, at : at + HEAD_DIM] = b_ref[head_set * NZ + head]
    deep = HEADS * HEAD_DIM
    for at in range(0, out_ref.shape[1], TILE_N):
        lanes = slice(at, at + TILE_N)
        out = jnp.dot(rows_ref[:, :deep], w_ref[:, lanes], preferred_element_type=jnp.float32)
        out = out + jnp.dot(
            rows_ref[:, deep:], w2_ref[:, lanes], preferred_element_type=jnp.float32
        )
        out_ref[:, lanes] = out.astype(out_ref.dtype)


def project(core, a, b, w_own, w_other, dtype):
    deep, width = w_own.shape
    return pl.pallas_call(
        project_kernel,
        out_shape=jax.ShapeDtypeStruct((BLOCK, width), dtype),
        in_specs=in_smem(1) + in_vmem(4),
        out_specs=in_vmem(1)[0],
        scratch_shapes=[pltpu.VMEM((BLOCK, 2 * deep), jnp.bfloat16)],
        compiler_params=pltpu.CompilerParams(vmem_limit_bytes=8 * MIB),
        cost_estimate=pl.CostEstimate(
            flops=2 * BLOCK * 2 * deep * width, bytes_accessed=4 * MIB, transcendentals=0
        ),
    )(core, a, b, w_own, w_other)


def add_kernel(near_ref, far_ref, out_ref):
    out_ref[...] = (near_ref[...] + far_ref[...].astype(jnp.float32)).astype(out_ref.dtype)


def add(near, far):
    return pl.pallas_call(
        add_kernel,
        out_shape=jax.ShapeDtypeStruct(near.shape, jnp.bfloat16),
        in_specs=in_vmem(2),
        out_specs=in_vmem(1)[0],
        compiler_params=pltpu.CompilerParams(vmem_limit_bytes=4 * MIB),
    )(near, far)


def live_tiles(frame_mask, columns):
    y = lax.axis_index("y")
    ids = jnp.arange(ROWS, dtype=jnp.int32)
    blocks = jnp.arange(ROWS * NY, dtype=jnp.int32)
    slots = jnp.arange(ROWS * len(columns), dtype=jnp.int32)
    mine = ids * NY + y
    theirs = jnp.concatenate([ids * NY + (y - back) % NY for back in columns])
    rows = jnp.sum(
        jnp.where(mine[:, None, None] == blocks[None, :, None], frame_mask[None], 0), axis=1
    )
    hit = jnp.sum(jnp.where(theirs[:, None] == blocks, rows[:, None, :], 0), axis=2)
    hit = jnp.where(hit != 0, 1, 0)
    rank = jnp.sum(jnp.where(slots[None, :] < slots[:, None], hit[:, None, :], 0), axis=2)
    count = jnp.sum(hit, axis=1)
    tiles = (count + 1) // 2
    start = jnp.sum(jnp.where(ids[None, :] < ids[:, None], tiles[None, :], 0), axis=1)
    e = jnp.arange(ROWS * ROWS * len(columns) // 2, dtype=jnp.int32)
    chosen = (start[:, None] <= e) & (e < (start + tiles)[:, None])
    pick = lambda x: jnp.sum(jnp.where(chosen, x[:, None], 0), axis=0)
    at = 2 * (e - pick(start))
    live = jnp.where(jnp.any(chosen, axis=0), jnp.clip(pick(count) - at, 0, 2) * HALF, 0)

    def key_at(place):
        found = chosen[:, None, :] & (hit[:, :, None] > 0) & (rank[:, :, None] == place)
        return jnp.sum(jnp.where(found, slots[None, :, None], 0), axis=(0, 1))

    table = jnp.stack([pick(ids), key_at(at), key_at(at + 1), live])
    return jnp.sum(tiles, keepdims=True).astype(jnp.int32), table.astype(jnp.int32)


def local(queries, keys, values, frame_mask, w_out):
    xl, c = lax.axis_index("xl"), lax.axis_index("c")
    core = jnp.stack([c]).astype(jnp.int32)

    groups = [live_tiles(frame_mask, columns) for columns in ((0,), (1, 3), (2,))]
    slots, sent = split(core, queries, keys, values)
    got = lax.ppermute(sent, "c", shift(NC, 1))
    slots = lax.dynamic_update_slice(slots, got, ((1 - c) * NZ, 0, 0))
    slots, w_out = lax.optimization_barrier((slots, w_out))

    width = w_out.shape[1] // (XL * NC)

    def w_columns(to_xl, to_c):
        return lax.dynamic_slice(w_out, (0, (to_xl * NC + to_c) * width), (w_out.shape[0], width))

    w_own = [w_columns(to_xl, c) for to_xl in (1 - xl, xl)]
    w_other = [
        lax.ppermute(w_columns(to_xl, 1 - c), "c", shift(NC, 1)) for to_xl in (1 - xl, xl)
    ]

    slots = lax.all_to_all(slots, ("xh", "z"), 0, 0, tiled=True)
    own_query, kv = slots[:, :HALF], slots[:, HALF:]
    query = jnp.concatenate([own_query, lax.ppermute(own_query, "c", shift(NC, 1))], axis=1)
    before = lax.ppermute(kv, "y", shift(NY, 1))
    after = lax.ppermute(kv, "y", shift(NY, -1))
    low = lax.ppermute(before[: ROWS // 2], "y", shift(NY, 1))
    high = lax.ppermute(after[ROWS // 2 :], "y", shift(NY, -1))
    state = attend(*groups[0], query, [kv], None, False)
    state = attend(*groups[1], query, [before, after], state, False)
    here, sent = attend(*groups[2], query, [low, high], state, True)
    there = lax.ppermute(sent, "c", shift(NC, 1))
    merged = merge(here, there)
    merged, w_own, w_other = lax.optimization_barrier((merged, w_own, w_other))
    attended = lax.all_to_all(merged, ("xh", "z"), 0, 0, tiled=True)
    other_rows = lax.ppermute(attended, "c", shift(NC, 1))
    far = project(core, attended, other_rows, w_own[0], w_other[0], jnp.bfloat16)
    far = lax.ppermute(far, "xl", shift(XL, 1))
    near = project(core, attended, other_rows, w_own[1], w_other[1], jnp.float32)
    return add(near, far)


def solution(mesh):
    fine = Mesh(mesh.devices.reshape(XH, NZ, NY, XL, NC), ("xh", "z", "y", "xl", "c"))
    seq, head = ("xh", "z", "y"), ("xl", "c")
    in_specs = (P(seq, head), P(seq, head), P(seq, head), P(), P(head, None))
    return jax.shard_map(
        local, mesh=fine, in_specs=in_specs, out_specs=P(seq, head), check_vma=False
    )
```

```python
import jax
import jax.numpy as jnp
from jax import lax
from jax.experimental import pallas as pl
from jax.experimental.pallas import tpu as pltpu
from jax.sharding import Mesh
from jax.sharding import PartitionSpec as P

HEAD_DIM = 128
BLOCK = 128
HALF = 64
HEADS = 5
XH, NZ, NY, XL, NC = 2, 8, 4, 2, 2
ROWS = XH * NZ
UNROLL = 4
TILE_N = 256
LOW = -1e30
EXP2_SCALE = HEAD_DIM ** (-0.5) * 1.4426950408889634
MIB = 1024 * 1024


def shift(size, by):
    return [(i, (i + by) % size) for i in range(size)]


def in_vmem(count):
    return [pl.BlockSpec(memory_space=pltpu.VMEM)] * count


def in_smem(count):
    return [pl.BlockSpec(memory_space=pltpu.SMEM)] * count


def split_kernel(core_ref, q_hbm, k_hbm, v_hbm, keep_ref, send_ref, q_ref, k_ref, v_ref, sems):
    copies = [
        pltpu.make_async_copy(source, target, sems.at[i])
        for i, (source, target) in enumerate(
            ((q_hbm, q_ref), (k_hbm, k_ref), (v_hbm, v_ref))
        )
    ]
    for copy in copies:
        copy.start()
    core = core_ref[0]
    mine = pl.ds(pl.multiple_of(core * HALF, HALF), HALF)
    other = pl.ds(pl.multiple_of((1 - core) * HALF, HALF), HALF)
    for spare in range(HEADS, NZ):
        for head_set in range(NC):
            keep_ref[head_set * NZ + spare] = jnp.zeros((3 * HALF, HEAD_DIM), jnp.bfloat16)
    for copy in copies:
        copy.wait()
    for head in range(HEADS):
        lanes = slice(head * HEAD_DIM, (head + 1) * HEAD_DIM)
        for t, ref in enumerate((q_ref, k_ref, v_ref)):
            rows = slice(t * HALF, (t + 1) * HALF)
            keep_ref[core * NZ + head, rows, :] = ref[mine, lanes]
            send_ref[head, rows, :] = ref[other, lanes]


def split(core, queries, keys, values):
    return pl.pallas_call(
        split_kernel,
        out_shape=(
            jax.ShapeDtypeStruct((ROWS, 3 * HALF, HEAD_DIM), jnp.bfloat16),
            jax.ShapeDtypeStruct((HEADS, 3 * HALF, HEAD_DIM), jnp.bfloat16),
        ),
        in_specs=in_smem(1) + [pl.BlockSpec(memory_space=pl.ANY)] * 3,
        out_specs=tuple(in_vmem(2)),
        scratch_shapes=[pltpu.VMEM(queries.shape, jnp.bfloat16)] * 3
        + [pltpu.SemaphoreType.DMA((3,))],
        compiler_params=pltpu.CompilerParams(vmem_limit_bytes=56 * MIB),
    )(core, queries, keys, values)


def score_tiles(steps, table_ref, q_ref, kv_ref, s_ref, top_ref):
    lane = lax.broadcasted_iota(jnp.int32, (BLOCK, BLOCK), 1)

    def score(step, carry):
        tiles = []
        for u in range(UNROLL):
            e = step * UNROLL + u
            key = jnp.concatenate(
                [kv_ref[table_ref[1, e], :HALF, :], kv_ref[table_ref[2, e], :HALF, :]], axis=0
            )
            s = lax.dot_general(
                q_ref[table_ref[0, e]],
                key,
                (((1,), (1,)), ((), ())),
                preferred_element_type=jnp.float32,
            )
            s = jnp.where(lane < table_ref[3, e], s, LOW)
            s_ref[e] = s
            tiles.append(s)
        for u in range(UNROLL):
            block = table_ref[0, step * UNROLL + u]
            top_ref[block] = jnp.maximum(top_ref[block], tiles[u])
        return carry

    lax.fori_loop(0, steps, score, 0)


def mix_tiles(steps, table_ref, kv_ref, s_ref, m_ref, l_ref, a_ref):
    def mix(step, carry):
        weights, products = [], []
        for u in range(UNROLL):
            e = step * UNROLL + u
            value = jnp.concatenate(
                [kv_ref[table_ref[1, e], HALF:, :], kv_ref[table_ref[2, e], HALF:, :]], axis=0
            )
            weight = jnp.exp2((s_ref[e] - m_ref[table_ref[0, e]]) * EXP2_SCALE)
            weights.append(weight)
            products.append(
                jnp.dot(weight.astype(jnp.bfloat16), value, preferred_element_type=jnp.float32)
            )
        for u in range(UNROLL):
            block = table_ref[0, step * UNROLL + u]
            l_ref[block] = l_ref[block] + weights[u]
            a_ref[block] = a_ref[block] + products[u]
        return carry

    lax.fori_loop(0, steps, mix, 0)


def write_parcels(m_ref, l_ref, a_ref, keep_ref, send_ref):
    lane = lax.broadcasted_iota(jnp.int32, (BLOCK, BLOCK), 1)
    stats = jnp.zeros((BLOCK, BLOCK), jnp.float32)
    for block in range(ROWS):
        total = jnp.sum(l_ref[block], axis=1, keepdims=True)
        stats = jnp.where(lane == block, m_ref[block], stats)
        stats = jnp.where(lane == ROWS + block, total, stats)
        keep_ref[block] = a_ref[block, :HALF, :]
        send_ref[block] = a_ref[block, HALF:, :]
    keep_ref[ROWS] = stats[:HALF]
    send_ref[ROWS] = stats[HALF:]


def attend(count, table, query, parts, state, last):
    first = state is None
    slots = sum(part.shape[0] for part in parts)
    most = ROWS * slots // 2
    whole = jax.ShapeDtypeStruct((ROWS, BLOCK, BLOCK), jnp.float32)
    parcel = jax.ShapeDtypeStruct((ROWS + 1, HALF, HEAD_DIM), jnp.float32)

    def kernel(count_ref, table_ref, q_ref, *refs):
        part_refs, refs = refs[: len(parts)], refs[len(parts) :]
        if not first:
            (m_in, l_in, a_in), refs = refs[:3], refs[3:]
        if last:
            keep_ref, send_ref, kv_ref, s_ref, top_ref, m_ref, l_ref, a_ref = refs
        else:
            m_ref, l_ref, a_ref, kv_ref, s_ref, top_ref = refs
        at = 0
        for part in part_refs:
            kv_ref[at : at + part.shape[0]] = part[...]
            at += part.shape[0]
        steps = (count_ref[0] + (UNROLL - 1)) // UNROLL
        top_ref[...] = jnp.full(top_ref.shape, LOW, jnp.float32)
        score_tiles(steps, table_ref, q_ref, kv_ref, s_ref, top_ref)
        for block in range(ROWS):
            top = jnp.max(top_ref[block], axis=1, keepdims=True)
            if first:
                m_ref[block] = jnp.broadcast_to(top, (BLOCK, BLOCK))
                l_ref[block] = jnp.zeros((BLOCK, BLOCK), jnp.float32)
                a_ref[block] = jnp.zeros((BLOCK, HEAD_DIM), jnp.float32)
            else:
                new = jnp.maximum(m_in[block], top)
                fade = jnp.exp2((m_in[block] - new) * EXP2_SCALE)
                m_ref[block] = new
                l_ref[block] = l_in[block] * fade
                a_ref[block] = a_in[block] * fade
        mix_tiles(steps, table_ref, kv_ref, s_ref, m_ref, l_ref, a_ref)
        if last:
            write_parcels(m_ref, l_ref, a_ref, keep_ref, send_ref)

    scratch = [
        pltpu.VMEM((slots, 2 * HALF, HEAD_DIM), jnp.bfloat16),
        pltpu.VMEM((most, BLOCK, BLOCK), jnp.float32),
        pltpu.VMEM((ROWS, BLOCK, BLOCK), jnp.float32),
    ]
    if last:
        scratch += [pltpu.VMEM((ROWS, BLOCK, BLOCK), jnp.float32)] * 3
    return pl.pallas_call(
        kernel,
        out_shape=(parcel, parcel) if last else (whole, whole, whole),
        in_specs=in_smem(2) + in_vmem(1 + len(parts) + (0 if first else 3)),
        out_specs=tuple(in_vmem(2 if last else 3)),
        scratch_shapes=scratch,
        compiler_params=pltpu.CompilerParams(vmem_limit_bytes=28 * MIB),
        cost_estimate=pl.CostEstimate(
            flops=len(parts) * 40 * 2 * 128**3,
            bytes_accessed=6 * MIB,
            transcendentals=20 * 128 * 128,
        ),
    )(count, table, query, *parts, *(() if first else state))


def merge_kernel(here_ref, there_ref, out_ref):
    here, there = here_ref[ROWS], there_ref[ROWS]
    for block in range(ROWS):
        m0, m1 = here[:, block : block + 1], there[:, block : block + 1]
        l0 = here[:, ROWS + block : ROWS + block + 1]
        l1 = there[:, ROWS + block : ROWS + block + 1]
        m = jnp.maximum(m0, m1)
        f0 = jnp.exp2((m0 - m) * EXP2_SCALE)
        f1 = jnp.exp2((m1 - m) * EXP2_SCALE)
        mixed = here_ref[block] * f0 + there_ref[block] * f1
        out_ref[block] = (mixed / (l0 * f0 + l1 * f1)).astype(jnp.bfloat16)


def merge(here, there):
    return pl.pallas_call(
        merge_kernel,
        out_shape=jax.ShapeDtypeStruct((ROWS, HALF, HEAD_DIM), jnp.bfloat16),
        in_specs=in_vmem(2),
        out_specs=in_vmem(1)[0],
        compiler_params=pltpu.CompilerParams(vmem_limit_bytes=4 * MIB),
    )(here, there)


def project(core, a, b, w_own, w_other, added):
    deep, width = w_own.shape
    final = added is not None

    def kernel(core_ref, a_ref, b_ref, w_ref, w2_ref, *refs):
        if final:
            added_ref, refs = refs[0], refs[1:]
        out_ref, rows_ref = refs
        core = core_ref[0]
        mine = pl.ds(pl.multiple_of(core * HALF, HALF), HALF)
        other = pl.ds(pl.multiple_of((1 - core) * HALF, HALF), HALF)
        for which, head_set in enumerate((core, 1 - core)):
            for head in range(HEADS):
                at = (which * HEADS + head) * HEAD_DIM
                rows_ref[mine, at : at + HEAD_DIM] = a_ref[head_set * NZ + head]
                rows_ref[other, at : at + HEAD_DIM] = b_ref[head_set * NZ + head]
        for at in range(0, width, TILE_N):
            lanes = slice(at, at + TILE_N)
            out = jnp.dot(rows_ref[:, :deep], w_ref[:, lanes], preferred_element_type=jnp.float32)
            out = out + jnp.dot(
                rows_ref[:, deep:], w2_ref[:, lanes], preferred_element_type=jnp.float32
            )
            if final:
                out = out + added_ref[:, lanes]
            out_ref[:, lanes] = out.astype(out_ref.dtype)

    return pl.pallas_call(
        kernel,
        out_shape=jax.ShapeDtypeStruct((BLOCK, width), jnp.bfloat16 if final else jnp.float32),
        in_specs=in_smem(1) + in_vmem(5 if final else 4),
        out_specs=in_vmem(1)[0],
        scratch_shapes=[pltpu.VMEM((BLOCK, 2 * deep), jnp.bfloat16)],
        compiler_params=pltpu.CompilerParams(vmem_limit_bytes=8 * MIB),
        cost_estimate=pl.CostEstimate(
            flops=2 * BLOCK * 2 * deep * width, bytes_accessed=4 * MIB, transcendentals=0
        ),
    )(core, a, b, w_own, w_other, *((added,) if final else ()))


GROUPS = ((0,), (1, 3), (2,))


def tiles_kernel(place_ref, mask_ref, *refs):
    y = place_ref[1]
    for group, columns in enumerate(GROUPS):
        count_ref, table_ref = refs[2 * group], refs[2 * group + 1]

        def one_query_block(block, start, columns=columns, table_ref=table_ref):
            row = block * NY + y
            found = jnp.int32(0)
            for column, back in enumerate(columns):
                theirs = lax.rem(y - back + NY, NY)
                for i in range(ROWS):
                    table_ref[1 + lax.rem(found, 2), start + lax.div(found, 2)] = column * ROWS + i
                    found = found + jnp.where(mask_ref[row, i * NY + theirs] != 0, 1, 0)
            table_ref[1 + lax.rem(found, 2), start + lax.div(found, 2)] = 0
            tiles = lax.div(found + 1, 2)

            def fill(t, carry):
                table_ref[0, start + t] = block
                table_ref[3, start + t] = jnp.minimum(found - 2 * t, 2) * HALF
                return carry

            lax.fori_loop(0, tiles, fill, 0)
            return start + tiles

        total = lax.fori_loop(0, ROWS, one_query_block, jnp.int32(0))
        count_ref[0] = total
        for u in range(UNROLL):
            for r in range(4):
                table_ref[r, total + u] = 0


def live_tiles(place, frame_mask):
    out_shape = []
    for columns in GROUPS:
        most = ROWS * ROWS * len(columns) // 2
        out_shape += [
            jax.ShapeDtypeStruct((1,), jnp.int32),
            jax.ShapeDtypeStruct((4, most + 128), jnp.int32),
        ]
    flat = pl.pallas_call(
        tiles_kernel,
        out_shape=tuple(out_shape),
        in_specs=in_smem(2),
        out_specs=tuple(in_smem(len(out_shape))),
        compiler_params=pltpu.CompilerParams(vmem_limit_bytes=4 * MIB),
        cost_estimate=pl.CostEstimate(flops=10**6, bytes_accessed=10**5, transcendentals=0),
    )(place, frame_mask)
    return [(flat[2 * i], flat[2 * i + 1]) for i in range(len(GROUPS))]


def local(queries, keys, values, frame_mask, w_out):
    xl, c = lax.axis_index("xl"), lax.axis_index("c")
    core = jnp.stack([c, lax.axis_index("y")]).astype(jnp.int32)

    slots, sent = split(core, queries, keys, values)
    got = lax.ppermute(sent, "c", shift(NC, 1))
    slots = lax.dynamic_update_slice(slots, got, ((1 - c) * NZ, 0, 0))
    slots, w_out = lax.optimization_barrier((slots, w_out))

    width = w_out.shape[1] // (XL * NC)

    def w_columns(to_xl, to_c):
        return lax.dynamic_slice(w_out, (0, (to_xl * NC + to_c) * width), (w_out.shape[0], width))

    w_here, w_core, w_next, w_last = (
        w_columns(xl, c),
        w_columns(xl, 1 - c),
        w_columns(1 - xl, c),
        w_columns(1 - xl, 1 - c),
    )
    w_here, w_core, w_next, w_last, frame_mask = lax.optimization_barrier(
        (w_here, w_core, w_next, w_last, frame_mask)
    )
    places = [(x, core_) for x in range(XH * XL) for core_ in range(NC)]
    along_x = ("xh", "xl", "c")
    w_next = lax.ppermute(
        w_next, along_x, [(x * NC + k, (x + 1) % 4 * NC + k) for x, k in places]
    )
    w_last = lax.ppermute(
        w_last, along_x, [(x * NC + k, (x + 3) % 4 * NC + 1 - k) for x, k in places]
    )
    w_core = lax.ppermute(w_core, "c", shift(NC, 1))
    groups = live_tiles(core, frame_mask)

    slots = lax.all_to_all(slots, ("xh", "z"), 0, 0, tiled=True)
    slots, w_here, groups = lax.optimization_barrier((slots, w_here, groups))
    own_query, kv = slots[:, :HALF], slots[:, HALF:]
    before = lax.ppermute(kv, "y", shift(NY, 1))
    after = lax.ppermute(kv, "y", shift(NY, -1))
    query = jnp.concatenate([own_query, lax.ppermute(own_query, "c", shift(NC, 1))], axis=1)
    state = attend(*groups[0], query, [kv], None, False)
    before, after, state = lax.optimization_barrier((before, after, state))
    low = lax.ppermute(before[: ROWS // 2], "y", shift(NY, 1))
    high = lax.ppermute(after[ROWS // 2 :], "y", shift(NY, -1))
    state = attend(*groups[1], query, [before, after], state, False)
    low, high, w_next, w_last, w_core = lax.optimization_barrier(
        (low, high, w_next, w_last, w_core)
    )
    here, sent = attend(*groups[2], query, [low, high], state, True)
    there = lax.ppermute(sent, "c", shift(NC, 1))
    rows = lax.all_to_all(merge(here, there), ("xh", "z"), 0, 0, tiled=True)
    rows_xl = lax.ppermute(rows, "xl", shift(XL, 1))
    rows_core = lax.ppermute(rows, "c", shift(NC, 1))
    near = project(core, rows, rows_core, w_here, w_core, None)
    rows_both = lax.ppermute(rows_xl, "c", shift(NC, 1))
    return project(core, rows_xl, rows_both, w_next, w_last, near)


def solution(mesh):
    fine = Mesh(mesh.devices.reshape(XH, NZ, NY, XL, NC), ("xh", "z", "y", "xl", "c"))
    seq, head = ("xh", "z", "y"), ("xl", "c")
    in_specs = (P(seq, head), P(seq, head), P(seq, head), P(), P(head, None))
    return jax.shard_map(
        local, mesh=fine, in_specs=in_specs, out_specs=P(seq, head), check_vma=False
    )
```

```python
import jax
import jax.numpy as jnp
from jax import lax
from jax.experimental import pallas as pl
from jax.experimental.pallas import tpu as pltpu
from jax.sharding import Mesh
from jax.sharding import PartitionSpec as P

HEAD_DIM = 128
BLOCK = 128
HALF = 64
HEADS = 5
XH, NZ, NY, XL, NC = 2, 8, 4, 2, 2
ROWS = XH * NZ
UNROLL = 4
TILE_N = 256
LOW = -1e30
EXP2_SCALE = HEAD_DIM ** (-0.5) * 1.4426950408889634
MIB = 1024 * 1024


def shift(size, by):
    return [(i, (i + by) % size) for i in range(size)]


def in_vmem(count):
    return [pl.BlockSpec(memory_space=pltpu.VMEM)] * count


def in_smem(count):
    return [pl.BlockSpec(memory_space=pltpu.SMEM)] * count


def split_kernel(q_ref, k_ref, v_ref, keep_ref, send_ref, sems):
    core = lax.axis_index("c")
    mine = pl.ds(pl.multiple_of(core * HALF, HALF), HALF)
    other = pl.ds(pl.multiple_of((1 - core) * HALF, HALF), HALF)
    copies = []

    def copy(source, target):
        copies.append(pltpu.make_async_copy(source, target, sems.at[len(copies)]))
        copies[-1].start()

    for head in range(HEADS):
        lanes = slice(head * HEAD_DIM, (head + 1) * HEAD_DIM)
        for t, ref in enumerate((q_ref, k_ref, v_ref)):
            copy(ref.at[other, lanes], send_ref.at[head, pl.ds(t * HALF, HALF)])
    for head in range(HEADS):
        lanes = slice(head * HEAD_DIM, (head + 1) * HEAD_DIM)
        for t, ref in enumerate((q_ref, k_ref, v_ref)):
            copy(ref.at[mine, lanes], keep_ref.at[core * NZ + head, pl.ds(t * HALF, HALF)])
    for each in copies:
        each.wait()


def split(queries, keys, values):
    anywhere = pl.BlockSpec(memory_space=pl.ANY)
    return pl.pallas_call(
        split_kernel,
        out_shape=(
            jax.ShapeDtypeStruct((ROWS, 3 * HALF, HEAD_DIM), jnp.bfloat16),
            jax.ShapeDtypeStruct((HEADS, 3 * HALF, HEAD_DIM), jnp.bfloat16),
        ),
        in_specs=[anywhere] * 3,
        out_specs=(anywhere,) * 2,
        scratch_shapes=[pltpu.SemaphoreType.DMA((6 * HEADS,))],
        compiler_params=pltpu.CompilerParams(vmem_limit_bytes=56 * MIB),
    )(queries, keys, values)


def score_tiles(steps, tables, q_ref, kv_ref, s_ref, top_ref):
    block_ref, slot_ref, live_ref = tables
    lane = lax.broadcasted_iota(jnp.int32, (BLOCK, BLOCK), 1)

    def score(step, carry):
        tiles = []
        for u in range(UNROLL):
            e = step * UNROLL + u
            key = jnp.concatenate(
                [kv_ref[slot_ref[2 * e], :HALF, :], kv_ref[slot_ref[2 * e + 1], :HALF, :]], axis=0
            )
            s = lax.dot_general(
                q_ref[block_ref[e]],
                key,
                (((1,), (1,)), ((), ())),
                preferred_element_type=jnp.float32,
            )
            s = jnp.where(lane < live_ref[e], s, LOW)
            s_ref[e] = s
            tiles.append(s)
        for u in range(UNROLL):
            block = block_ref[step * UNROLL + u]
            top_ref[block] = jnp.maximum(top_ref[block], tiles[u])
        return carry

    lax.fori_loop(0, steps, score, 0)


def mix_tiles(steps, tables, kv_ref, s_ref, m_ref, l_ref, a_ref):
    block_ref, slot_ref, live_ref = tables

    def mix(step, carry):
        weights, products = [], []
        for u in range(UNROLL):
            e = step * UNROLL + u
            value = jnp.concatenate(
                [kv_ref[slot_ref[2 * e], HALF:, :], kv_ref[slot_ref[2 * e + 1], HALF:, :]], axis=0
            )
            weight = jnp.exp2((s_ref[e] - m_ref[block_ref[e]]) * EXP2_SCALE)
            weights.append(weight)
            products.append(
                jnp.dot(weight.astype(jnp.bfloat16), value, preferred_element_type=jnp.float32)
            )
        for u in range(UNROLL):
            block = block_ref[step * UNROLL + u]
            l_ref[block] = l_ref[block] + weights[u]
            a_ref[block] = a_ref[block] + products[u]
        return carry

    lax.fori_loop(0, steps, mix, 0)


def write_parcels(m_ref, l_ref, a_ref, keep_ref, send_ref):
    lane = lax.broadcasted_iota(jnp.int32, (BLOCK, BLOCK), 1)
    stats = jnp.zeros((BLOCK, BLOCK), jnp.float32)
    for block in range(ROWS):
        total = jnp.sum(l_ref[block], axis=1, keepdims=True)
        stats = jnp.where(lane == block, m_ref[block], stats)
        stats = jnp.where(lane == ROWS + block, total, stats)
        keep_ref[block] = a_ref[block, :HALF, :]
        send_ref[block] = a_ref[block, HALF:, :]
    keep_ref[ROWS] = stats[:HALF]
    send_ref[ROWS] = stats[HALF:]


def attend(tables, query, parts, state, last):
    first = state is None
    slots = sum(part.shape[0] for part in parts)
    most = ROWS * slots // 2
    whole = jax.ShapeDtypeStruct((ROWS, BLOCK, BLOCK), jnp.float32)
    parcel = jax.ShapeDtypeStruct((ROWS + 1, HALF, HEAD_DIM), jnp.float32)

    def kernel(count_ref, block_ref, slot_ref, live_ref, own_ref, other_ref, *refs):
        tables = (block_ref, slot_ref, live_ref)
        part_refs, refs = refs[: len(parts)], refs[len(parts) :]
        if not first:
            (m_in, l_in, a_in), refs = refs[:3], refs[3:]
        if last:
            keep_ref, send_ref, q_ref, kv_ref, s_ref, top_ref, m_ref, l_ref, a_ref = refs
        else:
            m_ref, l_ref, a_ref, q_ref, kv_ref, s_ref, top_ref = refs
        q_ref[:, :HALF, :] = own_ref[...]
        q_ref[:, HALF:, :] = other_ref[...]
        at = 0
        for part in part_refs:
            kv_ref[at : at + part.shape[0]] = part[...]
            at += part.shape[0]
        steps = (count_ref[0] + (UNROLL - 1)) // UNROLL
        top_ref[...] = jnp.full(top_ref.shape, LOW, jnp.float32)
        score_tiles(steps, tables, q_ref, kv_ref, s_ref, top_ref)
        for block in range(ROWS):
            top = jnp.max(top_ref[block], axis=1, keepdims=True)
            if first:
                m_ref[block] = jnp.broadcast_to(top, (BLOCK, BLOCK))
                l_ref[block] = jnp.zeros((BLOCK, BLOCK), jnp.float32)
                a_ref[block] = jnp.zeros((BLOCK, HEAD_DIM), jnp.float32)
            else:
                new = jnp.maximum(m_in[block], top)
                fade = jnp.exp2((m_in[block] - new) * EXP2_SCALE)
                m_ref[block] = new
                l_ref[block] = l_in[block] * fade
                a_ref[block] = a_in[block] * fade
        mix_tiles(steps, tables, kv_ref, s_ref, m_ref, l_ref, a_ref)
        if last:
            write_parcels(m_ref, l_ref, a_ref, keep_ref, send_ref)

    scratch = [
        pltpu.VMEM((ROWS, BLOCK, HEAD_DIM), jnp.bfloat16),
        pltpu.VMEM((slots, 2 * HALF, HEAD_DIM), jnp.bfloat16),
        pltpu.VMEM((most, BLOCK, BLOCK), jnp.float32),
        pltpu.VMEM((ROWS, BLOCK, BLOCK), jnp.float32),
    ]
    if last:
        scratch += [pltpu.VMEM((ROWS, BLOCK, BLOCK), jnp.float32)] * 3
    return pl.pallas_call(
        kernel,
        out_shape=(parcel, parcel) if last else (whole, whole, whole),
        in_specs=in_smem(4) + in_vmem(2 + len(parts) + (0 if first else 3)),
        out_specs=tuple(in_vmem(2 if last else 3)),
        scratch_shapes=scratch,
        compiler_params=pltpu.CompilerParams(vmem_limit_bytes=28 * MIB),
        cost_estimate=pl.CostEstimate(
            flops=len(parts) * 40 * 2 * 128**3,
            bytes_accessed=6 * MIB,
            transcendentals=20 * 128 * 128,
        ),
    )(*tables, *query, *parts, *(() if first else state))


def merge_kernel(here_ref, there_ref, out_ref):
    here, there = here_ref[ROWS], there_ref[ROWS]
    for block in range(ROWS):
        m0, m1 = here[:, block : block + 1], there[:, block : block + 1]
        l0 = here[:, ROWS + block : ROWS + block + 1]
        l1 = there[:, ROWS + block : ROWS + block + 1]
        m = jnp.maximum(m0, m1)
        f0 = jnp.exp2((m0 - m) * EXP2_SCALE)
        f1 = jnp.exp2((m1 - m) * EXP2_SCALE)
        mixed = here_ref[block] * f0 + there_ref[block] * f1
        out_ref[block] = (mixed / (l0 * f0 + l1 * f1)).astype(jnp.bfloat16)


def merge(here, there):
    return pl.pallas_call(
        merge_kernel,
        out_shape=jax.ShapeDtypeStruct((ROWS, HALF, HEAD_DIM), jnp.bfloat16),
        in_specs=in_vmem(2),
        out_specs=in_vmem(1)[0],
        compiler_params=pltpu.CompilerParams(vmem_limit_bytes=4 * MIB),
    )(here, there)


def project(a, b, w_own, w_other, added):
    deep, width = w_own.shape
    final = added is not None

    def kernel(a_ref, b_ref, w_ref, w2_ref, *refs):
        if final:
            added_ref, refs = refs[0], refs[1:]
        out_ref, rows_ref = refs
        core = lax.axis_index("c")
        mine = pl.ds(pl.multiple_of(core * HALF, HALF), HALF)
        other = pl.ds(pl.multiple_of((1 - core) * HALF, HALF), HALF)
        for which, head_set in enumerate((core, 1 - core)):
            for head in range(HEADS):
                at = (which * HEADS + head) * HEAD_DIM
                rows_ref[mine, at : at + HEAD_DIM] = a_ref[head_set * NZ + head]
                rows_ref[other, at : at + HEAD_DIM] = b_ref[head_set * NZ + head]
        for at in range(0, width, TILE_N):
            lanes = slice(at, at + TILE_N)
            out = jnp.dot(rows_ref[:, :deep], w_ref[:, lanes], preferred_element_type=jnp.float32)
            out = out + jnp.dot(
                rows_ref[:, deep:], w2_ref[:, lanes], preferred_element_type=jnp.float32
            )
            if final:
                out = out + added_ref[:, lanes]
            out_ref[:, lanes] = out.astype(out_ref.dtype)

    return pl.pallas_call(
        kernel,
        out_shape=jax.ShapeDtypeStruct((BLOCK, width), jnp.bfloat16 if final else jnp.float32),
        in_specs=in_vmem(5 if final else 4),
        out_specs=in_vmem(1)[0],
        scratch_shapes=[pltpu.VMEM((BLOCK, 2 * deep), jnp.bfloat16)],
        compiler_params=pltpu.CompilerParams(vmem_limit_bytes=8 * MIB),
        cost_estimate=pl.CostEstimate(
            flops=2 * BLOCK * 2 * deep * width, bytes_accessed=4 * MIB, transcendentals=0
        ),
    )(a, b, w_own, w_other, *((added,) if final else ()))


GROUPS = ((0,), (1, 3), (2,))


def tiles_kernel(mask_ref, *refs):
    y = lax.axis_index("y")
    for group, columns in enumerate(GROUPS):
        count_ref, block_ref, slot_ref, live_ref = refs[4 * group : 4 * group + 4]

        def one_query_block(block, start, columns=columns, refs=(block_ref, slot_ref, live_ref)):
            block_ref, slot_ref, live_ref = refs
            row = block * NY + y
            first = 2 * start
            at = first
            for column, back in enumerate(columns):
                theirs = (y - back + NY) & (NY - 1)
                for i in range(ROWS):
                    slot_ref[at] = column * ROWS + i
                    at = at + jnp.where(mask_ref[row, i * NY + theirs] != 0, 1, 0)
            slot_ref[at] = 0
            tiles = (at - first + 1) >> 1

            def fill(t, carry):
                block_ref[start + t] = block
                live_ref[start + t] = 2 * HALF
                return carry

            lax.fori_loop(0, tiles, fill, 0)

            @pl.when(((at - first) & 1) == 1)
            def _():
                live_ref[start + tiles - 1] = HALF

            return start + tiles

        total = lax.fori_loop(0, ROWS, one_query_block, jnp.int32(0))
        count_ref[0] = total
        for u in range(UNROLL):
            block_ref[total + u] = 0
            live_ref[total + u] = 0
            slot_ref[2 * (total + u)] = 0
            slot_ref[2 * (total + u) + 1] = 0


def live_tiles(frame_mask):
    out_shape = []
    for columns in GROUPS:
        most = ROWS * ROWS * len(columns) // 2 + 128
        out_shape += [
            jax.ShapeDtypeStruct((size,), jnp.int32) for size in (1, most, 2 * most, most)
        ]
    flat = pl.pallas_call(
        tiles_kernel,
        out_shape=tuple(out_shape),
        in_specs=in_smem(1),
        out_specs=tuple(in_smem(len(out_shape))),
        compiler_params=pltpu.CompilerParams(vmem_limit_bytes=4 * MIB),
        cost_estimate=pl.CostEstimate(flops=10**6, bytes_accessed=10**5, transcendentals=0),
    )(frame_mask)
    return [tuple(flat[4 * i : 4 * i + 4]) for i in range(len(GROUPS))]


def local(queries, keys, values, frame_mask, w_out):
    xl, c = lax.axis_index("xl"), lax.axis_index("c")

    slots, sent = split(queries, keys, values)
    got = lax.ppermute(sent, "c", shift(NC, 1))
    slots = lax.dynamic_update_slice(slots, got, ((1 - c) * NZ, 0, 0))
    slots, w_out = lax.optimization_barrier((slots, w_out))

    width = w_out.shape[1] // (XL * NC)

    def w_columns(to_xl, to_c):
        return lax.dynamic_slice(w_out, (0, (to_xl * NC + to_c) * width), (w_out.shape[0], width))

    w_here, w_core, w_next, w_last = (
        w_columns(xl, c),
        w_columns(xl, 1 - c),
        w_columns(1 - xl, c),
        w_columns(1 - xl, 1 - c),
    )
    w_here, w_core, w_next, w_last, frame_mask = lax.optimization_barrier(
        (w_here, w_core, w_next, w_last, frame_mask)
    )
    places = [(x, core_) for x in range(XH * XL) for core_ in range(NC)]
    along_x = ("xh", "xl", "c")
    w_next = lax.ppermute(
        w_next, along_x, [(x * NC + k, (x + 1) % 4 * NC + k) for x, k in places]
    )
    w_last = lax.ppermute(
        w_last, along_x, [(x * NC + k, (x + 3) % 4 * NC + 1 - k) for x, k in places]
    )
    w_core = lax.ppermute(w_core, "c", shift(NC, 1))
    groups = live_tiles(frame_mask)

    slots = lax.all_to_all(slots, ("xh", "z"), 0, 0, tiled=True)
    slots, w_here, groups = lax.optimization_barrier((slots, w_here, groups))
    slots, kv = lax.optimization_barrier((slots, slots[:, HALF:]))
    before = lax.ppermute(kv, "y", shift(NY, 1))
    after = lax.ppermute(kv, "y", shift(NY, -1))
    query = slots[:, :HALF]
    query = (query, lax.ppermute(query, "c", shift(NC, 1)))
    state = attend(groups[0], query, [kv], None, False)
    before, after, state = lax.optimization_barrier((before, after, state))
    low = lax.ppermute(before[: ROWS // 2], "y", shift(NY, 1))
    high = lax.ppermute(after[ROWS // 2 :], "y", shift(NY, -1))
    state = attend(groups[1], query, [before, after], state, False)
    low, high, w_next, w_last, w_core = lax.optimization_barrier(
        (low, high, w_next, w_last, w_core)
    )
    here, sent = attend(groups[2], query, [low, high], state, True)
    there = lax.ppermute(sent, "c", shift(NC, 1))
    rows = lax.all_to_all(merge(here, there), ("xh", "z"), 0, 0, tiled=True)
    rows_xl = lax.ppermute(rows, "xl", shift(XL, 1))
    rows_core = lax.ppermute(rows, "c", shift(NC, 1))
    near = project(rows, rows_core, w_here, w_core, None)
    rows_xl, near = lax.optimization_barrier((rows_xl, near))
    rows_both = lax.ppermute(rows_xl, "c", shift(NC, 1))
    return project(rows_xl, rows_both, w_next, w_last, near)


def solution(mesh):
    fine = Mesh(mesh.devices.reshape(XH, NZ, NY, XL, NC), ("xh", "z", "y", "xl", "c"))
    seq, head = ("xh", "z", "y"), ("xl", "c")
    in_specs = (P(seq, head), P(seq, head), P(seq, head), P(), P(head, None))
    return jax.shard_map(
        local, mesh=fine, in_specs=in_specs, out_specs=P(seq, head), check_vma=False
    )
```

```python
import jax
import jax.numpy as jnp
from jax import lax
from jax.experimental import pallas as pl
from jax.experimental.pallas import tpu as pltpu
from jax.sharding import Mesh
from jax.sharding import PartitionSpec as P

HEAD_DIM = 128
BLOCK = 128
HALF = 64
HEADS = 5
XH, NZ, NY, XL, NC = 2, 8, 4, 2, 2
ROWS = XH * NZ
UNROLL = 4
TILE_N = 256
LOW = -1e30
EXP2_SCALE = HEAD_DIM ** (-0.5) * 1.4426950408889634
MIB = 1024 * 1024


def shift(size, by):
    return [(i, (i + by) % size) for i in range(size)]


def in_vmem(count):
    return [pl.BlockSpec(memory_space=pltpu.VMEM)] * count


def in_smem(count):
    return [pl.BlockSpec(memory_space=pltpu.SMEM)] * count


def split_kernel(q_hbm, k_hbm, v_hbm, keep_hbm, send_hbm, whole_ref, keep_ref, send_ref, sems):
    core = lax.axis_index("c")
    mine = pl.ds(pl.multiple_of(core * HALF, HALF), HALF)
    other = pl.ds(pl.multiple_of((1 - core) * HALF, HALF), HALF)
    loads = [
        pltpu.make_async_copy(source, whole_ref.at[t], sems.at[t])
        for t, source in enumerate((q_hbm, k_hbm, v_hbm))
    ]
    for load in loads:
        load.start()
    for t, load in enumerate(loads):
        load.wait()
        rows = slice(t * HALF, (t + 1) * HALF)
        for head in range(HEADS):
            lanes = slice(head * HEAD_DIM, (head + 1) * HEAD_DIM)
            send_ref[head, rows, :] = whole_ref[t, other, lanes]
            keep_ref[head, rows, :] = whole_ref[t, mine, lanes]
    send = pltpu.make_async_copy(send_ref, send_hbm, sems.at[3])
    keep = pltpu.make_async_copy(keep_ref, keep_hbm.at[pl.ds(core * NZ, HEADS)], sems.at[4])
    send.start()
    keep.start()
    send.wait()
    keep.wait()


def split(queries, keys, values):
    anywhere = pl.BlockSpec(memory_space=pl.ANY)
    part = (HEADS, 3 * HALF, HEAD_DIM)
    return pl.pallas_call(
        split_kernel,
        out_shape=(
            jax.ShapeDtypeStruct((ROWS, 3 * HALF, HEAD_DIM), jnp.bfloat16),
            jax.ShapeDtypeStruct(part, jnp.bfloat16),
        ),
        in_specs=[anywhere] * 3,
        out_specs=(anywhere,) * 2,
        scratch_shapes=[
            pltpu.VMEM((3,) + queries.shape, jnp.bfloat16),
            pltpu.VMEM(part, jnp.bfloat16),
            pltpu.VMEM(part, jnp.bfloat16),
            pltpu.SemaphoreType.DMA((5,)),
        ],
        compiler_params=pltpu.CompilerParams(vmem_limit_bytes=56 * MIB),
    )(queries, keys, values)


def score_tiles(steps, tables, q_ref, kv_ref, s_ref, top_ref):
    block_ref, slot_ref, live_ref = tables
    lane = lax.broadcasted_iota(jnp.int32, (BLOCK, BLOCK), 1)

    def score(step, carry):
        tiles = []
        for u in range(UNROLL):
            e = step * UNROLL + u
            key = jnp.concatenate(
                [kv_ref[slot_ref[2 * e], :HALF, :], kv_ref[slot_ref[2 * e + 1], :HALF, :]], axis=0
            )
            s = lax.dot_general(
                q_ref[block_ref[e]],
                key,
                (((1,), (1,)), ((), ())),
                preferred_element_type=jnp.float32,
            )
            s = jnp.where(lane < live_ref[e], s, LOW)
            s_ref[e] = s
            tiles.append(s)
        for u in range(UNROLL):
            block = block_ref[step * UNROLL + u]
            top_ref[block] = jnp.maximum(top_ref[block], tiles[u])
        return carry

    lax.fori_loop(0, steps, score, 0)


def mix_tiles(steps, tables, kv_ref, s_ref, m_ref, l_ref, a_ref):
    block_ref, slot_ref, live_ref = tables

    def mix(step, carry):
        weights, products = [], []
        for u in range(UNROLL):
            e = step * UNROLL + u
            value = jnp.concatenate(
                [kv_ref[slot_ref[2 * e], HALF:, :], kv_ref[slot_ref[2 * e + 1], HALF:, :]], axis=0
            )
            weight = jnp.exp2((s_ref[e] - m_ref[block_ref[e]]) * EXP2_SCALE)
            weights.append(weight)
            products.append(
                jnp.dot(weight.astype(jnp.bfloat16), value, preferred_element_type=jnp.float32)
            )
        for u in range(UNROLL):
            block = block_ref[step * UNROLL + u]
            l_ref[block] = l_ref[block] + weights[u]
            a_ref[block] = a_ref[block] + products[u]
        return carry

    lax.fori_loop(0, steps, mix, 0)


def write_parcels(m_ref, l_ref, a_ref, keep_ref, send_ref):
    lane = lax.broadcasted_iota(jnp.int32, (BLOCK, BLOCK), 1)
    stats = jnp.zeros((BLOCK, BLOCK), jnp.float32)
    for block in range(ROWS):
        total = jnp.sum(l_ref[block], axis=1, keepdims=True)
        stats = jnp.where(lane == block, m_ref[block], stats)
        stats = jnp.where(lane == ROWS + block, total, stats)
        keep_ref[block] = a_ref[block, :HALF, :]
        send_ref[block] = a_ref[block, HALF:, :]
    keep_ref[ROWS] = stats[:HALF]
    send_ref[ROWS] = stats[HALF:]


def attend(tables, query, parts, state, last):
    first = state is None
    slots = sum(part.shape[0] for part in parts)
    most = ROWS * slots // 2
    whole = jax.ShapeDtypeStruct((ROWS, BLOCK, BLOCK), jnp.float32)
    parcel = jax.ShapeDtypeStruct((ROWS + 1, HALF, HEAD_DIM), jnp.float32)

    def kernel(count_ref, block_ref, slot_ref, live_ref, own_ref, other_ref, *refs):
        tables = (block_ref, slot_ref, live_ref)
        part_refs, refs = refs[: len(parts)], refs[len(parts) :]
        if not first:
            (m_in, l_in, a_in), refs = refs[:3], refs[3:]
        if last:
            keep_ref, send_ref, q_ref, kv_ref, s_ref, top_ref, m_ref, l_ref, a_ref = refs
        else:
            m_ref, l_ref, a_ref, q_ref, kv_ref, s_ref, top_ref = refs
        q_ref[:, :HALF, :] = own_ref[...]
        q_ref[:, HALF:, :] = other_ref[...]
        at = 0
        for part in part_refs:
            kv_ref[at : at + part.shape[0]] = part[...]
            at += part.shape[0]
        steps = (count_ref[0] + (UNROLL - 1)) // UNROLL
        top_ref[...] = jnp.full(top_ref.shape, LOW, jnp.float32)
        score_tiles(steps, tables, q_ref, kv_ref, s_ref, top_ref)
        for block in range(ROWS):
            top = jnp.max(top_ref[block], axis=1, keepdims=True)
            if first:
                m_ref[block] = jnp.broadcast_to(top, (BLOCK, BLOCK))
                l_ref[block] = jnp.zeros((BLOCK, BLOCK), jnp.float32)
                a_ref[block] = jnp.zeros((BLOCK, HEAD_DIM), jnp.float32)
            else:
                new = jnp.maximum(m_in[block], top)
                fade = jnp.exp2((m_in[block] - new) * EXP2_SCALE)
                m_ref[block] = new
                l_ref[block] = l_in[block] * fade
                a_ref[block] = a_in[block] * fade
        mix_tiles(steps, tables, kv_ref, s_ref, m_ref, l_ref, a_ref)
        if last:
            write_parcels(m_ref, l_ref, a_ref, keep_ref, send_ref)

    scratch = [
        pltpu.VMEM((ROWS, BLOCK, HEAD_DIM), jnp.bfloat16),
        pltpu.VMEM((slots, 2 * HALF, HEAD_DIM), jnp.bfloat16),
        pltpu.VMEM((most, BLOCK, BLOCK), jnp.float32),
        pltpu.VMEM((ROWS, BLOCK, BLOCK), jnp.float32),
    ]
    if last:
        scratch += [pltpu.VMEM((ROWS, BLOCK, BLOCK), jnp.float32)] * 3
    return pl.pallas_call(
        kernel,
        out_shape=(parcel, parcel) if last else (whole, whole, whole),
        in_specs=in_smem(4) + in_vmem(2 + len(parts) + (0 if first else 3)),
        out_specs=tuple(in_vmem(2 if last else 3)),
        scratch_shapes=scratch,
        compiler_params=pltpu.CompilerParams(vmem_limit_bytes=28 * MIB),
        cost_estimate=pl.CostEstimate(
            flops=len(parts) * 40 * 2 * 128**3,
            bytes_accessed=6 * MIB,
            transcendentals=20 * 128 * 128,
        ),
    )(*tables, *query, *parts, *(() if first else state))


def merge_kernel(here_ref, there_ref, out_ref):
    here, there = here_ref[ROWS], there_ref[ROWS]
    for block in range(ROWS):
        m0, m1 = here[:, block : block + 1], there[:, block : block + 1]
        l0 = here[:, ROWS + block : ROWS + block + 1]
        l1 = there[:, ROWS + block : ROWS + block + 1]
        m = jnp.maximum(m0, m1)
        f0 = jnp.exp2((m0 - m) * EXP2_SCALE)
        f1 = jnp.exp2((m1 - m) * EXP2_SCALE)
        mixed = here_ref[block] * f0 + there_ref[block] * f1
        out_ref[block] = (mixed / (l0 * f0 + l1 * f1)).astype(jnp.bfloat16)


def merge(here, there):
    return pl.pallas_call(
        merge_kernel,
        out_shape=jax.ShapeDtypeStruct((ROWS, HALF, HEAD_DIM), jnp.bfloat16),
        in_specs=in_vmem(2),
        out_specs=in_vmem(1)[0],
        compiler_params=pltpu.CompilerParams(vmem_limit_bytes=4 * MIB),
    )(here, there)


def project(a, b, w_own, w_other, added=None, staged=()):
    deep, width = w_own.shape
    final = added is not None

    def kernel(a_ref, b_ref, w_ref, w2_ref, *refs):
        if final:
            added_ref, refs = refs[0], refs[1:]
        sources, out_ref, targets = (
            refs[: len(staged)],
            refs[len(staged)],
            refs[len(staged) + 1 : 2 * len(staged) + 1],
        )
        rows_ref, sems = refs[2 * len(staged) + 1 :]
        copies = [
            pltpu.make_async_copy(source, target, sems.at[i])
            for i, (source, target) in enumerate(zip(sources, targets))
        ]
        for copy in copies:
            copy.start()
        core = lax.axis_index("c")
        mine = pl.ds(pl.multiple_of(core * HALF, HALF), HALF)
        other = pl.ds(pl.multiple_of((1 - core) * HALF, HALF), HALF)
        for which, head_set in enumerate((core, 1 - core)):
            for head in range(HEADS):
                at = (which * HEADS + head) * HEAD_DIM
                rows_ref[mine, at : at + HEAD_DIM] = a_ref[head_set * HEADS + head]
                rows_ref[other, at : at + HEAD_DIM] = b_ref[head_set * HEADS + head]
        for at in range(0, width, TILE_N):
            lanes = slice(at, at + TILE_N)
            out = jnp.dot(rows_ref[:, :deep], w_ref[:, lanes], preferred_element_type=jnp.float32)
            out = out + jnp.dot(
                rows_ref[:, deep:], w2_ref[:, lanes], preferred_element_type=jnp.float32
            )
            if final:
                out = out + added_ref[:, lanes]
            out_ref[:, lanes] = out.astype(out_ref.dtype)
        for copy in copies:
            copy.wait()

    out = jax.ShapeDtypeStruct((BLOCK, width), jnp.bfloat16 if final else jnp.float32)
    return pl.pallas_call(
        kernel,
        out_shape=(out,) + tuple(jax.ShapeDtypeStruct(x.shape, x.dtype) for x in staged),
        in_specs=in_vmem(5 if final else 4) + [pl.BlockSpec(memory_space=pl.ANY)] * len(staged),
        out_specs=tuple(in_vmem(1 + len(staged))),
        scratch_shapes=[
            pltpu.VMEM((BLOCK, 2 * deep), jnp.bfloat16),
            pltpu.SemaphoreType.DMA((max(len(staged), 1),)),
        ],
        compiler_params=pltpu.CompilerParams(vmem_limit_bytes=8 * MIB),
        cost_estimate=pl.CostEstimate(
            flops=2 * BLOCK * 2 * deep * width, bytes_accessed=4 * MIB, transcendentals=0
        ),
    )(a, b, w_own, w_other, *((added,) if final else ()), *staged)


GROUPS = ((0,), (1, 3), (2,))


def tiles_kernel(mask_ref, *refs):
    y = lax.axis_index("y")
    for group, columns in enumerate(GROUPS):
        count_ref, block_ref, slot_ref, live_ref = refs[4 * group : 4 * group + 4]

        def one_query_block(block, start, columns=columns, refs=(block_ref, slot_ref, live_ref)):
            block_ref, slot_ref, live_ref = refs
            row = block * NY + y
            first = 2 * start
            at = first
            for column, back in enumerate(columns):
                theirs = (y - back + NY) & (NY - 1)
                for i in range(ROWS):
                    slot_ref[at] = column * ROWS + i
                    at = at + jnp.where(mask_ref[row, i * NY + theirs] != 0, 1, 0)
            slot_ref[at] = 0
            tiles = (at - first + 1) >> 1

            def fill(t, carry):
                block_ref[start + t] = block
                live_ref[start + t] = 2 * HALF
                return carry

            lax.fori_loop(0, tiles, fill, 0)

            @pl.when(((at - first) & 1) == 1)
            def _():
                live_ref[start + tiles - 1] = HALF

            return start + tiles

        total = lax.fori_loop(0, ROWS, one_query_block, jnp.int32(0))
        count_ref[0] = total
        for u in range(UNROLL):
            block_ref[total + u] = 0
            live_ref[total + u] = 0
            slot_ref[2 * (total + u)] = 0
            slot_ref[2 * (total + u) + 1] = 0


def live_tiles(frame_mask):
    out_shape = []
    for columns in GROUPS:
        most = ROWS * ROWS * len(columns) // 2 + 128
        out_shape += [
            jax.ShapeDtypeStruct((size,), jnp.int32) for size in (1, most, 2 * most, most)
        ]
    flat = pl.pallas_call(
        tiles_kernel,
        out_shape=tuple(out_shape),
        in_specs=in_smem(1),
        out_specs=tuple(in_smem(len(out_shape))),
        compiler_params=pltpu.CompilerParams(vmem_limit_bytes=4 * MIB),
        cost_estimate=pl.CostEstimate(flops=10**6, bytes_accessed=10**5, transcendentals=0),
    )(frame_mask)
    return [tuple(flat[4 * i : 4 * i + 4]) for i in range(len(GROUPS))]


def local(queries, keys, values, frame_mask, w_out):
    xl, c = lax.axis_index("xl"), lax.axis_index("c")

    width = w_out.shape[1] // (XL * NC)

    def w_columns(w, to_xl, to_c):
        return lax.dynamic_slice(w, (0, (to_xl * NC + to_c) * width), (w.shape[0], width))

    slots, sent = split(queries, keys, values)
    sent, w_out = lax.optimization_barrier((sent, w_out))
    got = lax.ppermute(sent, "c", shift(NC, 1))
    w_core = lax.ppermute(w_columns(w_out, xl, 1 - c), "c", shift(NC, 1))
    slots = lax.dynamic_update_slice(slots, got, ((1 - c) * NZ, 0, 0))
    slots, w_out = lax.optimization_barrier((slots, w_out))
    w_here, w_next, w_last = (
        w_columns(w_out, xl, c),
        w_columns(w_out, 1 - xl, c),
        w_columns(w_out, 1 - xl, 1 - c),
    )
    w_here, w_next, w_last, frame_mask = lax.optimization_barrier(
        (w_here, w_next, w_last, frame_mask)
    )
    places = [(x, core_) for x in range(XH * XL) for core_ in range(NC)]
    along_x = ("xh", "xl", "c")
    w_next = lax.ppermute(
        w_next, along_x, [(x * NC + k, (x + 1) % 4 * NC + k) for x, k in places]
    )
    w_last = lax.ppermute(
        w_last, along_x, [(x * NC + k, (x + 3) % 4 * NC + 1 - k) for x, k in places]
    )
    groups = live_tiles(frame_mask)

    slots = lax.all_to_all(slots, ("xh", "z"), 0, 0, tiled=True)
    slots, w_here, w_core, groups = lax.optimization_barrier((slots, w_here, w_core, groups))
    low, high = slots[: ROWS // 2, HALF:], slots[ROWS // 2 :, HALF:]
    slots, low, high = lax.optimization_barrier((slots, low, high))
    before_low = lax.ppermute(low, "y", shift(NY, 1))
    after_high = lax.ppermute(high, "y", shift(NY, -1))
    query = slots[:, :HALF]
    query = (query, lax.ppermute(query, "c", shift(NC, 1)))
    before_high = lax.ppermute(high, "y", shift(NY, 1))
    after_low = lax.ppermute(low, "y", shift(NY, -1))
    state = attend(groups[0], query, [low, high], None, False)
    before_low, after_high, state = lax.optimization_barrier((before_low, after_high, state))
    far_low = lax.ppermute(before_low, "y", shift(NY, 1))
    far_high = lax.ppermute(after_high, "y", shift(NY, -1))
    state = attend(
        groups[1], query, [before_low, before_high, after_low, after_high], state, False
    )
    here, sent = attend(groups[2], query, [far_low, far_high], state, True)
    there = lax.ppermute(sent, "c", shift(NC, 1))
    there, w_next, w_last = lax.optimization_barrier((there, w_next, w_last))
    rows = lax.all_to_all(merge(here, there), ("xh", "z"), 0, 0, tiled=True)
    rows = rows.reshape(XH, NZ, HALF, HEAD_DIM)[:, :HEADS]
    rows = rows.reshape(XH * HEADS, HALF, HEAD_DIM)
    rows_xl = lax.ppermute(rows, "xl", shift(XL, 1))
    rows_core = lax.ppermute(rows, "c", shift(NC, 1))
    near, w_next, w_last = project(rows, rows_core, w_here, w_core, None, (w_next, w_last))
    rows_xl, near = lax.optimization_barrier((rows_xl, near))
    rows_both = lax.ppermute(rows_xl, "c", shift(NC, 1))
    return project(rows_xl, rows_both, w_next, w_last, near)[0]


def solution(mesh):
    fine = Mesh(mesh.devices.reshape(XH, NZ, NY, XL, NC), ("xh", "z", "y", "xl", "c"))
    seq, head = ("xh", "z", "y"), ("xl", "c")
    in_specs = (P(seq, head), P(seq, head), P(seq, head), P(), P(head, None))
    return jax.shard_map(
        local, mesh=fine, in_specs=in_specs, out_specs=P(seq, head), check_vma=False
    )
```

```python
import jax
import jax.numpy as jnp
from jax import lax
from jax.experimental import pallas as pl
from jax.experimental.pallas import tpu as pltpu
from jax.sharding import Mesh
from jax.sharding import PartitionSpec as P

HEAD_DIM = 128
BLOCK = 128
HALF = 64
HEADS = 5
XH, NZ, NY, XL, NC = 2, 8, 4, 2, 2
ROWS = XH * NZ
UNROLL = 4
TILE_N = 256
LOW = -1e30
EXP2_SCALE = HEAD_DIM ** (-0.5) * 1.4426950408889634
MIB = 1024 * 1024


def shift(size, by):
    return [(i, (i + by) % size) for i in range(size)]


def in_vmem(count):
    return [pl.BlockSpec(memory_space=pltpu.VMEM)] * count


def in_smem(count):
    return [pl.BlockSpec(memory_space=pltpu.SMEM)] * count


def swap_planes(x):
    pairs = [((0, 0), (0, 0)), ((1, 1), (1, 1)), ((0, 1), (1, 0)), ((1, 0), (0, 1))]
    return lax.ppermute(x, ("xh", "c"), [(a * NC + b, d * NC + e) for (a, b), (d, e) in pairs])


def split_kernel(q_hbm, k_hbm, v_hbm, out_hbm, slots_hbm, whole_ref, out_ref, sems):
    del slots_hbm
    loads = [
        pltpu.make_async_copy(source, whole_ref.at[t], sems.at[t])
        for t, source in enumerate((q_hbm, k_hbm, v_hbm))
    ]
    for load in loads:
        load.start()
    for t, load in enumerate(loads):
        load.wait()
        for head in range(HEADS):
            lanes = slice(head * HEAD_DIM, (head + 1) * HEAD_DIM)
            out_ref[head, t * BLOCK : (t + 1) * BLOCK, :] = whole_ref[t, :, lanes]
    out = pltpu.make_async_copy(out_ref, out_hbm, sems.at[3])
    out.start()
    out.wait()


def split(queries, keys, values):
    anywhere = pl.BlockSpec(memory_space=pl.ANY)
    part = (HEADS, 3 * BLOCK, HEAD_DIM)
    return pl.pallas_call(
        split_kernel,
        out_shape=(
            jax.ShapeDtypeStruct(part, jnp.bfloat16),
            jax.ShapeDtypeStruct((NZ,) + part[1:], jnp.bfloat16),
        ),
        in_specs=[anywhere] * 3,
        out_specs=(anywhere,) * 2,
        scratch_shapes=[
            pltpu.VMEM((3,) + queries.shape, jnp.bfloat16),
            pltpu.VMEM(part, jnp.bfloat16),
            pltpu.SemaphoreType.DMA((4,)),
        ],
        compiler_params=pltpu.CompilerParams(vmem_limit_bytes=56 * MIB),
    )(queries, keys, values)


def score_tiles(count, tables, q_ref, kv_ref, s_ref, top_ref):
    block_ref, slot_ref = tables

    def score(step, carry):
        tiles = []
        for u in range(UNROLL):
            e = step * UNROLL + u
            s = lax.dot_general(
                q_ref[block_ref[e]],
                kv_ref[slot_ref[e], :BLOCK, :],
                (((1,), (1,)), ((), ())),
                preferred_element_type=jnp.float32,
            )
            s = jnp.where(e < count, s, LOW)
            s_ref[e] = s
            tiles.append(s)
        for u in range(UNROLL):
            block = block_ref[step * UNROLL + u]
            top_ref[block] = jnp.maximum(top_ref[block], tiles[u])
        return carry

    lax.fori_loop(0, (count + (UNROLL - 1)) // UNROLL, score, 0)


def mix_tiles(count, tables, kv_ref, s_ref, m_ref, l_ref, a_ref):
    block_ref, slot_ref = tables

    def mix(step, carry):
        weights, products = [], []
        for u in range(UNROLL):
            e = step * UNROLL + u
            weight = jnp.exp2((s_ref[e] - m_ref[block_ref[e]]) * EXP2_SCALE)
            weights.append(weight)
            products.append(
                jnp.dot(
                    weight.astype(jnp.bfloat16),
                    kv_ref[slot_ref[e], BLOCK:, :],
                    preferred_element_type=jnp.float32,
                )
            )
        for u in range(UNROLL):
            block = block_ref[step * UNROLL + u]
            l_ref[block] = l_ref[block] + weights[u]
            a_ref[block] = a_ref[block] + products[u]
        return carry

    lax.fori_loop(0, (count + (UNROLL - 1)) // UNROLL, mix, 0)


def write_parcels(m_ref, l_ref, a_ref, stats_ref, keep_ref, send_ref):
    core = lax.axis_index("c")
    mine = pl.ds(pl.multiple_of(core * HALF, HALF), HALF)
    other = pl.ds(pl.multiple_of((1 - core) * HALF, HALF), HALF)
    lane = lax.broadcasted_iota(jnp.int32, (BLOCK, BLOCK), 1)
    stats = jnp.zeros((BLOCK, BLOCK), jnp.float32)
    for block in range(ROWS):
        total = jnp.sum(l_ref[block], axis=1, keepdims=True)
        stats = jnp.where(lane == block, m_ref[block], stats)
        stats = jnp.where(lane == ROWS + block, total, stats)
        keep_ref[block] = a_ref[block, mine, :]
        send_ref[block] = a_ref[block, other, :]
    stats_ref[...] = stats
    keep_ref[ROWS] = stats_ref[mine, :]
    send_ref[ROWS] = stats_ref[other, :]


def attend(tables, query, parts, state, last):
    first = state is None
    slots = sum(part.shape[0] for part in parts)
    most = ROWS * slots
    whole = jax.ShapeDtypeStruct((ROWS, BLOCK, BLOCK), jnp.float32)
    parcel = jax.ShapeDtypeStruct((ROWS + 1, HALF, HEAD_DIM), jnp.float32)

    def kernel(count_ref, block_ref, slot_ref, own_ref, other_ref, *refs):
        tables = (block_ref, slot_ref)
        core = lax.axis_index("c")
        part_refs, refs = refs[: len(parts)], refs[len(parts) :]
        if not first:
            (m_in, l_in, a_in), refs = refs[:3], refs[3:]
        if last:
            keep_ref, send_ref, q_ref, kv_ref, s_ref, top_ref, m_ref, l_ref, a_ref, stats_ref = refs
        else:
            m_ref, l_ref, a_ref, q_ref, kv_ref, s_ref, top_ref = refs
        q_ref[pl.ds(core * NZ, NZ)] = own_ref[...]
        q_ref[pl.ds((1 - core) * NZ, NZ)] = other_ref[...]
        at = 0
        for part in part_refs:
            kv_ref[at : at + part.shape[0]] = part[...]
            at += part.shape[0]
        count = count_ref[0]
        top_ref[...] = jnp.full(top_ref.shape, LOW, jnp.float32)
        score_tiles(count, tables, q_ref, kv_ref, s_ref, top_ref)
        for block in range(ROWS):
            top = jnp.max(top_ref[block], axis=1, keepdims=True)
            if first:
                m_ref[block] = jnp.broadcast_to(top, (BLOCK, BLOCK))
                l_ref[block] = jnp.zeros((BLOCK, BLOCK), jnp.float32)
                a_ref[block] = jnp.zeros((BLOCK, HEAD_DIM), jnp.float32)
            else:
                new = jnp.maximum(m_in[block], top)
                fade = jnp.exp2((m_in[block] - new) * EXP2_SCALE)
                m_ref[block] = new
                l_ref[block] = l_in[block] * fade
                a_ref[block] = a_in[block] * fade
        mix_tiles(count, tables, kv_ref, s_ref, m_ref, l_ref, a_ref)
        if last:
            write_parcels(m_ref, l_ref, a_ref, stats_ref, keep_ref, send_ref)

    scratch = [
        pltpu.VMEM((ROWS, BLOCK, HEAD_DIM), jnp.bfloat16),
        pltpu.VMEM((slots, 2 * BLOCK, HEAD_DIM), jnp.bfloat16),
        pltpu.VMEM((most, BLOCK, BLOCK), jnp.float32),
        pltpu.VMEM((ROWS, BLOCK, BLOCK), jnp.float32),
    ]
    if last:
        scratch += [pltpu.VMEM((ROWS, BLOCK, BLOCK), jnp.float32)] * 3
        scratch += [pltpu.VMEM((BLOCK, BLOCK), jnp.float32)]
    return pl.pallas_call(
        kernel,
        out_shape=(parcel, parcel) if last else (whole, whole, whole),
        in_specs=in_smem(3) + in_vmem(2 + len(parts) + (0 if first else 3)),
        out_specs=tuple(in_vmem(2 if last else 3)),
        scratch_shapes=scratch,
        compiler_params=pltpu.CompilerParams(vmem_limit_bytes=28 * MIB),
        cost_estimate=pl.CostEstimate(
            flops=len(parts) * 40 * 2 * 128**3,
            bytes_accessed=6 * MIB,
            transcendentals=20 * 128 * 128,
        ),
    )(*tables, *query, *parts, *(() if first else state))


def merge_kernel(here_ref, there_ref, out_ref):
    here, there = here_ref[ROWS], there_ref[ROWS]
    for block in range(ROWS):
        m0, m1 = here[:, block : block + 1], there[:, block : block + 1]
        l0 = here[:, ROWS + block : ROWS + block + 1]
        l1 = there[:, ROWS + block : ROWS + block + 1]
        m = jnp.maximum(m0, m1)
        f0 = jnp.exp2((m0 - m) * EXP2_SCALE)
        f1 = jnp.exp2((m1 - m) * EXP2_SCALE)
        mixed = here_ref[block] * f0 + there_ref[block] * f1
        out_ref[block] = (mixed / (l0 * f0 + l1 * f1)).astype(jnp.bfloat16)


def merge(here, there):
    return pl.pallas_call(
        merge_kernel,
        out_shape=jax.ShapeDtypeStruct((ROWS, HALF, HEAD_DIM), jnp.bfloat16),
        in_specs=in_vmem(2),
        out_specs=in_vmem(1)[0],
        compiler_params=pltpu.CompilerParams(vmem_limit_bytes=4 * MIB),
    )(here, there)


def project(a, b, w_own, w_other, added=None, staged=()):
    deep, width = w_own.shape
    final = added is not None

    def kernel(a_ref, b_ref, w_ref, w2_ref, *refs):
        if final:
            added_ref, refs = refs[0], refs[1:]
        sources, out_ref, targets = (
            refs[: len(staged)],
            refs[len(staged)],
            refs[len(staged) + 1 : 2 * len(staged) + 1],
        )
        rows_ref, sems = refs[2 * len(staged) + 1 :]
        copies = [
            pltpu.make_async_copy(source, target, sems.at[i])
            for i, (source, target) in enumerate(zip(sources, targets))
        ]
        for copy in copies:
            copy.start()
        core = lax.axis_index("c")
        mine = pl.ds(pl.multiple_of(core * HALF, HALF), HALF)
        other = pl.ds(pl.multiple_of((1 - core) * HALF, HALF), HALF)
        for which, head_set in enumerate((core, 1 - core)):
            for head in range(HEADS):
                at = (which * HEADS + head) * HEAD_DIM
                rows_ref[mine, at : at + HEAD_DIM] = a_ref[head_set * HEADS + head]
                rows_ref[other, at : at + HEAD_DIM] = b_ref[head_set * HEADS + head]
        for at in range(0, width, TILE_N):
            lanes = slice(at, at + TILE_N)
            out = jnp.dot(rows_ref[:, :deep], w_ref[:, lanes], preferred_element_type=jnp.float32)
            out = out + jnp.dot(
                rows_ref[:, deep:], w2_ref[:, lanes], preferred_element_type=jnp.float32
            )
            if final:
                out = out + added_ref[:, lanes]
            out_ref[:, lanes] = out.astype(out_ref.dtype)
        for copy in copies:
            copy.wait()

    out = jax.ShapeDtypeStruct((BLOCK, width), jnp.bfloat16 if final else jnp.float32)
    return pl.pallas_call(
        kernel,
        out_shape=(out,) + tuple(jax.ShapeDtypeStruct(x.shape, x.dtype) for x in staged),
        in_specs=in_vmem(5 if final else 4) + [pl.BlockSpec(memory_space=pl.ANY)] * len(staged),
        out_specs=tuple(in_vmem(1 + len(staged))),
        scratch_shapes=[
            pltpu.VMEM((BLOCK, 2 * deep), jnp.bfloat16),
            pltpu.SemaphoreType.DMA((max(len(staged), 1),)),
        ],
        compiler_params=pltpu.CompilerParams(vmem_limit_bytes=8 * MIB),
        cost_estimate=pl.CostEstimate(
            flops=2 * BLOCK * 2 * deep * width, bytes_accessed=4 * MIB, transcendentals=0
        ),
    )(a, b, w_own, w_other, *((added,) if final else ()), *staged)


GROUPS = ((0,), (1, 3), (2,))


def tiles_kernel(mask_ref, *refs):
    y, core = lax.axis_index("y"), lax.axis_index("c")
    for group, columns in enumerate(GROUPS):
        count_ref, block_ref, slot_ref = refs[3 * group : 3 * group + 3]

        def one_query_block(block, at, columns=columns, refs=(block_ref, slot_ref)):
            block_ref, slot_ref = refs
            row = block * NY + y
            for column, back in enumerate(columns):
                first = core * (NZ * NY) + ((y - back + NY) & (NY - 1))
                for i in range(NZ):
                    block_ref[at] = block
                    slot_ref[at] = column * NZ + i
                    at = at + jnp.where(mask_ref[row, first + i * NY] != 0, 1, 0)
            return at

        total = lax.fori_loop(0, ROWS, one_query_block, jnp.int32(0))
        count_ref[0] = total
        for u in range(UNROLL):
            block_ref[total + u] = 0
            slot_ref[total + u] = 0


def live_tiles(frame_mask):
    out_shape = []
    for columns in GROUPS:
        most = ROWS * NZ * len(columns) + 128
        out_shape += [jax.ShapeDtypeStruct((size,), jnp.int32) for size in (1, most, most)]
    flat = pl.pallas_call(
        tiles_kernel,
        out_shape=tuple(out_shape),
        in_specs=in_smem(1),
        out_specs=tuple(in_smem(len(out_shape))),
        compiler_params=pltpu.CompilerParams(vmem_limit_bytes=4 * MIB),
        cost_estimate=pl.CostEstimate(flops=10**6, bytes_accessed=10**5, transcendentals=0),
    )(frame_mask)
    return [tuple(flat[3 * i : 3 * i + 3]) for i in range(len(GROUPS))]


def local(queries, keys, values, frame_mask, w_out):
    xl, c = lax.axis_index("xl"), lax.axis_index("c")

    width = w_out.shape[1] // (XL * NC)

    def w_columns(w, to_xl, to_c):
        return lax.dynamic_slice(w, (0, (to_xl * NC + to_c) * width), (w.shape[0], width))

    sent, slots = split(queries, keys, values)
    sent, w_out = lax.optimization_barrier((sent, w_out))
    got = swap_planes(sent)
    w_core = lax.ppermute(w_columns(w_out, xl, 1 - c), "c", shift(NC, 1))
    slots = lax.dynamic_update_slice(slots, got, (0, 0, 0))
    slots, w_out = lax.optimization_barrier((slots, w_out))
    w_here, w_next, w_last = (
        w_columns(w_out, xl, c),
        w_columns(w_out, 1 - xl, c),
        w_columns(w_out, 1 - xl, 1 - c),
    )
    w_here, w_next, w_last, frame_mask = lax.optimization_barrier(
        (w_here, w_next, w_last, frame_mask)
    )
    places = [(x, core_) for x in range(XH * XL) for core_ in range(NC)]
    along_x = ("xh", "xl", "c")
    w_next = lax.ppermute(
        w_next, along_x, [(x * NC + k, (x + 1) % 4 * NC + k) for x, k in places]
    )
    w_last = lax.ppermute(
        w_last, along_x, [(x * NC + k, (x + 3) % 4 * NC + 1 - k) for x, k in places]
    )
    groups = live_tiles(frame_mask)

    slots = lax.all_to_all(slots, "z", 0, 0, tiled=True)
    slots, w_here, w_core, groups = lax.optimization_barrier((slots, w_here, w_core, groups))
    low, high = slots[: NZ // 2, BLOCK:], slots[NZ // 2 :, BLOCK:]
    slots, low, high = lax.optimization_barrier((slots, low, high))
    before_low = lax.ppermute(low, "y", shift(NY, 1))
    after_high = lax.ppermute(high, "y", shift(NY, -1))
    query = slots[:, :BLOCK]
    query = (query, lax.ppermute(query, "c", shift(NC, 1)))
    before_high = lax.ppermute(high, "y", shift(NY, 1))
    after_low = lax.ppermute(low, "y", shift(NY, -1))
    state = attend(groups[0], query, [low, high], None, False)
    before_low, after_high, state = lax.optimization_barrier((before_low, after_high, state))
    far_low = lax.ppermute(before_low, "y", shift(NY, 1))
    far_high = lax.ppermute(after_high, "y", shift(NY, -1))
    state = attend(
        groups[1], query, [before_low, before_high, after_low, after_high], state, False
    )
    here, sent = attend(groups[2], query, [far_low, far_high], state, True)
    there = lax.ppermute(sent, "c", shift(NC, 1))
    there, w_next, w_last = lax.optimization_barrier((there, w_next, w_last))
    rows = lax.all_to_all(merge(here, there), ("xh", "z"), 0, 0, tiled=True)
    rows = rows.reshape(XH, NZ, HALF, HEAD_DIM)[:, :HEADS]
    rows = rows.reshape(XH * HEADS, HALF, HEAD_DIM)
    rows_xl = lax.ppermute(rows, "xl", shift(XL, 1))
    rows_core = lax.ppermute(rows, "c", shift(NC, 1))
    near, w_next, w_last = project(rows, rows_core, w_here, w_core, None, (w_next, w_last))
    rows_xl, near = lax.optimization_barrier((rows_xl, near))
    rows_both = lax.ppermute(rows_xl, "c", shift(NC, 1))
    return project(rows_xl, rows_both, w_next, w_last, near)[0]


def solution(mesh):
    fine = Mesh(mesh.devices.reshape(XH, NZ, NY, XL, NC), ("xh", "z", "y", "xl", "c"))
    seq, head = ("xh", "z", "y"), ("xl", "c")
    in_specs = (P(seq, head), P(seq, head), P(seq, head), P(), P(head, None))
    return jax.shard_map(
        local, mesh=fine, in_specs=in_specs, out_specs=P(seq, head), check_vma=False
    )
```

```python
import jax
import jax.numpy as jnp
from jax import lax
from jax.experimental import pallas as pl
from jax.experimental.pallas import tpu as pltpu
from jax.sharding import Mesh
from jax.sharding import PartitionSpec as P

HEAD_DIM = 128
BLOCK = 128
HEADS = 5
XH, NZ, NY, XL, NC = 2, 8, 4, 2, 2
ROWS = XH * NZ
UNROLL = 4
TILE_N = 256
LOW = -1e30
EXP2_SCALE = HEAD_DIM ** (-0.5) * 1.4426950408889634
MIB = 1024 * 1024


def shift(size, by):
    return [(i, (i + by) % size) for i in range(size)]


def in_vmem(count):
    return [pl.BlockSpec(memory_space=pltpu.VMEM)] * count


def in_smem(count):
    return [pl.BlockSpec(memory_space=pltpu.SMEM)] * count


def split_kernel(q_hbm, k_hbm, v_hbm, slots_hbm, whole_ref, out_ref, sems):
    loads = [
        pltpu.make_async_copy(source, whole_ref.at[t], sems.at[t])
        for t, source in enumerate((q_hbm, k_hbm, v_hbm))
    ]
    for load in loads:
        load.start()
    for t, load in enumerate(loads):
        load.wait()
        for head in range(HEADS):
            lanes = slice(head * HEAD_DIM, (head + 1) * HEAD_DIM)
            out_ref[head, t * BLOCK : (t + 1) * BLOCK, :] = whole_ref[t, :, lanes]
    out = pltpu.make_async_copy(out_ref, slots_hbm.at[:HEADS], sems.at[3])
    out.start()
    out.wait()


def split(queries, keys, values):
    anywhere = pl.BlockSpec(memory_space=pl.ANY)
    part = (3 * BLOCK, HEAD_DIM)
    return pl.pallas_call(
        split_kernel,
        out_shape=jax.ShapeDtypeStruct((NZ,) + part, jnp.bfloat16),
        in_specs=[anywhere] * 3,
        out_specs=anywhere,
        scratch_shapes=[
            pltpu.VMEM((3,) + queries.shape, jnp.bfloat16),
            pltpu.VMEM((HEADS,) + part, jnp.bfloat16),
            pltpu.SemaphoreType.DMA((4,)),
        ],
        compiler_params=pltpu.CompilerParams(vmem_limit_bytes=56 * MIB),
    )(queries, keys, values)


def score_tiles(count, tables, q_ref, kv_ref, s_ref, top_ref):
    block_ref, slot_ref = tables

    def score(step, carry):
        tiles = []
        for u in range(UNROLL):
            e = step * UNROLL + u
            s = lax.dot_general(
                q_ref[block_ref[e]],
                kv_ref[slot_ref[e], :BLOCK, :],
                (((1,), (1,)), ((), ())),
                preferred_element_type=jnp.float32,
            )
            s = jnp.where(e < count, s, LOW)
            s_ref[e] = s
            tiles.append(s)
        for u in range(UNROLL):
            block = block_ref[step * UNROLL + u]
            top_ref[block] = jnp.maximum(top_ref[block], tiles[u])
        return carry

    lax.fori_loop(0, (count + (UNROLL - 1)) // UNROLL, score, 0)


def mix_tiles(count, tables, kv_ref, s_ref, m_ref, l_ref, a_ref):
    block_ref, slot_ref = tables

    def mix(step, carry):
        weights, products = [], []
        for u in range(UNROLL):
            e = step * UNROLL + u
            weight = jnp.exp2((s_ref[e] - m_ref[block_ref[e]]) * EXP2_SCALE)
            weights.append(weight)
            products.append(
                jnp.dot(
                    weight.astype(jnp.bfloat16),
                    kv_ref[slot_ref[e], BLOCK:, :],
                    preferred_element_type=jnp.float32,
                )
            )
        for u in range(UNROLL):
            block = block_ref[step * UNROLL + u]
            l_ref[block] = l_ref[block] + weights[u]
            a_ref[block] = a_ref[block] + products[u]
        return carry

    lax.fori_loop(0, (count + (UNROLL - 1)) // UNROLL, mix, 0)


def write_parcels(m_ref, l_ref, a_ref, keep_ref, keep_stats_ref, send_ref, send_stats_ref):
    plane = lax.axis_index("xh")
    lane = lax.broadcasted_iota(jnp.int32, (BLOCK, BLOCK), 1)

    def stats_of(first):
        stats = jnp.zeros((BLOCK, BLOCK), jnp.float32)
        for i in range(NZ):
            total = jnp.sum(l_ref[first + i], axis=1, keepdims=True)
            stats = jnp.where(lane == i, m_ref[first + i], stats)
            stats = jnp.where(lane == NZ + i, total, stats)
        return stats

    own, other = plane * NZ, (1 - plane) * NZ
    for i in range(NZ):
        keep_ref[i] = a_ref[own + i]
        send_ref[i] = a_ref[other + i].astype(jnp.bfloat16)
    keep_stats_ref[...] = stats_of(own)
    send_stats_ref[...] = stats_of(other).T[: 2 * NZ]


def attend(tables, query, parts, state, last):
    first = state is None
    slots = sum(part.shape[0] for part in parts)
    most = ROWS * slots
    whole = jax.ShapeDtypeStruct((ROWS, BLOCK, BLOCK), jnp.float32)
    parcels = (
        jax.ShapeDtypeStruct((NZ, BLOCK, HEAD_DIM), jnp.float32),
        jax.ShapeDtypeStruct((BLOCK, BLOCK), jnp.float32),
        jax.ShapeDtypeStruct((NZ, BLOCK, HEAD_DIM), jnp.bfloat16),
        jax.ShapeDtypeStruct((2 * NZ, BLOCK), jnp.float32),
    )

    def kernel(count_ref, block_ref, slot_ref, own_ref, other_ref, *refs):
        tables = (block_ref, slot_ref)
        plane = lax.axis_index("xh")
        part_refs, refs = refs[: len(parts)], refs[len(parts) :]
        if not first:
            (m_in, l_in, a_in), refs = refs[:3], refs[3:]
        if last:
            parcel_refs, refs = refs[:4], refs[4:]
            q_ref, kv_ref, s_ref, top_ref, m_ref, l_ref, a_ref = refs
        else:
            m_ref, l_ref, a_ref, q_ref, kv_ref, s_ref, top_ref = refs
        q_ref[pl.ds(plane * NZ, NZ)] = own_ref[...]
        q_ref[pl.ds((1 - plane) * NZ, NZ)] = other_ref[...]
        at = 0
        for part in part_refs:
            kv_ref[at : at + part.shape[0]] = part[...]
            at += part.shape[0]
        count = count_ref[0]
        top_ref[...] = jnp.full(top_ref.shape, LOW, jnp.float32)
        score_tiles(count, tables, q_ref, kv_ref, s_ref, top_ref)
        for block in range(ROWS):
            top = jnp.max(top_ref[block], axis=1, keepdims=True)
            if first:
                m_ref[block] = jnp.broadcast_to(top, (BLOCK, BLOCK))
                l_ref[block] = jnp.zeros((BLOCK, BLOCK), jnp.float32)
                a_ref[block] = jnp.zeros((BLOCK, HEAD_DIM), jnp.float32)
            else:
                new = jnp.maximum(m_in[block], top)
                fade = jnp.exp2((m_in[block] - new) * EXP2_SCALE)
                m_ref[block] = new
                l_ref[block] = l_in[block] * fade
                a_ref[block] = a_in[block] * fade
        mix_tiles(count, tables, kv_ref, s_ref, m_ref, l_ref, a_ref)
        if last:
            write_parcels(m_ref, l_ref, a_ref, *parcel_refs)

    scratch = [
        pltpu.VMEM((ROWS, BLOCK, HEAD_DIM), jnp.bfloat16),
        pltpu.VMEM((slots, 2 * BLOCK, HEAD_DIM), jnp.bfloat16),
        pltpu.VMEM((most, BLOCK, BLOCK), jnp.float32),
        pltpu.VMEM((ROWS, BLOCK, BLOCK), jnp.float32),
    ]
    if last:
        scratch += [pltpu.VMEM((ROWS, BLOCK, BLOCK), jnp.float32)] * 3
    return pl.pallas_call(
        kernel,
        out_shape=parcels if last else (whole, whole, whole),
        in_specs=in_smem(3) + in_vmem(2 + len(parts) + (0 if first else 3)),
        out_specs=tuple(in_vmem(4 if last else 3)),
        scratch_shapes=scratch,
        compiler_params=pltpu.CompilerParams(vmem_limit_bytes=28 * MIB),
        cost_estimate=pl.CostEstimate(
            flops=len(parts) * 40 * 2 * 128**3,
            bytes_accessed=6 * MIB,
            transcendentals=20 * 128 * 128,
        ),
    )(*tables, *query, *parts, *(() if first else state))


def merge_kernel(here_ref, here_stats_ref, there_ref, there_stats_ref, out_ref, rows_ref):
    rows_ref[: 2 * NZ, :] = there_stats_ref[...]
    rows_ref[2 * NZ :, :] = jnp.zeros((BLOCK - 2 * NZ, BLOCK), jnp.float32)
    here, there = here_stats_ref[...], rows_ref[...].T
    for i in range(NZ):
        m0, m1 = here[:, i : i + 1], there[:, i : i + 1]
        l0, l1 = here[:, NZ + i : NZ + i + 1], there[:, NZ + i : NZ + i + 1]
        m = jnp.maximum(m0, m1)
        f0 = jnp.exp2((m0 - m) * EXP2_SCALE)
        f1 = jnp.exp2((m1 - m) * EXP2_SCALE)
        mixed = here_ref[i] * f0 + there_ref[i].astype(jnp.float32) * f1
        out_ref[i] = (mixed / (l0 * f0 + l1 * f1)).astype(jnp.bfloat16)


def merge(here, here_stats, there, there_stats):
    return pl.pallas_call(
        merge_kernel,
        out_shape=jax.ShapeDtypeStruct(here.shape, jnp.bfloat16),
        in_specs=in_vmem(4),
        out_specs=in_vmem(1)[0],
        scratch_shapes=[pltpu.VMEM((BLOCK, BLOCK), jnp.float32)],
        compiler_params=pltpu.CompilerParams(vmem_limit_bytes=4 * MIB),
    )(here, here_stats, there, there_stats)


def project(a, b, w_own, w_other, added=None, staged=()):
    deep, width = w_own.shape
    final = added is not None

    def kernel(a_ref, b_ref, w_ref, w2_ref, *refs):
        if final:
            added_ref, refs = refs[0], refs[1:]
        sources, out_ref, targets = (
            refs[: len(staged)],
            refs[len(staged)],
            refs[len(staged) + 1 : 2 * len(staged) + 1],
        )
        rows_ref, sems = refs[2 * len(staged) + 1 :]
        copies = [
            pltpu.make_async_copy(source, target, sems.at[i])
            for i, (source, target) in enumerate(zip(sources, targets))
        ]
        for copy in copies:
            copy.start()
        for which, ref in enumerate((a_ref, b_ref)):
            for head in range(HEADS):
                at = (which * HEADS + head) * HEAD_DIM
                rows_ref[:, at : at + HEAD_DIM] = ref[head]
        for at in range(0, width, TILE_N):
            lanes = slice(at, at + TILE_N)
            out = jnp.dot(rows_ref[:, :deep], w_ref[:, lanes], preferred_element_type=jnp.float32)
            out = out + jnp.dot(
                rows_ref[:, deep:], w2_ref[:, lanes], preferred_element_type=jnp.float32
            )
            if final:
                out = out + added_ref[:, lanes]
            out_ref[:, lanes] = out.astype(out_ref.dtype)
        for copy in copies:
            copy.wait()

    out = jax.ShapeDtypeStruct((BLOCK, width), jnp.bfloat16 if final else jnp.float32)
    return pl.pallas_call(
        kernel,
        out_shape=(out,) + tuple(jax.ShapeDtypeStruct(x.shape, x.dtype) for x in staged),
        in_specs=in_vmem(5 if final else 4) + [pl.BlockSpec(memory_space=pl.ANY)] * len(staged),
        out_specs=tuple(in_vmem(1 + len(staged))),
        scratch_shapes=[
            pltpu.VMEM((BLOCK, 2 * deep), jnp.bfloat16),
            pltpu.SemaphoreType.DMA((max(len(staged), 1),)),
        ],
        compiler_params=pltpu.CompilerParams(vmem_limit_bytes=8 * MIB),
        cost_estimate=pl.CostEstimate(
            flops=2 * BLOCK * 2 * deep * width, bytes_accessed=4 * MIB, transcendentals=0
        ),
    )(a, b, w_own, w_other, *((added,) if final else ()), *staged)


GROUPS = ((0,), (1, 3), (2,))


def tiles_kernel(mask_ref, *refs):
    y, plane = lax.axis_index("y"), lax.axis_index("xh")
    for group, columns in enumerate(GROUPS):
        count_ref, block_ref, slot_ref = refs[3 * group : 3 * group + 3]

        def one_query_block(block, at, columns=columns, refs=(block_ref, slot_ref)):
            block_ref, slot_ref = refs
            row = block * NY + y
            for column, back in enumerate(columns):
                first = plane * (NZ * NY) + ((y - back + NY) & (NY - 1))
                for i in range(NZ):
                    block_ref[at] = block
                    slot_ref[at] = column * NZ + i
                    at = at + jnp.where(mask_ref[row, first + i * NY] != 0, 1, 0)
            return at

        total = lax.fori_loop(0, ROWS, one_query_block, jnp.int32(0))
        count_ref[0] = total
        for u in range(UNROLL):
            block_ref[total + u] = 0
            slot_ref[total + u] = 0


def live_tiles(frame_mask):
    out_shape = []
    for columns in GROUPS:
        most = ROWS * NZ * len(columns) + 128
        out_shape += [jax.ShapeDtypeStruct((size,), jnp.int32) for size in (1, most, most)]
    flat = pl.pallas_call(
        tiles_kernel,
        out_shape=tuple(out_shape),
        in_specs=in_smem(1),
        out_specs=tuple(in_smem(len(out_shape))),
        compiler_params=pltpu.CompilerParams(vmem_limit_bytes=4 * MIB),
        cost_estimate=pl.CostEstimate(flops=10**6, bytes_accessed=10**5, transcendentals=0),
    )(frame_mask)
    return [tuple(flat[3 * i : 3 * i + 3]) for i in range(len(GROUPS))]


def local(queries, keys, values, frame_mask, w_out):
    xl, c = lax.axis_index("xl"), lax.axis_index("c")

    width = w_out.shape[1] // (XL * NC)

    def w_columns(w, to_xl, to_c):
        return lax.dynamic_slice(w, (0, (to_xl * NC + to_c) * width), (w.shape[0], width))

    slots = split(queries, keys, values)
    slots, w_out = lax.optimization_barrier((slots, w_out))
    w_here, w_core, w_next, w_last = (
        w_columns(w_out, xl, c),
        w_columns(w_out, xl, 1 - c),
        w_columns(w_out, 1 - xl, c),
        w_columns(w_out, 1 - xl, 1 - c),
    )
    w_here, w_core, w_next, w_last, frame_mask = lax.optimization_barrier(
        (w_here, w_core, w_next, w_last, frame_mask)
    )
    places = [(x, core_) for x in range(XH * XL) for core_ in range(NC)]
    along_x = ("xh", "xl", "c")
    w_next = lax.ppermute(
        w_next, along_x, [(x * NC + k, (x + 1) % 4 * NC + k) for x, k in places]
    )
    w_last = lax.ppermute(
        w_last, along_x, [(x * NC + k, (x + 3) % 4 * NC + 1 - k) for x, k in places]
    )
    groups = live_tiles(frame_mask)

    slots = lax.all_to_all(slots, "z", 0, 0, tiled=True)
    slots, w_here, w_core, groups = lax.optimization_barrier((slots, w_here, w_core, groups))
    low, high = slots[: NZ // 2, BLOCK:], slots[NZ // 2 :, BLOCK:]
    slots, low, high = lax.optimization_barrier((slots, low, high))
    before_low = lax.ppermute(low, "y", shift(NY, 1))
    after_high = lax.ppermute(high, "y", shift(NY, -1))
    query = slots[:, :BLOCK]
    query = (query, lax.ppermute(query, "xh", shift(XH, 1)))
    before_high = lax.ppermute(high, "y", shift(NY, 1))
    after_low = lax.ppermute(low, "y", shift(NY, -1))
    state = attend(groups[0], query, [low, high], None, False)
    before_low, after_high, state = lax.optimization_barrier((before_low, after_high, state))
    far_low = lax.ppermute(before_low, "y", shift(NY, 1))
    far_high = lax.ppermute(after_high, "y", shift(NY, -1))
    state = attend(
        groups[1], query, [before_low, before_high, after_low, after_high], state, False
    )
    here, here_stats, sent, sent_stats = attend(
        groups[2], query, [far_low, far_high], state, True
    )
    sent, w_core, w_next, w_last = lax.optimization_barrier((sent, w_core, w_next, w_last))
    w_core = lax.ppermute(w_core, "c", shift(NC, 1))
    there = lax.ppermute(sent, "xh", shift(XH, 1))
    there_stats = lax.ppermute(sent_stats, "xh", shift(XH, 1))
    heads = merge(here, here_stats, there, there_stats)
    heads = lax.all_to_all(heads, "z", 0, 0, tiled=True)[:HEADS]
    heads_xl = lax.ppermute(heads, "xl", shift(XL, 1))
    heads_core = lax.ppermute(heads, "c", shift(NC, 1))
    near, w_next, w_last = project(heads, heads_core, w_here, w_core, None, (w_next, w_last))
    heads_xl, near = lax.optimization_barrier((heads_xl, near))
    heads_both = lax.ppermute(heads_xl, "c", shift(NC, 1))
    return project(heads_xl, heads_both, w_next, w_last, near)[0]


def solution(mesh):
    fine = Mesh(mesh.devices.reshape(XH, NZ, NY, XL, NC), ("xh", "z", "y", "xl", "c"))
    seq, head = ("xh", "z", "y"), ("xl", "c")
    in_specs = (P(seq, head), P(seq, head), P(seq, head), P(), P(head, None))
    return jax.shard_map(
        local, mesh=fine, in_specs=in_specs, out_specs=P(seq, head), check_vma=False
    )
```

```python
import jax
import jax.numpy as jnp
from jax import lax
from jax.experimental import pallas as pl
from jax.experimental.pallas import tpu as pltpu
from jax.sharding import Mesh
from jax.sharding import PartitionSpec as P

HEAD_DIM = 128
BLOCK = 128
HEADS = 5
XH, NZ, NY, XL, NC = 2, 8, 4, 2, 2
ROWS = XH * NZ
UNROLL = 4
TILE_N = 256
LOW = -1e30
EXP2_SCALE = HEAD_DIM ** (-0.5) * 1.4426950408889634
MIB = 1024 * 1024


def shift(size, by):
    return [(i, (i + by) % size) for i in range(size)]


def in_vmem(count):
    return [pl.BlockSpec(memory_space=pltpu.VMEM)] * count


def in_smem(count):
    return [pl.BlockSpec(memory_space=pltpu.SMEM)] * count


def split_kernel(q_hbm, k_hbm, v_hbm, slots_hbm, whole_ref, out_ref, sems):
    loads = [
        pltpu.make_async_copy(source, whole_ref.at[t], sems.at[t])
        for t, source in enumerate((q_hbm, k_hbm, v_hbm))
    ]
    for load in loads:
        load.start()
    for t, load in enumerate(loads):
        load.wait()
        for head in range(HEADS):
            lanes = slice(head * HEAD_DIM, (head + 1) * HEAD_DIM)
            out_ref[head, t * BLOCK : (t + 1) * BLOCK, :] = whole_ref[t, :, lanes]
    out = pltpu.make_async_copy(out_ref, slots_hbm.at[:HEADS], sems.at[3])
    out.start()
    out.wait()


def split(queries, keys, values):
    anywhere = pl.BlockSpec(memory_space=pl.ANY)
    part = (3 * BLOCK, HEAD_DIM)
    return pl.pallas_call(
        split_kernel,
        out_shape=jax.ShapeDtypeStruct((NZ,) + part, jnp.bfloat16),
        in_specs=[anywhere] * 3,
        out_specs=anywhere,
        scratch_shapes=[
            pltpu.VMEM((3,) + queries.shape, jnp.bfloat16),
            pltpu.VMEM((HEADS,) + part, jnp.bfloat16),
            pltpu.SemaphoreType.DMA((4,)),
        ],
        compiler_params=pltpu.CompilerParams(vmem_limit_bytes=56 * MIB),
    )(queries, keys, values)


def score_tiles(count, tables, q_ref, kv_ref, s_ref, top_ref):
    block_ref, slot_ref = tables

    def score(step, carry):
        tiles = []
        for u in range(UNROLL):
            e = step * UNROLL + u
            s = lax.dot_general(
                q_ref[block_ref[e]],
                kv_ref[slot_ref[e], :BLOCK, :],
                (((1,), (1,)), ((), ())),
                preferred_element_type=jnp.float32,
            )
            s = jnp.where(e < count, s, LOW)
            s_ref[e] = s
            tiles.append(s)
        for u in range(UNROLL):
            block = block_ref[step * UNROLL + u]
            top_ref[block] = jnp.maximum(top_ref[block], tiles[u])
        return carry

    lax.fori_loop(0, (count + (UNROLL - 1)) // UNROLL, score, 0)


def mix_tiles(count, tables, kv_ref, s_ref, m_ref, l_ref, a_ref):
    block_ref, slot_ref = tables

    def mix(step, carry):
        weights, products = [], []
        for u in range(UNROLL):
            e = step * UNROLL + u
            weight = jnp.exp2((s_ref[e] - m_ref[block_ref[e]]) * EXP2_SCALE)
            weights.append(weight)
            products.append(
                jnp.dot(
                    weight.astype(jnp.bfloat16),
                    kv_ref[slot_ref[e], BLOCK:, :],
                    preferred_element_type=jnp.float32,
                )
            )
        for u in range(UNROLL):
            block = block_ref[step * UNROLL + u]
            l_ref[block] = l_ref[block] + weights[u]
            a_ref[block] = a_ref[block] + products[u]
        return carry

    lax.fori_loop(0, (count + (UNROLL - 1)) // UNROLL, mix, 0)


def stats_of(m_ref, l_ref):
    lane = lax.broadcasted_iota(jnp.int32, (BLOCK, BLOCK), 1)
    stats = jnp.zeros((BLOCK, BLOCK), jnp.float32)
    for i in range(NZ):
        total = jnp.sum(l_ref[i], axis=1, keepdims=True)
        stats = jnp.where(lane == i, m_ref[i], stats)
        stats = jnp.where(lane == NZ + i, total, stats)
    return stats


def hold_parts(parts, kv_ref):
    at = 0
    for part in parts:
        kv_ref[at : at + part.shape[0]] = part[...]
        at += part.shape[0]


def attend_last(tables, query, parts, state, mine):
    slots = sum(part.shape[0] for part in parts)

    def kernel(count_ref, block_ref, slot_ref, q_ref, *refs):
        part_refs, refs = refs[: len(parts)], refs[len(parts) :]
        (m_in, l_in, a_in), refs = refs[:3], refs[3:]
        sums_ref, stats_ref, kv_ref, s_ref, top_ref, m_ref, l_ref, a_ref = refs
        tables = (block_ref, slot_ref)
        plane = lax.axis_index("xh")
        first = (plane if mine else 1 - plane) * NZ
        hold_parts(part_refs, kv_ref)
        count = count_ref[0]
        top_ref[...] = jnp.full(top_ref.shape, LOW, jnp.float32)
        score_tiles(count, tables, q_ref, kv_ref, s_ref, top_ref)
        for i in range(NZ):
            top = jnp.max(top_ref[i], axis=1, keepdims=True)
            old = m_in[first + i]
            new = jnp.maximum(old, top)
            fade = jnp.exp2((old - new) * EXP2_SCALE)
            m_ref[i] = new
            l_ref[i] = l_in[first + i] * fade
            a_ref[i] = a_in[first + i] * fade
        mix_tiles(count, tables, kv_ref, s_ref, m_ref, l_ref, a_ref)
        sums_ref[...] = a_ref[...].astype(sums_ref.dtype)
        stats = stats_of(m_ref, l_ref)
        stats_ref[...] = stats if mine else stats.T[: 2 * NZ]

    half = pltpu.VMEM((NZ, BLOCK, BLOCK), jnp.float32)
    return pl.pallas_call(
        kernel,
        out_shape=(
            jax.ShapeDtypeStruct((NZ, BLOCK, HEAD_DIM), jnp.float32 if mine else jnp.bfloat16),
            jax.ShapeDtypeStruct((BLOCK if mine else 2 * NZ, BLOCK), jnp.float32),
        ),
        in_specs=in_smem(3) + in_vmem(1 + len(parts) + 3),
        out_specs=tuple(in_vmem(2)),
        scratch_shapes=[
            pltpu.VMEM((slots, 2 * BLOCK, HEAD_DIM), jnp.bfloat16),
            pltpu.VMEM((NZ * slots, BLOCK, BLOCK), jnp.float32),
            half,
            half,
            half,
            half,
        ],
        compiler_params=pltpu.CompilerParams(vmem_limit_bytes=28 * MIB),
        cost_estimate=pl.CostEstimate(
            flops=20 * 2 * 128**3, bytes_accessed=3 * MIB, transcendentals=10 * 128 * 128
        ),
    )(*tables, query, *parts, *state)


def attend(tables, query, parts, state):
    first = state is None
    slots = sum(part.shape[0] for part in parts)
    whole = jax.ShapeDtypeStruct((ROWS, BLOCK, BLOCK), jnp.float32)

    def kernel(count_ref, block_ref, slot_ref, own_ref, other_ref, *refs):
        tables = (block_ref, slot_ref)
        plane = lax.axis_index("xh")
        part_refs, refs = refs[: len(parts)], refs[len(parts) :]
        if not first:
            (m_in, l_in, a_in), refs = refs[:3], refs[3:]
        m_ref, l_ref, a_ref, q_ref, kv_ref, s_ref, top_ref = refs
        q_ref[pl.ds(plane * NZ, NZ)] = own_ref[...]
        q_ref[pl.ds((1 - plane) * NZ, NZ)] = other_ref[...]
        hold_parts(part_refs, kv_ref)
        count = count_ref[0]
        top_ref[...] = jnp.full(top_ref.shape, LOW, jnp.float32)
        score_tiles(count, tables, q_ref, kv_ref, s_ref, top_ref)
        for block in range(ROWS):
            top = jnp.max(top_ref[block], axis=1, keepdims=True)
            if first:
                m_ref[block] = jnp.broadcast_to(top, (BLOCK, BLOCK))
                l_ref[block] = jnp.zeros((BLOCK, BLOCK), jnp.float32)
                a_ref[block] = jnp.zeros((BLOCK, HEAD_DIM), jnp.float32)
            else:
                new = jnp.maximum(m_in[block], top)
                fade = jnp.exp2((m_in[block] - new) * EXP2_SCALE)
                m_ref[block] = new
                l_ref[block] = l_in[block] * fade
                a_ref[block] = a_in[block] * fade
        mix_tiles(count, tables, kv_ref, s_ref, m_ref, l_ref, a_ref)

    return pl.pallas_call(
        kernel,
        out_shape=(whole, whole, whole),
        in_specs=in_smem(3) + in_vmem(2 + len(parts) + (0 if first else 3)),
        out_specs=tuple(in_vmem(3)),
        scratch_shapes=[
            pltpu.VMEM((ROWS, BLOCK, HEAD_DIM), jnp.bfloat16),
            pltpu.VMEM((slots, 2 * BLOCK, HEAD_DIM), jnp.bfloat16),
            pltpu.VMEM((ROWS * slots, BLOCK, BLOCK), jnp.float32),
            pltpu.VMEM((ROWS, BLOCK, BLOCK), jnp.float32),
        ],
        compiler_params=pltpu.CompilerParams(vmem_limit_bytes=28 * MIB),
        cost_estimate=pl.CostEstimate(
            flops=len(parts) * 40 * 2 * 128**3,
            bytes_accessed=6 * MIB,
            transcendentals=20 * 128 * 128,
        ),
    )(*tables, *query, *parts, *(() if first else state))


def merge_kernel(here_ref, here_stats_ref, there_ref, there_stats_ref, out_ref, rows_ref):
    rows_ref[: 2 * NZ, :] = there_stats_ref[...]
    rows_ref[2 * NZ :, :] = jnp.zeros((BLOCK - 2 * NZ, BLOCK), jnp.float32)
    here, there = here_stats_ref[...], rows_ref[...].T
    for i in range(NZ):
        m0, m1 = here[:, i : i + 1], there[:, i : i + 1]
        l0, l1 = here[:, NZ + i : NZ + i + 1], there[:, NZ + i : NZ + i + 1]
        m = jnp.maximum(m0, m1)
        f0 = jnp.exp2((m0 - m) * EXP2_SCALE)
        f1 = jnp.exp2((m1 - m) * EXP2_SCALE)
        mixed = here_ref[i] * f0 + there_ref[i].astype(jnp.float32) * f1
        out_ref[i] = (mixed / (l0 * f0 + l1 * f1)).astype(jnp.bfloat16)


def merge(here, here_stats, there, there_stats):
    return pl.pallas_call(
        merge_kernel,
        out_shape=jax.ShapeDtypeStruct(here.shape, jnp.bfloat16),
        in_specs=in_vmem(4),
        out_specs=in_vmem(1)[0],
        scratch_shapes=[pltpu.VMEM((BLOCK, BLOCK), jnp.float32)],
        compiler_params=pltpu.CompilerParams(vmem_limit_bytes=4 * MIB),
    )(here, here_stats, there, there_stats)


def project(a, b, w_own, w_other, dtype):
    deep, width = w_own.shape
    tiles = width // TILE_N

    def kernel(a_ref, b_ref, w_hbm, w2_hbm, out_ref, rows_ref, w_ref, sems):
        copies = []
        for tile in range(tiles):
            lanes = pl.ds(tile * TILE_N, TILE_N)
            for which, source in enumerate((w_hbm, w2_hbm)):
                copies.append(
                    pltpu.make_async_copy(
                        source.at[:, lanes], w_ref.at[which, tile], sems.at[which, tile]
                    )
                )
                copies[-1].start()
        for which, ref in enumerate((a_ref, b_ref)):
            for head in range(HEADS):
                at = (which * HEADS + head) * HEAD_DIM
                rows_ref[:, at : at + HEAD_DIM] = ref[head]
        for tile in range(tiles):
            copies[2 * tile].wait()
            copies[2 * tile + 1].wait()
            out = jnp.dot(rows_ref[:, :deep], w_ref[0, tile], preferred_element_type=jnp.float32)
            out = out + jnp.dot(
                rows_ref[:, deep:], w_ref[1, tile], preferred_element_type=jnp.float32
            )
            out_ref[:, tile * TILE_N : (tile + 1) * TILE_N] = out.astype(out_ref.dtype)

    anywhere = pl.BlockSpec(memory_space=pl.ANY)
    return pl.pallas_call(
        kernel,
        out_shape=jax.ShapeDtypeStruct((BLOCK, width), dtype),
        in_specs=in_vmem(2) + [anywhere] * 2,
        out_specs=in_vmem(1)[0],
        scratch_shapes=[
            pltpu.VMEM((BLOCK, 2 * deep), jnp.bfloat16),
            pltpu.VMEM((2, tiles, deep, TILE_N), jnp.bfloat16),
            pltpu.SemaphoreType.DMA((2, tiles)),
        ],
        compiler_params=pltpu.CompilerParams(vmem_limit_bytes=12 * MIB),
        cost_estimate=pl.CostEstimate(
            flops=2 * BLOCK * 2 * deep * width, bytes_accessed=4 * MIB, transcendentals=0
        ),
    )(a, b, w_own, w_other)


def add_kernel(near_ref, far_ref, out_ref):
    out_ref[...] = (near_ref[...] + far_ref[...].astype(jnp.float32)).astype(out_ref.dtype)


def add(near, far):
    return pl.pallas_call(
        add_kernel,
        out_shape=jax.ShapeDtypeStruct(near.shape, jnp.bfloat16),
        in_specs=in_vmem(2),
        out_specs=in_vmem(1)[0],
        compiler_params=pltpu.CompilerParams(vmem_limit_bytes=4 * MIB),
    )(near, far)


GROUPS = (((0,), None), ((1, 3), None), ((2,), 1), ((2,), 0))


def tiles_kernel(mask_ref, *refs):
    y, plane = lax.axis_index("y"), lax.axis_index("xh")
    for group, (columns, on) in enumerate(GROUPS):
        count_ref, block_ref, slot_ref = refs[3 * group : 3 * group + 3]
        first_block = 0 if on is None else ((plane + on) & (XH - 1)) * NZ

        def one_query_block(
            block, at, columns=columns, refs=(block_ref, slot_ref), first_block=first_block
        ):
            block_ref, slot_ref = refs
            row = (first_block + block) * NY + y
            for column, back in enumerate(columns):
                first = plane * (NZ * NY) + ((y - back + NY) & (NY - 1))
                for i in range(NZ):
                    block_ref[at] = block
                    slot_ref[at] = column * NZ + i
                    at = at + jnp.where(mask_ref[row, first + i * NY] != 0, 1, 0)
            return at

        total = lax.fori_loop(0, ROWS if on is None else NZ, one_query_block, jnp.int32(0))
        count_ref[0] = total
        for u in range(UNROLL):
            block_ref[total + u] = 0
            slot_ref[total + u] = 0


def live_tiles(frame_mask):
    out_shape = []
    for columns, on in GROUPS:
        most = (ROWS if on is None else NZ) * NZ * len(columns) + 128
        out_shape += [jax.ShapeDtypeStruct((size,), jnp.int32) for size in (1, most, most)]
    flat = pl.pallas_call(
        tiles_kernel,
        out_shape=tuple(out_shape),
        in_specs=in_smem(1),
        out_specs=tuple(in_smem(len(out_shape))),
        compiler_params=pltpu.CompilerParams(vmem_limit_bytes=4 * MIB),
        cost_estimate=pl.CostEstimate(flops=10**6, bytes_accessed=10**5, transcendentals=0),
    )(frame_mask)
    return [tuple(flat[3 * i : 3 * i + 3]) for i in range(len(GROUPS))]


def local(queries, keys, values, frame_mask, w_out):
    xl, c = lax.axis_index("xl"), lax.axis_index("c")

    width = w_out.shape[1] // (XL * NC)

    def w_columns(w, to_xl, to_c):
        return lax.dynamic_slice(w, (0, (to_xl * NC + to_c) * width), (w.shape[0], width))

    slots = split(queries, keys, values)
    slots, w_out = lax.optimization_barrier((slots, w_out))
    w_own = [w_columns(w_out, to_xl, c) for to_xl in (1 - xl, xl)]
    w_sent = [w_columns(w_out, to_xl, 1 - c) for to_xl in (1 - xl, xl)]
    w_own, w_sent, frame_mask = lax.optimization_barrier((w_own, w_sent, frame_mask))
    groups = live_tiles(frame_mask)

    slots = lax.all_to_all(slots, "z", 0, 0, tiled=True)
    slots, w_own, w_sent, groups = lax.optimization_barrier((slots, w_own, w_sent, groups))
    low, high = slots[: NZ // 2, BLOCK:], slots[NZ // 2 :, BLOCK:]
    slots, low, high = lax.optimization_barrier((slots, low, high))
    before_low = lax.ppermute(low, "y", shift(NY, 1))
    after_high = lax.ppermute(high, "y", shift(NY, -1))
    query = slots[:, :BLOCK]
    query = (query, lax.ppermute(query, "xh", shift(XH, 1)))
    before_high = lax.ppermute(high, "y", shift(NY, 1))
    after_low = lax.ppermute(low, "y", shift(NY, -1))
    state = attend(groups[0], query, [low, high], None)
    before_low, after_high, state = lax.optimization_barrier((before_low, after_high, state))
    far_low = lax.ppermute(before_low, "y", shift(NY, 1))
    far_high = lax.ppermute(after_high, "y", shift(NY, -1))
    state = attend(groups[1], query, [before_low, before_high, after_low, after_high], state)
    far_parts = [far_low, far_high]
    sent, sent_stats = attend_last(groups[2], query[1], far_parts, state, False)
    there = lax.ppermute(sent, "xh", shift(XH, 1))
    there_stats = lax.ppermute(sent_stats, "xh", shift(XH, 1))
    here, here_stats = attend_last(groups[3], query[0], far_parts, state, True)
    here, w_sent = lax.optimization_barrier((here, w_sent))
    w_here = [lax.ppermute(w, "c", shift(NC, 1)) for w in w_sent]
    heads = merge(here, here_stats, there, there_stats)
    heads = lax.all_to_all(heads, "z", 0, 0, tiled=True)[:HEADS]
    heads_core = lax.ppermute(heads, "c", shift(NC, 1))
    far = project(heads, heads_core, w_own[0], w_here[0], jnp.bfloat16)
    far = lax.ppermute(far, "xl", shift(XL, 1))
    near = project(heads, heads_core, w_own[1], w_here[1], jnp.float32)
    return add(near, far)


def solution(mesh):
    fine = Mesh(mesh.devices.reshape(XH, NZ, NY, XL, NC), ("xh", "z", "y", "xl", "c"))
    seq, head = ("xh", "z", "y"), ("xl", "c")
    in_specs = (P(seq, head), P(seq, head), P(seq, head), P(), P(head, None))
    return jax.shard_map(
        local, mesh=fine, in_specs=in_specs, out_specs=P(seq, head), check_vma=False
    )
```

```python
import jax
import jax.numpy as jnp
from jax import lax
from jax.experimental import pallas as pl
from jax.experimental.pallas import tpu as pltpu
from jax.sharding import Mesh
from jax.sharding import PartitionSpec as P

HEAD_DIM = 128
BLOCK = 128
HEADS = 5
XH, NZ, NY, XL, NC = 2, 8, 4, 2, 2
ROWS = XH * NZ
UNROLL = 4
TILE_N = 256
LOW = -1e30
EXP2_SCALE = HEAD_DIM ** (-0.5) * 1.4426950408889634
MIB = 1024 * 1024


def shift(size, by):
    return [(i, (i + by) % size) for i in range(size)]


def in_vmem(count):
    return [pl.BlockSpec(memory_space=pltpu.VMEM)] * count


def in_smem(count):
    return [pl.BlockSpec(memory_space=pltpu.SMEM)] * count


def split_kernel(q_hbm, k_hbm, v_hbm, slots_hbm, whole_ref, out_ref, sems):
    loads = [
        pltpu.make_async_copy(source, whole_ref.at[t], sems.at[t])
        for t, source in enumerate((q_hbm, k_hbm, v_hbm))
    ]
    for load in loads:
        load.start()
    for t, load in enumerate(loads):
        load.wait()
        for head in range(HEADS):
            lanes = slice(head * HEAD_DIM, (head + 1) * HEAD_DIM)
            out_ref[head, t * BLOCK : (t + 1) * BLOCK, :] = whole_ref[t, :, lanes]
    out = pltpu.make_async_copy(out_ref, slots_hbm.at[:HEADS], sems.at[3])
    out.start()
    out.wait()


def split(queries, keys, values):
    anywhere = pl.BlockSpec(memory_space=pl.ANY)
    part = (3 * BLOCK, HEAD_DIM)
    return pl.pallas_call(
        split_kernel,
        out_shape=jax.ShapeDtypeStruct((NZ,) + part, jnp.bfloat16),
        in_specs=[anywhere] * 3,
        out_specs=anywhere,
        scratch_shapes=[
            pltpu.VMEM((3,) + queries.shape, jnp.bfloat16),
            pltpu.VMEM((HEADS,) + part, jnp.bfloat16),
            pltpu.SemaphoreType.DMA((4,)),
        ],
        compiler_params=pltpu.CompilerParams(vmem_limit_bytes=56 * MIB),
    )(queries, keys, values)


def score_tiles(count, tables, q_ref, kv_ref, s_ref, top_ref):
    block_ref, slot_ref = tables

    def score(step, carry):
        tiles = []
        for u in range(UNROLL):
            e = step * UNROLL + u
            s = lax.dot_general(
                q_ref[block_ref[e]],
                kv_ref[slot_ref[e], :BLOCK, :],
                (((1,), (1,)), ((), ())),
                preferred_element_type=jnp.float32,
            )
            s = jnp.where(e < count, s, LOW)
            s_ref[e] = s
            tiles.append(s)
        for u in range(UNROLL):
            block = block_ref[step * UNROLL + u]
            top_ref[block] = jnp.maximum(top_ref[block], tiles[u])
        return carry

    lax.fori_loop(0, (count + (UNROLL - 1)) // UNROLL, score, 0)


def mix_tiles(count, tables, kv_ref, s_ref, m_ref, l_ref, a_ref):
    block_ref, slot_ref = tables

    def mix(step, carry):
        weights, products = [], []
        for u in range(UNROLL):
            e = step * UNROLL + u
            weight = jnp.exp2((s_ref[e] - m_ref[block_ref[e]]) * EXP2_SCALE)
            weights.append(weight)
            products.append(
                jnp.dot(
                    weight.astype(jnp.bfloat16),
                    kv_ref[slot_ref[e], BLOCK:, :],
                    preferred_element_type=jnp.float32,
                )
            )
        for u in range(UNROLL):
            block = block_ref[step * UNROLL + u]
            l_ref[block] = l_ref[block] + weights[u]
            a_ref[block] = a_ref[block] + products[u]
        return carry

    lax.fori_loop(0, (count + (UNROLL - 1)) // UNROLL, mix, 0)


def stats_of(m_ref, l_ref):
    lane = lax.broadcasted_iota(jnp.int32, (BLOCK, BLOCK), 1)
    stats = jnp.zeros((BLOCK, BLOCK), jnp.float32)
    for i in range(NZ):
        total = jnp.sum(l_ref[i], axis=1, keepdims=True)
        stats = jnp.where(lane == i, m_ref[i], stats)
        stats = jnp.where(lane == NZ + i, total, stats)
    return stats


def hold_parts(parts, kv_ref):
    at = 0
    for part in parts:
        kv_ref[at : at + part.shape[0]] = part[...]
        at += part.shape[0]


def attend_last(tables, query, parts, state, mine):
    slots = sum(part.shape[0] for part in parts)

    def kernel(count_ref, block_ref, slot_ref, q_ref, *refs):
        part_refs, refs = refs[: len(parts)], refs[len(parts) :]
        (m_in, l_in, a_in), refs = refs[:3], refs[3:]
        sums_ref, stats_ref, kv_ref, s_ref, top_ref, m_ref, l_ref, a_ref = refs
        tables = (block_ref, slot_ref)
        plane = lax.axis_index("xh")
        first = (plane if mine else 1 - plane) * NZ
        hold_parts(part_refs, kv_ref)
        count = count_ref[0]
        top_ref[...] = jnp.full(top_ref.shape, LOW, jnp.float32)
        score_tiles(count, tables, q_ref, kv_ref, s_ref, top_ref)
        for i in range(NZ):
            top = jnp.max(top_ref[i], axis=1, keepdims=True)
            old = m_in[first + i]
            new = jnp.maximum(old, top)
            fade = jnp.exp2((old - new) * EXP2_SCALE)
            m_ref[i] = new
            l_ref[i] = l_in[first + i] * fade
            a_ref[i] = a_in[first + i] * fade
        mix_tiles(count, tables, kv_ref, s_ref, m_ref, l_ref, a_ref)
        sums_ref[...] = a_ref[...].astype(sums_ref.dtype)
        stats = stats_of(m_ref, l_ref)
        stats_ref[...] = stats if mine else stats.T[: 2 * NZ]

    half = pltpu.VMEM((NZ, BLOCK, BLOCK), jnp.float32)
    return pl.pallas_call(
        kernel,
        out_shape=(
            jax.ShapeDtypeStruct((NZ, BLOCK, HEAD_DIM), jnp.float32 if mine else jnp.bfloat16),
            jax.ShapeDtypeStruct((BLOCK if mine else 2 * NZ, BLOCK), jnp.float32),
        ),
        in_specs=in_smem(3) + in_vmem(1 + len(parts) + 3),
        out_specs=tuple(in_vmem(2)),
        scratch_shapes=[
            pltpu.VMEM((slots, 2 * BLOCK, HEAD_DIM), jnp.bfloat16),
            pltpu.VMEM((NZ * slots, BLOCK, BLOCK), jnp.float32),
            half,
            half,
            half,
            half,
        ],
        compiler_params=pltpu.CompilerParams(vmem_limit_bytes=28 * MIB),
        cost_estimate=pl.CostEstimate(
            flops=20 * 2 * 128**3, bytes_accessed=3 * MIB, transcendentals=10 * 128 * 128
        ),
    )(*tables, query, *parts, *state)


def attend(tables, query, parts, state):
    first = state is None
    slots = sum(part.shape[0] for part in parts)
    whole = jax.ShapeDtypeStruct((ROWS, BLOCK, BLOCK), jnp.float32)

    def kernel(count_ref, block_ref, slot_ref, own_ref, other_ref, *refs):
        tables = (block_ref, slot_ref)
        plane = lax.axis_index("xh")
        part_refs, refs = refs[: len(parts)], refs[len(parts) :]
        if not first:
            (m_in, l_in, a_in), refs = refs[:3], refs[3:]
        m_ref, l_ref, a_ref, q_ref, kv_ref, s_ref, top_ref = refs
        q_ref[pl.ds(plane * NZ, NZ)] = own_ref[...]
        q_ref[pl.ds((1 - plane) * NZ, NZ)] = other_ref[...]
        hold_parts(part_refs, kv_ref)
        count = count_ref[0]
        top_ref[...] = jnp.full(top_ref.shape, LOW, jnp.float32)
        score_tiles(count, tables, q_ref, kv_ref, s_ref, top_ref)
        for block in range(ROWS):
            top = jnp.max(top_ref[block], axis=1, keepdims=True)
            if first:
                m_ref[block] = jnp.broadcast_to(top, (BLOCK, BLOCK))
                l_ref[block] = jnp.zeros((BLOCK, BLOCK), jnp.float32)
                a_ref[block] = jnp.zeros((BLOCK, HEAD_DIM), jnp.float32)
            else:
                new = jnp.maximum(m_in[block], top)
                fade = jnp.exp2((m_in[block] - new) * EXP2_SCALE)
                m_ref[block] = new
                l_ref[block] = l_in[block] * fade
                a_ref[block] = a_in[block] * fade
        mix_tiles(count, tables, kv_ref, s_ref, m_ref, l_ref, a_ref)

    return pl.pallas_call(
        kernel,
        out_shape=(whole, whole, whole),
        in_specs=in_smem(3) + in_vmem(2 + len(parts) + (0 if first else 3)),
        out_specs=tuple(in_vmem(3)),
        scratch_shapes=[
            pltpu.VMEM((ROWS, BLOCK, HEAD_DIM), jnp.bfloat16),
            pltpu.VMEM((slots, 2 * BLOCK, HEAD_DIM), jnp.bfloat16),
            pltpu.VMEM((ROWS * slots, BLOCK, BLOCK), jnp.float32),
            pltpu.VMEM((ROWS, BLOCK, BLOCK), jnp.float32),
        ],
        compiler_params=pltpu.CompilerParams(vmem_limit_bytes=28 * MIB),
        cost_estimate=pl.CostEstimate(
            flops=len(parts) * 40 * 2 * 128**3,
            bytes_accessed=6 * MIB,
            transcendentals=20 * 128 * 128,
        ),
    )(*tables, *query, *parts, *(() if first else state))


def merge_kernel(here_ref, here_stats_ref, there_ref, there_stats_ref, out_ref, rows_ref):
    rows_ref[: 2 * NZ, :] = there_stats_ref[...]
    rows_ref[2 * NZ :, :] = jnp.zeros((BLOCK - 2 * NZ, BLOCK), jnp.float32)
    here, there = here_stats_ref[...], rows_ref[...].T
    for i in range(NZ):
        m0, m1 = here[:, i : i + 1], there[:, i : i + 1]
        l0, l1 = here[:, NZ + i : NZ + i + 1], there[:, NZ + i : NZ + i + 1]
        m = jnp.maximum(m0, m1)
        f0 = jnp.exp2((m0 - m) * EXP2_SCALE)
        f1 = jnp.exp2((m1 - m) * EXP2_SCALE)
        mixed = here_ref[i] * f0 + there_ref[i].astype(jnp.float32) * f1
        out_ref[i] = (mixed / (l0 * f0 + l1 * f1)).astype(jnp.bfloat16)


def merge(here, here_stats, there, there_stats):
    return pl.pallas_call(
        merge_kernel,
        out_shape=jax.ShapeDtypeStruct(here.shape, jnp.bfloat16),
        in_specs=in_vmem(4),
        out_specs=in_vmem(1)[0],
        scratch_shapes=[pltpu.VMEM((BLOCK, BLOCK), jnp.float32)],
        compiler_params=pltpu.CompilerParams(vmem_limit_bytes=4 * MIB),
    )(here, here_stats, there, there_stats)


def project(a, b, w_own, w_other, dtype):
    deep, width = w_own.shape
    tiles = width // TILE_N

    def kernel(a_ref, b_ref, w_hbm, w2_hbm, out_ref, rows_ref, w_ref, sems):
        copies = []
        for tile in range(tiles):
            lanes = pl.ds(tile * TILE_N, TILE_N)
            for which, source in enumerate((w_hbm, w2_hbm)):
                copies.append(
                    pltpu.make_async_copy(
                        source.at[:, lanes], w_ref.at[which, tile], sems.at[which, tile]
                    )
                )
                copies[-1].start()
        for which, ref in enumerate((a_ref, b_ref)):
            for head in range(HEADS):
                at = (which * HEADS + head) * HEAD_DIM
                rows_ref[:, at : at + HEAD_DIM] = ref[head]
        for tile in range(tiles):
            copies[2 * tile].wait()
            copies[2 * tile + 1].wait()
            out = jnp.dot(rows_ref[:, :deep], w_ref[0, tile], preferred_element_type=jnp.float32)
            out = out + jnp.dot(
                rows_ref[:, deep:], w_ref[1, tile], preferred_element_type=jnp.float32
            )
            out_ref[:, tile * TILE_N : (tile + 1) * TILE_N] = out.astype(out_ref.dtype)

    anywhere = pl.BlockSpec(memory_space=pl.ANY)
    return pl.pallas_call(
        kernel,
        out_shape=jax.ShapeDtypeStruct((BLOCK, width), dtype),
        in_specs=in_vmem(2) + [anywhere] * 2,
        out_specs=in_vmem(1)[0],
        scratch_shapes=[
            pltpu.VMEM((BLOCK, 2 * deep), jnp.bfloat16),
            pltpu.VMEM((2, tiles, deep, TILE_N), jnp.bfloat16),
            pltpu.SemaphoreType.DMA((2, tiles)),
        ],
        compiler_params=pltpu.CompilerParams(vmem_limit_bytes=12 * MIB),
        cost_estimate=pl.CostEstimate(
            flops=2 * BLOCK * 2 * deep * width, bytes_accessed=4 * MIB, transcendentals=0
        ),
    )(a, b, w_own, w_other)


def add_kernel(near_ref, far_ref, out_ref):
    out_ref[...] = (near_ref[...] + far_ref[...].astype(jnp.float32)).astype(out_ref.dtype)


def add(near, far):
    return pl.pallas_call(
        add_kernel,
        out_shape=jax.ShapeDtypeStruct(near.shape, jnp.bfloat16),
        in_specs=in_vmem(2),
        out_specs=in_vmem(1)[0],
        compiler_params=pltpu.CompilerParams(vmem_limit_bytes=4 * MIB),
    )(near, far)


GROUPS = (((0,), None), ((1, 3), None), ((2,), 1), ((2,), 0))


def tiles_kernel(mask_ref, *refs):
    y, plane = lax.axis_index("y"), lax.axis_index("xh")
    for group, (columns, on) in enumerate(GROUPS):
        count_ref, block_ref, slot_ref = refs[3 * group : 3 * group + 3]
        first_block = 0 if on is None else ((plane + on) & (XH - 1)) * NZ

        def one_query_block(
            block, at, columns=columns, refs=(block_ref, slot_ref), first_block=first_block
        ):
            block_ref, slot_ref = refs
            row = (first_block + block) * NY + y
            for column, back in enumerate(columns):
                first = plane * (NZ * NY) + ((y - back + NY) & (NY - 1))
                for i in range(NZ):
                    block_ref[at] = block
                    slot_ref[at] = column * NZ + i
                    at = at + jnp.where(mask_ref[row, first + i * NY] != 0, 1, 0)
            return at

        total = lax.fori_loop(0, ROWS if on is None else NZ, one_query_block, jnp.int32(0))
        count_ref[0] = total
        for u in range(UNROLL):
            block_ref[total + u] = 0
            slot_ref[total + u] = 0


def live_tiles(frame_mask):
    out_shape = []
    for columns, on in GROUPS:
        most = (ROWS if on is None else NZ) * NZ * len(columns) + 128
        out_shape += [jax.ShapeDtypeStruct((size,), jnp.int32) for size in (1, most, most)]
    flat = pl.pallas_call(
        tiles_kernel,
        out_shape=tuple(out_shape),
        in_specs=in_smem(1),
        out_specs=tuple(in_smem(len(out_shape))),
        compiler_params=pltpu.CompilerParams(vmem_limit_bytes=4 * MIB),
        cost_estimate=pl.CostEstimate(flops=10**6, bytes_accessed=10**5, transcendentals=0),
    )(frame_mask)
    return [tuple(flat[3 * i : 3 * i + 3]) for i in range(len(GROUPS))]


def local(queries, keys, values, frame_mask, w_out):
    xl, c = lax.axis_index("xl"), lax.axis_index("c")

    width = w_out.shape[1] // (XL * NC)

    def w_columns(w, to_xl, to_c):
        return lax.dynamic_slice(w, (0, (to_xl * NC + to_c) * width), (w.shape[0], width))

    slots = split(queries, keys, values)
    slots, w_out = lax.optimization_barrier((slots, w_out))
    w_own = [w_columns(w_out, to_xl, c) for to_xl in (1 - xl, xl)]
    w_sent = [w_columns(w_out, to_xl, 1 - c) for to_xl in (1 - xl, xl)]
    w_own, w_sent, frame_mask = lax.optimization_barrier((w_own, w_sent, frame_mask))
    groups = live_tiles(frame_mask)

    slots = lax.all_to_all(slots, "z", 0, 0, tiled=True)
    slots, w_own, w_sent, groups = lax.optimization_barrier((slots, w_own, w_sent, groups))
    low, high = slots[: NZ // 2, BLOCK:], slots[NZ // 2 :, BLOCK:]
    slots, low, high = lax.optimization_barrier((slots, low, high))
    before_low = lax.ppermute(low, "y", shift(NY, 1))
    after_high = lax.ppermute(high, "y", shift(NY, -1))
    query = slots[:, :BLOCK]
    query = (query, lax.ppermute(query, "xh", shift(XH, 1)))
    before_high = lax.ppermute(high, "y", shift(NY, 1))
    after_low = lax.ppermute(low, "y", shift(NY, -1))
    state = attend(groups[0], query, [low, high], None)
    before_low, after_high, state = lax.optimization_barrier((before_low, after_high, state))
    far_low = lax.ppermute(before_low, "y", shift(NY, 1))
    far_high = lax.ppermute(after_high, "y", shift(NY, -1))
    state = attend(groups[1], query, [before_low, before_high, after_low, after_high], state)
    far_parts = [far_low, far_high]
    sent, sent_stats = attend_last(groups[2], query[1], far_parts, state, False)
    sent, sent_stats, state = lax.optimization_barrier((sent, sent_stats, state))
    there = lax.ppermute(sent, "xh", shift(XH, 1))
    there_stats = lax.ppermute(sent_stats, "xh", shift(XH, 1))
    here, here_stats = attend_last(groups[3], query[0], far_parts, state, True)
    heads = merge(here, here_stats, there, there_stats)
    heads, w_sent = lax.optimization_barrier((heads, w_sent))
    w_here = [lax.ppermute(w, "c", shift(NC, 1)) for w in w_sent]
    heads = lax.all_to_all(heads, "z", 0, 0, tiled=True)[:HEADS]
    heads_core = lax.ppermute(heads, "c", shift(NC, 1))
    far = project(heads, heads_core, w_own[0], w_here[0], jnp.bfloat16)
    far = lax.ppermute(far, "xl", shift(XL, 1))
    near = project(heads, heads_core, w_own[1], w_here[1], jnp.float32)
    return add(near, far)


def solution(mesh):
    fine = Mesh(mesh.devices.reshape(XH, NZ, NY, XL, NC), ("xh", "z", "y", "xl", "c"))
    seq, head = ("xh", "z", "y"), ("xl", "c")
    in_specs = (P(seq, head), P(seq, head), P(seq, head), P(), P(head, None))
    return jax.shard_map(
        local, mesh=fine, in_specs=in_specs, out_specs=P(seq, head), check_vma=False
    )
```

```python
import jax
import jax.numpy as jnp
from jax import lax
from jax.experimental import pallas as pl
from jax.experimental.pallas import tpu as pltpu
from jax.sharding import Mesh
from jax.sharding import PartitionSpec as P

HEAD_DIM = 128
BLOCK = 128
HEADS = 5
XH, NZ, NY, XL, NC = 2, 8, 4, 2, 2
ROWS = XH * NZ
UNROLL = 4
TILE_N = 256
LOW = -1e30
EXP2_SCALE = HEAD_DIM ** (-0.5) * 1.4426950408889634
MIB = 1024 * 1024


def shift(size, by):
    return [(i, (i + by) % size) for i in range(size)]


def in_vmem(count):
    return [pl.BlockSpec(memory_space=pltpu.VMEM)] * count


def in_smem(count):
    return [pl.BlockSpec(memory_space=pltpu.SMEM)] * count


def split_kernel(q_hbm, k_hbm, v_hbm, slots_hbm, whole_ref, out_ref, sems):
    loads = [
        pltpu.make_async_copy(source, whole_ref.at[t], sems.at[t])
        for t, source in enumerate((q_hbm, k_hbm, v_hbm))
    ]
    for load in loads:
        load.start()
    for t, load in enumerate(loads):
        load.wait()
        for head in range(HEADS):
            lanes = slice(head * HEAD_DIM, (head + 1) * HEAD_DIM)
            out_ref[head, t * BLOCK : (t + 1) * BLOCK, :] = whole_ref[t, :, lanes]
    out = pltpu.make_async_copy(out_ref, slots_hbm.at[:HEADS], sems.at[3])
    out.start()
    out.wait()


def split(queries, keys, values):
    anywhere = pl.BlockSpec(memory_space=pl.ANY)
    part = (3 * BLOCK, HEAD_DIM)
    return pl.pallas_call(
        split_kernel,
        out_shape=jax.ShapeDtypeStruct((NZ,) + part, jnp.bfloat16),
        in_specs=[anywhere] * 3,
        out_specs=anywhere,
        scratch_shapes=[
            pltpu.VMEM((3,) + queries.shape, jnp.bfloat16),
            pltpu.VMEM((HEADS,) + part, jnp.bfloat16),
            pltpu.SemaphoreType.DMA((4,)),
        ],
        compiler_params=pltpu.CompilerParams(vmem_limit_bytes=56 * MIB),
    )(queries, keys, values)


def score_tiles(count, tables, q_ref, kv_ref, s_ref, top_ref):
    block_ref, slot_ref = tables

    def score(step, carry):
        tiles = []
        for u in range(UNROLL):
            e = step * UNROLL + u
            s = lax.dot_general(
                q_ref[block_ref[e]],
                kv_ref[slot_ref[e], :BLOCK, :],
                (((1,), (1,)), ((), ())),
                preferred_element_type=jnp.float32,
            )
            s = jnp.where(e < count, s, LOW)
            s_ref[e] = s
            tiles.append(s)
        for u in range(UNROLL):
            block = block_ref[step * UNROLL + u]
            top_ref[block] = jnp.maximum(top_ref[block], tiles[u])
        return carry

    lax.fori_loop(0, (count + (UNROLL - 1)) // UNROLL, score, 0)


def mix_tiles(count, tables, kv_ref, s_ref, m_ref, l_ref, a_ref):
    block_ref, slot_ref = tables

    def mix(step, carry):
        weights, products = [], []
        for u in range(UNROLL):
            e = step * UNROLL + u
            weight = jnp.exp2((s_ref[e] - m_ref[block_ref[e]]) * EXP2_SCALE)
            weights.append(weight)
            products.append(
                jnp.dot(
                    weight.astype(jnp.bfloat16),
                    kv_ref[slot_ref[e], BLOCK:, :],
                    preferred_element_type=jnp.float32,
                )
            )
        for u in range(UNROLL):
            block = block_ref[step * UNROLL + u]
            l_ref[block] = l_ref[block] + weights[u]
            a_ref[block] = a_ref[block] + products[u]
        return carry

    lax.fori_loop(0, (count + (UNROLL - 1)) // UNROLL, mix, 0)


def stats_of(m_ref, l_ref):
    lane = lax.broadcasted_iota(jnp.int32, (BLOCK, BLOCK), 1)
    stats = jnp.zeros((BLOCK, BLOCK), jnp.float32)
    for i in range(NZ):
        total = jnp.sum(l_ref[i], axis=1, keepdims=True)
        stats = jnp.where(lane == i, m_ref[i], stats)
        stats = jnp.where(lane == NZ + i, total, stats)
    return stats


def hold_parts(parts, kv_ref):
    at = 0
    for part in parts:
        kv_ref[at : at + part.shape[0]] = part[...]
        at += part.shape[0]


def attend_last(tables, query, parts, state, mine):
    slots = sum(part.shape[0] for part in parts)

    def kernel(count_ref, block_ref, slot_ref, q_ref, *refs):
        part_refs, refs = refs[: len(parts)], refs[len(parts) :]
        (m_in, l_in, a_in), refs = refs[:3], refs[3:]
        sums_ref, stats_ref, kv_ref, s_ref, top_ref, m_ref, l_ref, a_ref = refs
        tables = (block_ref, slot_ref)
        plane = lax.axis_index("xh")
        first = (plane if mine else 1 - plane) * NZ
        hold_parts(part_refs, kv_ref)
        count = count_ref[0]
        top_ref[...] = jnp.full(top_ref.shape, LOW, jnp.float32)
        score_tiles(count, tables, q_ref, kv_ref, s_ref, top_ref)
        for i in range(NZ):
            top = jnp.max(top_ref[i], axis=1, keepdims=True)
            old = m_in[first + i]
            new = jnp.maximum(old, top)
            fade = jnp.exp2((old - new) * EXP2_SCALE)
            m_ref[i] = new
            l_ref[i] = l_in[first + i] * fade
            a_ref[i] = a_in[first + i] * fade
        mix_tiles(count, tables, kv_ref, s_ref, m_ref, l_ref, a_ref)
        sums_ref[...] = a_ref[...].astype(sums_ref.dtype)
        stats = stats_of(m_ref, l_ref)
        stats_ref[...] = stats if mine else stats.T[: 2 * NZ]

    half = pltpu.VMEM((NZ, BLOCK, BLOCK), jnp.float32)
    return pl.pallas_call(
        kernel,
        out_shape=(
            jax.ShapeDtypeStruct((NZ, BLOCK, HEAD_DIM), jnp.float32 if mine else jnp.bfloat16),
            jax.ShapeDtypeStruct((BLOCK if mine else 2 * NZ, BLOCK), jnp.float32),
        ),
        in_specs=in_smem(3) + in_vmem(1 + len(parts) + 3),
        out_specs=tuple(in_vmem(2)),
        scratch_shapes=[
            pltpu.VMEM((slots, 2 * BLOCK, HEAD_DIM), jnp.bfloat16),
            pltpu.VMEM((NZ * slots, BLOCK, BLOCK), jnp.float32),
            half,
            half,
            half,
            half,
        ],
        compiler_params=pltpu.CompilerParams(vmem_limit_bytes=28 * MIB),
        cost_estimate=pl.CostEstimate(
            flops=20 * 2 * 128**3, bytes_accessed=3 * MIB, transcendentals=10 * 128 * 128
        ),
    )(*tables, query, *parts, *state)


def attend(tables, query, parts, state):
    first = state is None
    slots = sum(part.shape[0] for part in parts)
    whole = jax.ShapeDtypeStruct((ROWS, BLOCK, BLOCK), jnp.float32)

    def kernel(count_ref, block_ref, slot_ref, own_ref, other_ref, *refs):
        tables = (block_ref, slot_ref)
        plane = lax.axis_index("xh")
        part_refs, refs = refs[: len(parts)], refs[len(parts) :]
        if not first:
            (m_in, l_in, a_in), refs = refs[:3], refs[3:]
        m_ref, l_ref, a_ref, q_ref, kv_ref, s_ref, top_ref = refs
        q_ref[pl.ds(plane * NZ, NZ)] = own_ref[...]
        q_ref[pl.ds((1 - plane) * NZ, NZ)] = other_ref[...]
        hold_parts(part_refs, kv_ref)
        count = count_ref[0]
        top_ref[...] = jnp.full(top_ref.shape, LOW, jnp.float32)
        score_tiles(count, tables, q_ref, kv_ref, s_ref, top_ref)
        for block in range(ROWS):
            top = jnp.max(top_ref[block], axis=1, keepdims=True)
            if first:
                m_ref[block] = jnp.broadcast_to(top, (BLOCK, BLOCK))
                l_ref[block] = jnp.zeros((BLOCK, BLOCK), jnp.float32)
                a_ref[block] = jnp.zeros((BLOCK, HEAD_DIM), jnp.float32)
            else:
                new = jnp.maximum(m_in[block], top)
                fade = jnp.exp2((m_in[block] - new) * EXP2_SCALE)
                m_ref[block] = new
                l_ref[block] = l_in[block] * fade
                a_ref[block] = a_in[block] * fade
        mix_tiles(count, tables, kv_ref, s_ref, m_ref, l_ref, a_ref)

    return pl.pallas_call(
        kernel,
        out_shape=(whole, whole, whole),
        in_specs=in_smem(3) + in_vmem(2 + len(parts) + (0 if first else 3)),
        out_specs=tuple(in_vmem(3)),
        scratch_shapes=[
            pltpu.VMEM((ROWS, BLOCK, HEAD_DIM), jnp.bfloat16),
            pltpu.VMEM((slots, 2 * BLOCK, HEAD_DIM), jnp.bfloat16),
            pltpu.VMEM((ROWS * slots, BLOCK, BLOCK), jnp.float32),
            pltpu.VMEM((ROWS, BLOCK, BLOCK), jnp.float32),
        ],
        compiler_params=pltpu.CompilerParams(vmem_limit_bytes=28 * MIB),
        cost_estimate=pl.CostEstimate(
            flops=len(parts) * 40 * 2 * 128**3,
            bytes_accessed=6 * MIB,
            transcendentals=20 * 128 * 128,
        ),
    )(*tables, *query, *parts, *(() if first else state))


def merge_kernel(here_ref, here_stats_ref, there_ref, there_stats_ref, out_ref, rows_ref):
    rows_ref[: 2 * NZ, :] = there_stats_ref[...]
    rows_ref[2 * NZ :, :] = jnp.zeros((BLOCK - 2 * NZ, BLOCK), jnp.float32)
    here, there = here_stats_ref[...], rows_ref[...].T
    for i in range(NZ):
        m0, m1 = here[:, i : i + 1], there[:, i : i + 1]
        l0, l1 = here[:, NZ + i : NZ + i + 1], there[:, NZ + i : NZ + i + 1]
        m = jnp.maximum(m0, m1)
        f0 = jnp.exp2((m0 - m) * EXP2_SCALE)
        f1 = jnp.exp2((m1 - m) * EXP2_SCALE)
        mixed = here_ref[i] * f0 + there_ref[i].astype(jnp.float32) * f1
        out_ref[i] = (mixed / (l0 * f0 + l1 * f1)).astype(jnp.bfloat16)


def merge(here, here_stats, there, there_stats):
    return pl.pallas_call(
        merge_kernel,
        out_shape=jax.ShapeDtypeStruct(here.shape, jnp.bfloat16),
        in_specs=in_vmem(4),
        out_specs=in_vmem(1)[0],
        scratch_shapes=[pltpu.VMEM((BLOCK, BLOCK), jnp.float32)],
        compiler_params=pltpu.CompilerParams(vmem_limit_bytes=4 * MIB),
    )(here, here_stats, there, there_stats)


def project(a, b, w_own, w_other, first, width, dtype):
    deep = w_own.shape[0]
    tiles = width // TILE_N

    def kernel(a_ref, b_ref, w_hbm, w2_hbm, out_ref, rows_ref, w_ref, sems):
        copies = []
        for tile in range(tiles):
            lanes = pl.ds(first + tile * TILE_N, TILE_N)
            for which, source in enumerate((w_hbm, w2_hbm)):
                copies.append(
                    pltpu.make_async_copy(
                        source.at[:, lanes], w_ref.at[which, tile], sems.at[which, tile]
                    )
                )
                copies[-1].start()
        for which, ref in enumerate((a_ref, b_ref)):
            for head in range(HEADS):
                at = (which * HEADS + head) * HEAD_DIM
                rows_ref[:, at : at + HEAD_DIM] = ref[head]
        for tile in range(tiles):
            copies[2 * tile].wait()
            copies[2 * tile + 1].wait()
            out = jnp.dot(rows_ref[:, :deep], w_ref[0, tile], preferred_element_type=jnp.float32)
            out = out + jnp.dot(
                rows_ref[:, deep:], w_ref[1, tile], preferred_element_type=jnp.float32
            )
            out_ref[:, tile * TILE_N : (tile + 1) * TILE_N] = out.astype(out_ref.dtype)

    anywhere = pl.BlockSpec(memory_space=pl.ANY)
    return pl.pallas_call(
        kernel,
        out_shape=jax.ShapeDtypeStruct((BLOCK, width), dtype),
        in_specs=in_vmem(2) + [anywhere] * 2,
        out_specs=in_vmem(1)[0],
        scratch_shapes=[
            pltpu.VMEM((BLOCK, 2 * deep), jnp.bfloat16),
            pltpu.VMEM((2, tiles, deep, TILE_N), jnp.bfloat16),
            pltpu.SemaphoreType.DMA((2, tiles)),
        ],
        compiler_params=pltpu.CompilerParams(vmem_limit_bytes=12 * MIB),
        cost_estimate=pl.CostEstimate(
            flops=2 * BLOCK * 2 * deep * width, bytes_accessed=4 * MIB, transcendentals=0
        ),
    )(a, b, w_own, w_other)


def add_kernel(near_ref, *refs):
    out_ref = refs[-1]
    at = 0
    for far_ref in refs[:-1]:
        lanes = slice(at, at + far_ref.shape[1])
        out = near_ref[:, lanes] + far_ref[...].astype(jnp.float32)
        out_ref[:, lanes] = out.astype(out_ref.dtype)
        at += far_ref.shape[1]


def add(near, far):
    return pl.pallas_call(
        add_kernel,
        out_shape=jax.ShapeDtypeStruct(near.shape, jnp.bfloat16),
        in_specs=in_vmem(1 + len(far)),
        out_specs=in_vmem(1)[0],
        compiler_params=pltpu.CompilerParams(vmem_limit_bytes=4 * MIB),
    )(near, *far)


GROUPS = (((0,), None), ((1, 3), None), ((2,), 1), ((2,), 0))


def tiles_kernel(mask_ref, *refs):
    y, plane = lax.axis_index("y"), lax.axis_index("xh")
    for group, (columns, on) in enumerate(GROUPS):
        count_ref, block_ref, slot_ref = refs[3 * group : 3 * group + 3]
        first_block = 0 if on is None else ((plane + on) & (XH - 1)) * NZ

        def one_query_block(
            block, at, columns=columns, refs=(block_ref, slot_ref), first_block=first_block
        ):
            block_ref, slot_ref = refs
            row = (first_block + block) * NY + y
            for column, back in enumerate(columns):
                first = plane * (NZ * NY) + ((y - back + NY) & (NY - 1))
                for i in range(NZ):
                    block_ref[at] = block
                    slot_ref[at] = column * NZ + i
                    at = at + jnp.where(mask_ref[row, first + i * NY] != 0, 1, 0)
            return at

        total = lax.fori_loop(0, ROWS if on is None else NZ, one_query_block, jnp.int32(0))
        count_ref[0] = total
        for u in range(UNROLL):
            block_ref[total + u] = 0
            slot_ref[total + u] = 0


def live_tiles(frame_mask):
    out_shape = []
    for columns, on in GROUPS:
        most = (ROWS if on is None else NZ) * NZ * len(columns) + 128
        out_shape += [jax.ShapeDtypeStruct((size,), jnp.int32) for size in (1, most, most)]
    flat = pl.pallas_call(
        tiles_kernel,
        out_shape=tuple(out_shape),
        in_specs=in_smem(1),
        out_specs=tuple(in_smem(len(out_shape))),
        compiler_params=pltpu.CompilerParams(vmem_limit_bytes=4 * MIB),
        cost_estimate=pl.CostEstimate(flops=10**6, bytes_accessed=10**5, transcendentals=0),
    )(frame_mask)
    return [tuple(flat[3 * i : 3 * i + 3]) for i in range(len(GROUPS))]


def local(queries, keys, values, frame_mask, w_out):
    xl, c = lax.axis_index("xl"), lax.axis_index("c")

    width = w_out.shape[1] // (XL * NC)

    def w_columns(w, to_xl, to_c):
        return lax.dynamic_slice(w, (0, (to_xl * NC + to_c) * width), (w.shape[0], width))

    slots = split(queries, keys, values)
    slots, w_out = lax.optimization_barrier((slots, w_out))
    w_own = [w_columns(w_out, to_xl, c) for to_xl in (1 - xl, xl)]
    w_sent = [w_columns(w_out, to_xl, 1 - c) for to_xl in (1 - xl, xl)]
    w_own, w_sent, frame_mask = lax.optimization_barrier((w_own, w_sent, frame_mask))
    w_here = [lax.ppermute(w, "c", shift(NC, 1)) for w in w_sent]
    groups = live_tiles(frame_mask)

    slots = lax.all_to_all(slots, "z", 0, 0, tiled=True)
    slots, w_own, groups = lax.optimization_barrier((slots, w_own, groups))
    low, high = slots[: NZ // 2, BLOCK:], slots[NZ // 2 :, BLOCK:]
    slots, low, high = lax.optimization_barrier((slots, low, high))
    before_low = lax.ppermute(low, "y", shift(NY, 1))
    after_high = lax.ppermute(high, "y", shift(NY, -1))
    query = slots[:, :BLOCK]
    query = (query, lax.ppermute(query, "xh", shift(XH, 1)))
    before_high = lax.ppermute(high, "y", shift(NY, 1))
    after_low = lax.ppermute(low, "y", shift(NY, -1))
    state = attend(groups[0], query, [low, high], None)
    before_low, after_high, state = lax.optimization_barrier((before_low, after_high, state))
    far_low = lax.ppermute(before_low, "y", shift(NY, 1))
    far_high = lax.ppermute(after_high, "y", shift(NY, -1))
    state = attend(groups[1], query, [before_low, before_high, after_low, after_high], state)
    far_parts = [far_low, far_high]
    sent, sent_stats = attend_last(groups[2], query[1], far_parts, state, False)
    sent, sent_stats, state = lax.optimization_barrier((sent, sent_stats, state))
    there = lax.ppermute(sent, "xh", shift(XH, 1))
    there_stats = lax.ppermute(sent_stats, "xh", shift(XH, 1))
    here, here_stats = attend_last(groups[3], query[0], far_parts, state, True)
    there, w_here = lax.optimization_barrier((there, w_here))
    heads = merge(here, here_stats, there, there_stats)
    heads = lax.all_to_all(heads, "z", 0, 0, tiled=True)[:HEADS]
    heads_core = lax.ppermute(heads, "c", shift(NC, 1))
    early = width // TILE_N // 2 * TILE_N
    far = [
        lax.ppermute(
            project(heads, heads_core, w_own[0], w_here[0], first, columns, jnp.bfloat16),
            "xl",
            shift(XL, 1),
        )
        for first, columns in ((0, early), (early, width - early))
    ]
    near = project(heads, heads_core, w_own[1], w_here[1], 0, width, jnp.float32)
    return add(near, far)


def solution(mesh):
    fine = Mesh(mesh.devices.reshape(XH, NZ, NY, XL, NC), ("xh", "z", "y", "xl", "c"))
    seq, head = ("xh", "z", "y"), ("xl", "c")
    in_specs = (P(seq, head), P(seq, head), P(seq, head), P(), P(head, None))
    return jax.shard_map(
        local, mesh=fine, in_specs=in_specs, out_specs=P(seq, head), check_vma=False
    )
```

```python
import jax
import jax.numpy as jnp
from jax import lax
from jax.experimental import pallas as pl
from jax.experimental.pallas import tpu as pltpu
from jax.sharding import Mesh
from jax.sharding import PartitionSpec as P

HEAD_DIM = 128
BLOCK = 128
HEADS = 5
XH, NZ, NY, XL, NC = 2, 8, 4, 2, 2
ROWS = XH * NZ
UNROLL = 4
TILE_N = 256
LOW = -1e30
EXP2_SCALE = HEAD_DIM ** (-0.5) * 1.4426950408889634
MIB = 1024 * 1024


def shift(size, by):
    return [(i, (i + by) % size) for i in range(size)]


def in_vmem(count):
    return [pl.BlockSpec(memory_space=pltpu.VMEM)] * count


def in_smem(count):
    return [pl.BlockSpec(memory_space=pltpu.SMEM)] * count


def split_kernel(q_hbm, k_hbm, v_hbm, slots_hbm, whole_ref, out_ref, sems):
    loads = [
        pltpu.make_async_copy(source, whole_ref.at[t], sems.at[t])
        for t, source in enumerate((q_hbm, k_hbm, v_hbm))
    ]
    for load in loads:
        load.start()
    for t, load in enumerate(loads):
        load.wait()
        for head in range(HEADS):
            lanes = slice(head * HEAD_DIM, (head + 1) * HEAD_DIM)
            out_ref[head, t * BLOCK : (t + 1) * BLOCK, :] = whole_ref[t, :, lanes]
    out = pltpu.make_async_copy(out_ref, slots_hbm.at[:HEADS], sems.at[3])
    out.start()
    out.wait()


def split(queries, keys, values):
    anywhere = pl.BlockSpec(memory_space=pl.ANY)
    part = (3 * BLOCK, HEAD_DIM)
    return pl.pallas_call(
        split_kernel,
        out_shape=jax.ShapeDtypeStruct((NZ,) + part, jnp.bfloat16),
        in_specs=[anywhere] * 3,
        out_specs=anywhere,
        scratch_shapes=[
            pltpu.VMEM((3,) + queries.shape, jnp.bfloat16),
            pltpu.VMEM((HEADS,) + part, jnp.bfloat16),
            pltpu.SemaphoreType.DMA((4,)),
        ],
        compiler_params=pltpu.CompilerParams(vmem_limit_bytes=56 * MIB),
    )(queries, keys, values)


def score_tiles(count, tables, q_ref, kv_ref, s_ref, top_ref):
    block_ref, slot_ref = tables

    def score(step, carry):
        tiles = []
        for u in range(UNROLL):
            e = step * UNROLL + u
            s = lax.dot_general(
                q_ref[block_ref[e]],
                kv_ref[slot_ref[e], :BLOCK, :],
                (((1,), (1,)), ((), ())),
                preferred_element_type=jnp.float32,
            )
            s = jnp.where(e < count, s, LOW)
            s_ref[e] = s
            tiles.append(s)
        for u in range(UNROLL):
            block = block_ref[step * UNROLL + u]
            top_ref[block] = jnp.maximum(top_ref[block], tiles[u])
        return carry

    lax.fori_loop(0, (count + (UNROLL - 1)) // UNROLL, score, 0)


def mix_tiles(count, tables, kv_ref, s_ref, m_ref, l_ref, a_ref):
    block_ref, slot_ref = tables

    def mix(step, carry):
        weights, products = [], []
        for u in range(UNROLL):
            e = step * UNROLL + u
            weight = jnp.exp2((s_ref[e] - m_ref[block_ref[e]]) * EXP2_SCALE)
            weights.append(weight)
            products.append(
                jnp.dot(
                    weight.astype(jnp.bfloat16),
                    kv_ref[slot_ref[e], BLOCK:, :],
                    preferred_element_type=jnp.float32,
                )
            )
        for u in range(UNROLL):
            block = block_ref[step * UNROLL + u]
            l_ref[block] = l_ref[block] + weights[u]
            a_ref[block] = a_ref[block] + products[u]
        return carry

    lax.fori_loop(0, (count + (UNROLL - 1)) // UNROLL, mix, 0)


def stats_of(m_ref, l_ref):
    lane = lax.broadcasted_iota(jnp.int32, (BLOCK, BLOCK), 1)
    stats = jnp.zeros((BLOCK, BLOCK), jnp.float32)
    for i in range(NZ):
        total = jnp.sum(l_ref[i], axis=1, keepdims=True)
        stats = jnp.where(lane == i, m_ref[i], stats)
        stats = jnp.where(lane == NZ + i, total, stats)
    return stats


def hold_parts(parts, kv_ref):
    at = 0
    for part in parts:
        kv_ref[at : at + part.shape[0]] = part[...]
        at += part.shape[0]


def attend_last(tables, query, parts, state, mine):
    slots = sum(part.shape[0] for part in parts)

    def kernel(count_ref, block_ref, slot_ref, q_ref, *refs):
        part_refs, refs = refs[: len(parts)], refs[len(parts) :]
        (m_in, l_in, a_in), refs = refs[:3], refs[3:]
        sums_ref, stats_ref, kv_ref, s_ref, top_ref, m_ref, l_ref, a_ref = refs
        tables = (block_ref, slot_ref)
        plane = lax.axis_index("xh")
        first = (plane if mine else 1 - plane) * NZ
        hold_parts(part_refs, kv_ref)
        count = count_ref[0]
        top_ref[...] = jnp.full(top_ref.shape, LOW, jnp.float32)
        score_tiles(count, tables, q_ref, kv_ref, s_ref, top_ref)
        for i in range(NZ):
            top = jnp.max(top_ref[i], axis=1, keepdims=True)
            old = m_in[first + i]
            new = jnp.maximum(old, top)
            fade = jnp.exp2((old - new) * EXP2_SCALE)
            m_ref[i] = new
            l_ref[i] = l_in[first + i] * fade
            a_ref[i] = a_in[first + i] * fade
        mix_tiles(count, tables, kv_ref, s_ref, m_ref, l_ref, a_ref)
        sums_ref[...] = a_ref[...].astype(sums_ref.dtype)
        stats = stats_of(m_ref, l_ref)
        stats_ref[...] = stats if mine else stats.T[: 2 * NZ]

    half = pltpu.VMEM((NZ, BLOCK, BLOCK), jnp.float32)
    return pl.pallas_call(
        kernel,
        out_shape=(
            jax.ShapeDtypeStruct((NZ, BLOCK, HEAD_DIM), jnp.float32 if mine else jnp.bfloat16),
            jax.ShapeDtypeStruct((BLOCK if mine else 2 * NZ, BLOCK), jnp.float32),
        ),
        in_specs=in_smem(3) + in_vmem(1 + len(parts) + 3),
        out_specs=tuple(in_vmem(2)),
        scratch_shapes=[
            pltpu.VMEM((slots, 2 * BLOCK, HEAD_DIM), jnp.bfloat16),
            pltpu.VMEM((NZ * slots, BLOCK, BLOCK), jnp.float32),
            half,
            half,
            half,
            half,
        ],
        compiler_params=pltpu.CompilerParams(vmem_limit_bytes=28 * MIB),
        cost_estimate=pl.CostEstimate(
            flops=20 * 2 * 128**3, bytes_accessed=3 * MIB, transcendentals=10 * 128 * 128
        ),
    )(*tables, query, *parts, *state)


def attend(tables, query, parts, state):
    first = state is None
    slots = sum(part.shape[0] for part in parts)
    whole = jax.ShapeDtypeStruct((ROWS, BLOCK, BLOCK), jnp.float32)

    def kernel(count_ref, block_ref, slot_ref, own_ref, other_ref, *refs):
        tables = (block_ref, slot_ref)
        plane = lax.axis_index("xh")
        part_refs, refs = refs[: len(parts)], refs[len(parts) :]
        if not first:
            (m_in, l_in, a_in), refs = refs[:3], refs[3:]
        m_ref, l_ref, a_ref, q_ref, kv_ref, s_ref, top_ref = refs
        q_ref[pl.ds(plane * NZ, NZ)] = own_ref[...]
        q_ref[pl.ds((1 - plane) * NZ, NZ)] = other_ref[...]
        hold_parts(part_refs, kv_ref)
        count = count_ref[0]
        top_ref[...] = jnp.full(top_ref.shape, LOW, jnp.float32)
        score_tiles(count, tables, q_ref, kv_ref, s_ref, top_ref)
        for block in range(ROWS):
            top = jnp.max(top_ref[block], axis=1, keepdims=True)
            if first:
                m_ref[block] = jnp.broadcast_to(top, (BLOCK, BLOCK))
                l_ref[block] = jnp.zeros((BLOCK, BLOCK), jnp.float32)
                a_ref[block] = jnp.zeros((BLOCK, HEAD_DIM), jnp.float32)
            else:
                new = jnp.maximum(m_in[block], top)
                fade = jnp.exp2((m_in[block] - new) * EXP2_SCALE)
                m_ref[block] = new
                l_ref[block] = l_in[block] * fade
                a_ref[block] = a_in[block] * fade
        mix_tiles(count, tables, kv_ref, s_ref, m_ref, l_ref, a_ref)

    return pl.pallas_call(
        kernel,
        out_shape=(whole, whole, whole),
        in_specs=in_smem(3) + in_vmem(2 + len(parts) + (0 if first else 3)),
        out_specs=tuple(in_vmem(3)),
        scratch_shapes=[
            pltpu.VMEM((ROWS, BLOCK, HEAD_DIM), jnp.bfloat16),
            pltpu.VMEM((slots, 2 * BLOCK, HEAD_DIM), jnp.bfloat16),
            pltpu.VMEM((ROWS * slots, BLOCK, BLOCK), jnp.float32),
            pltpu.VMEM((ROWS, BLOCK, BLOCK), jnp.float32),
        ],
        compiler_params=pltpu.CompilerParams(vmem_limit_bytes=28 * MIB),
        cost_estimate=pl.CostEstimate(
            flops=len(parts) * 40 * 2 * 128**3,
            bytes_accessed=6 * MIB,
            transcendentals=20 * 128 * 128,
        ),
    )(*tables, *query, *parts, *(() if first else state))


def merge_kernel(here_ref, here_stats_ref, there_ref, there_stats_ref, out_ref, rows_ref):
    rows_ref[: 2 * NZ, :] = there_stats_ref[...]
    rows_ref[2 * NZ :, :] = jnp.zeros((BLOCK - 2 * NZ, BLOCK), jnp.float32)
    here, there = here_stats_ref[...], rows_ref[...].T
    for i in range(NZ):
        m0, m1 = here[:, i : i + 1], there[:, i : i + 1]
        l0, l1 = here[:, NZ + i : NZ + i + 1], there[:, NZ + i : NZ + i + 1]
        m = jnp.maximum(m0, m1)
        f0 = jnp.exp2((m0 - m) * EXP2_SCALE)
        f1 = jnp.exp2((m1 - m) * EXP2_SCALE)
        mixed = here_ref[i] * f0 + there_ref[i].astype(jnp.float32) * f1
        out_ref[i] = (mixed / (l0 * f0 + l1 * f1)).astype(jnp.bfloat16)


def merge(here, here_stats, there, there_stats):
    return pl.pallas_call(
        merge_kernel,
        out_shape=jax.ShapeDtypeStruct(here.shape, jnp.bfloat16),
        in_specs=in_vmem(4),
        out_specs=in_vmem(1)[0],
        scratch_shapes=[pltpu.VMEM((BLOCK, BLOCK), jnp.float32)],
        compiler_params=pltpu.CompilerParams(vmem_limit_bytes=4 * MIB),
    )(here, here_stats, there, there_stats)


def project(a, b, w_own, w_other, first, width, dtype):
    deep = w_own.shape[0]
    tiles = width // TILE_N

    def kernel(a_ref, b_ref, w_hbm, w2_hbm, out_ref, rows_ref, w_ref, sems):
        copies = []
        for tile in range(tiles):
            lanes = pl.ds(first + tile * TILE_N, TILE_N)
            for which, source in enumerate((w_hbm, w2_hbm)):
                copies.append(
                    pltpu.make_async_copy(
                        source.at[:, lanes], w_ref.at[which, tile], sems.at[which, tile]
                    )
                )
                copies[-1].start()
        for which, ref in enumerate((a_ref, b_ref)):
            for head in range(HEADS):
                at = (which * HEADS + head) * HEAD_DIM
                rows_ref[:, at : at + HEAD_DIM] = ref[head]
        for tile in range(tiles):
            copies[2 * tile].wait()
            copies[2 * tile + 1].wait()
            out = jnp.dot(rows_ref[:, :deep], w_ref[0, tile], preferred_element_type=jnp.float32)
            out = out + jnp.dot(
                rows_ref[:, deep:], w_ref[1, tile], preferred_element_type=jnp.float32
            )
            out_ref[:, tile * TILE_N : (tile + 1) * TILE_N] = out.astype(out_ref.dtype)

    anywhere = pl.BlockSpec(memory_space=pl.ANY)
    return pl.pallas_call(
        kernel,
        out_shape=jax.ShapeDtypeStruct((BLOCK, width), dtype),
        in_specs=in_vmem(2) + [anywhere] * 2,
        out_specs=in_vmem(1)[0],
        scratch_shapes=[
            pltpu.VMEM((BLOCK, 2 * deep), jnp.bfloat16),
            pltpu.VMEM((2, tiles, deep, TILE_N), jnp.bfloat16),
            pltpu.SemaphoreType.DMA((2, tiles)),
        ],
        compiler_params=pltpu.CompilerParams(vmem_limit_bytes=12 * MIB),
        cost_estimate=pl.CostEstimate(
            flops=2 * BLOCK * 2 * deep * width, bytes_accessed=4 * MIB, transcendentals=0
        ),
    )(a, b, w_own, w_other)


def add_kernel(near_ref, *refs):
    out_ref = refs[-1]
    at = 0
    for far_ref in refs[:-1]:
        lanes = slice(at, at + far_ref.shape[1])
        out = near_ref[:, lanes] + far_ref[...].astype(jnp.float32)
        out_ref[:, lanes] = out.astype(out_ref.dtype)
        at += far_ref.shape[1]


def add(near, far):
    return pl.pallas_call(
        add_kernel,
        out_shape=jax.ShapeDtypeStruct(near.shape, jnp.bfloat16),
        in_specs=in_vmem(1 + len(far)),
        out_specs=in_vmem(1)[0],
        compiler_params=pltpu.CompilerParams(vmem_limit_bytes=4 * MIB),
    )(near, *far)


GROUPS = (((0,), None), ((1, 3), None), ((2,), 1), ((2,), 0))


def tiles_kernel(mask_ref, *refs):
    y, plane = lax.axis_index("y"), lax.axis_index("xh")
    for group, (columns, on) in enumerate(GROUPS):
        count_ref, block_ref, slot_ref = refs[3 * group : 3 * group + 3]
        first_block = 0 if on is None else ((plane + on) & (XH - 1)) * NZ

        def one_query_block(
            block, at, columns=columns, refs=(block_ref, slot_ref), first_block=first_block
        ):
            block_ref, slot_ref = refs
            row = (first_block + block) * NY + y
            for column, back in enumerate(columns):
                first = plane * (NZ * NY) + ((y - back + NY) & (NY - 1))
                for i in range(NZ):
                    block_ref[at] = block
                    slot_ref[at] = column * NZ + i
                    at = at + jnp.where(mask_ref[row, first + i * NY] != 0, 1, 0)
            return at

        total = lax.fori_loop(0, ROWS if on is None else NZ, one_query_block, jnp.int32(0))
        count_ref[0] = total
        for u in range(UNROLL):
            block_ref[total + u] = 0
            slot_ref[total + u] = 0


def live_tiles(frame_mask):
    out_shape = []
    for columns, on in GROUPS:
        most = (ROWS if on is None else NZ) * NZ * len(columns) + 128
        out_shape += [jax.ShapeDtypeStruct((size,), jnp.int32) for size in (1, most, most)]
    flat = pl.pallas_call(
        tiles_kernel,
        out_shape=tuple(out_shape),
        in_specs=in_smem(1),
        out_specs=tuple(in_smem(len(out_shape))),
        compiler_params=pltpu.CompilerParams(vmem_limit_bytes=4 * MIB),
        cost_estimate=pl.CostEstimate(flops=10**6, bytes_accessed=10**5, transcendentals=0),
    )(frame_mask)
    return [tuple(flat[3 * i : 3 * i + 3]) for i in range(len(GROUPS))]


def local(queries, keys, values, frame_mask, w_out):
    xl, c = lax.axis_index("xl"), lax.axis_index("c")

    width = w_out.shape[1] // (XL * NC)

    def w_columns(w, to_xl, to_c):
        return lax.dynamic_slice(w, (0, (to_xl * NC + to_c) * width), (w.shape[0], width))

    slots = split(queries, keys, values)
    slots, w_out = lax.optimization_barrier((slots, w_out))
    w_own = [w_columns(w_out, to_xl, c) for to_xl in (1 - xl, xl)]
    w_sent = [w_columns(w_out, to_xl, 1 - c) for to_xl in (1 - xl, xl)]
    w_own, w_sent, frame_mask = lax.optimization_barrier((w_own, w_sent, frame_mask))
    w_here = [lax.ppermute(w, "c", shift(NC, 1)) for w in w_sent]
    groups = live_tiles(frame_mask)

    slots = lax.all_to_all(slots, "z", 0, 0, tiled=True)
    slots, w_own, groups = lax.optimization_barrier((slots, w_own, groups))
    low, high = slots[: NZ // 2, BLOCK:], slots[NZ // 2 :, BLOCK:]
    slots, low, high = lax.optimization_barrier((slots, low, high))
    before_low = lax.ppermute(low, "y", shift(NY, 1))
    after_high = lax.ppermute(high, "y", shift(NY, -1))
    query = slots[:, :BLOCK]
    query = (query, lax.ppermute(query, "xh", shift(XH, 1)))
    late_low, late_high, w_here = lax.optimization_barrier((low, high, w_here))
    before_high = lax.ppermute(late_high, "y", shift(NY, 1))
    after_low = lax.ppermute(late_low, "y", shift(NY, -1))
    state = attend(groups[0], query, [low, high], None)
    before_low, after_high, state = lax.optimization_barrier((before_low, after_high, state))
    far_low = lax.ppermute(before_low, "y", shift(NY, 1))
    far_high = lax.ppermute(after_high, "y", shift(NY, -1))
    state = attend(groups[1], query, [before_low, before_high, after_low, after_high], state)
    far_parts = [far_low, far_high]
    sent, sent_stats = attend_last(groups[2], query[1], far_parts, state, False)
    sent, sent_stats, state = lax.optimization_barrier((sent, sent_stats, state))
    there = lax.ppermute(sent, "xh", shift(XH, 1))
    there_stats = lax.ppermute(sent_stats, "xh", shift(XH, 1))
    here, here_stats = attend_last(groups[3], query[0], far_parts, state, True)
    heads = merge(here, here_stats, there, there_stats)
    heads = lax.all_to_all(heads, "z", 0, 0, tiled=True)[:HEADS]
    heads_core = lax.ppermute(heads, "c", shift(NC, 1))
    early = width // TILE_N // 2 * TILE_N
    far = [
        lax.ppermute(
            project(heads, heads_core, w_own[0], w_here[0], first, columns, jnp.bfloat16),
            "xl",
            shift(XL, 1),
        )
        for first, columns in ((0, early), (early, width - early))
    ]
    near = project(heads, heads_core, w_own[1], w_here[1], 0, width, jnp.float32)
    return add(near, far)


def solution(mesh):
    fine = Mesh(mesh.devices.reshape(XH, NZ, NY, XL, NC), ("xh", "z", "y", "xl", "c"))
    seq, head = ("xh", "z", "y"), ("xl", "c")
    in_specs = (P(seq, head), P(seq, head), P(seq, head), P(), P(head, None))
    return jax.shard_map(
        local, mesh=fine, in_specs=in_specs, out_specs=P(seq, head), check_vma=False
    )
```

```python
import jax
import jax.numpy as jnp
from jax import lax
from jax.experimental import pallas as pl
from jax.experimental.pallas import tpu as pltpu
from jax.sharding import Mesh
from jax.sharding import PartitionSpec as P

HEAD_DIM = 128
BLOCK = 128
HEADS = 5
XH, NZ, NY, XL, NC = 2, 8, 4, 2, 2
ROWS = XH * NZ
UNROLL = 8
TILE_N = 256
LOW = -1e30
EXP2_SCALE = HEAD_DIM ** (-0.5) * 1.4426950408889634
MIB = 1024 * 1024


def shift(size, by):
    return [(i, (i + by) % size) for i in range(size)]


def in_vmem(count):
    return [pl.BlockSpec(memory_space=pltpu.VMEM)] * count


def in_smem(count):
    return [pl.BlockSpec(memory_space=pltpu.SMEM)] * count


def split_kernel(q_hbm, k_hbm, v_hbm, slots_hbm, whole_ref, out_ref, sems):
    loads = [
        pltpu.make_async_copy(source, whole_ref.at[t], sems.at[t])
        for t, source in enumerate((q_hbm, k_hbm, v_hbm))
    ]
    for load in loads:
        load.start()
    for t, load in enumerate(loads):
        load.wait()
        for head in range(HEADS):
            lanes = slice(head * HEAD_DIM, (head + 1) * HEAD_DIM)
            out_ref[head, t * BLOCK : (t + 1) * BLOCK, :] = whole_ref[t, :, lanes]
    out = pltpu.make_async_copy(out_ref, slots_hbm.at[:HEADS], sems.at[3])
    out.start()
    out.wait()


def split(queries, keys, values):
    anywhere = pl.BlockSpec(memory_space=pl.ANY)
    part = (3 * BLOCK, HEAD_DIM)
    return pl.pallas_call(
        split_kernel,
        out_shape=jax.ShapeDtypeStruct((NZ,) + part, jnp.bfloat16),
        in_specs=[anywhere] * 3,
        out_specs=anywhere,
        scratch_shapes=[
            pltpu.VMEM((3,) + queries.shape, jnp.bfloat16),
            pltpu.VMEM((HEADS,) + part, jnp.bfloat16),
            pltpu.SemaphoreType.DMA((4,)),
        ],
        compiler_params=pltpu.CompilerParams(vmem_limit_bytes=56 * MIB),
    )(queries, keys, values)


def score_tiles(count, tables, q_ref, kv_ref, s_ref, top_ref):
    block_ref, slot_ref = tables

    def score(step, carry):
        tiles = []
        for u in range(UNROLL):
            e = step * UNROLL + u
            s = lax.dot_general(
                q_ref[block_ref[e]],
                kv_ref[slot_ref[e], :BLOCK, :],
                (((1,), (1,)), ((), ())),
                preferred_element_type=jnp.float32,
            )
            s = jnp.where(e < count, s, LOW)
            s_ref[e] = s
            tiles.append(s)
        for u in range(UNROLL):
            block = block_ref[step * UNROLL + u]
            top_ref[block] = jnp.maximum(top_ref[block], tiles[u])
        return carry

    lax.fori_loop(0, (count + (UNROLL - 1)) // UNROLL, score, 0)


def mix_tiles(count, tables, kv_ref, s_ref, m_ref, l_ref, a_ref):
    block_ref, slot_ref = tables

    def mix(step, carry):
        weights, products = [], []
        for u in range(UNROLL):
            e = step * UNROLL + u
            weight = jnp.exp2((s_ref[e] - m_ref[block_ref[e]]) * EXP2_SCALE)
            weights.append(weight)
            products.append(
                jnp.dot(
                    weight.astype(jnp.bfloat16),
                    kv_ref[slot_ref[e], BLOCK:, :],
                    preferred_element_type=jnp.float32,
                )
            )
        for u in range(UNROLL):
            block = block_ref[step * UNROLL + u]
            l_ref[block] = l_ref[block] + weights[u]
            a_ref[block] = a_ref[block] + products[u]
        return carry

    lax.fori_loop(0, (count + (UNROLL - 1)) // UNROLL, mix, 0)


def stats_of(m_ref, l_ref):
    lane = lax.broadcasted_iota(jnp.int32, (BLOCK, BLOCK), 1)
    stats = jnp.zeros((BLOCK, BLOCK), jnp.float32)
    for i in range(NZ):
        total = jnp.sum(l_ref[i], axis=1, keepdims=True)
        stats = jnp.where(lane == i, m_ref[i], stats)
        stats = jnp.where(lane == NZ + i, total, stats)
    return stats


def hold_parts(parts, kv_ref):
    at = 0
    for part in parts:
        kv_ref[at : at + part.shape[0]] = part[...]
        at += part.shape[0]


def attend_last(tables, query, parts, state, mine):
    slots = sum(part.shape[0] for part in parts)

    def kernel(count_ref, block_ref, slot_ref, q_ref, *refs):
        part_refs, refs = refs[: len(parts)], refs[len(parts) :]
        (m_in, l_in, a_in), refs = refs[:3], refs[3:]
        sums_ref, stats_ref, kv_ref, s_ref, top_ref, m_ref, l_ref, a_ref = refs
        tables = (block_ref, slot_ref)
        plane = lax.axis_index("xh")
        first = (plane if mine else 1 - plane) * NZ
        hold_parts(part_refs, kv_ref)
        count = count_ref[0]
        top_ref[...] = jnp.full(top_ref.shape, LOW, jnp.float32)
        score_tiles(count, tables, q_ref, kv_ref, s_ref, top_ref)
        for i in range(NZ):
            top = jnp.max(top_ref[i], axis=1, keepdims=True)
            old = m_in[first + i]
            new = jnp.maximum(old, top)
            fade = jnp.exp2((old - new) * EXP2_SCALE)
            m_ref[i] = new
            l_ref[i] = l_in[first + i] * fade
            a_ref[i] = a_in[first + i] * fade
        mix_tiles(count, tables, kv_ref, s_ref, m_ref, l_ref, a_ref)
        sums_ref[...] = a_ref[...].astype(sums_ref.dtype)
        stats = stats_of(m_ref, l_ref)
        stats_ref[...] = stats if mine else stats.T[: 2 * NZ]

    half = pltpu.VMEM((NZ, BLOCK, BLOCK), jnp.float32)
    return pl.pallas_call(
        kernel,
        out_shape=(
            jax.ShapeDtypeStruct((NZ, BLOCK, HEAD_DIM), jnp.float32 if mine else jnp.bfloat16),
            jax.ShapeDtypeStruct((BLOCK if mine else 2 * NZ, BLOCK), jnp.float32),
        ),
        in_specs=in_smem(3) + in_vmem(1 + len(parts) + 3),
        out_specs=tuple(in_vmem(2)),
        scratch_shapes=[
            pltpu.VMEM((slots, 2 * BLOCK, HEAD_DIM), jnp.bfloat16),
            pltpu.VMEM((NZ * slots, BLOCK, BLOCK), jnp.float32),
            half,
            half,
            half,
            half,
        ],
        compiler_params=pltpu.CompilerParams(vmem_limit_bytes=28 * MIB),
        cost_estimate=pl.CostEstimate(
            flops=20 * 2 * 128**3, bytes_accessed=3 * MIB, transcendentals=10 * 128 * 128
        ),
    )(*tables, query, *parts, *state)


def attend(tables, query, parts, state):
    first = state is None
    slots = sum(part.shape[0] for part in parts)
    whole = jax.ShapeDtypeStruct((ROWS, BLOCK, BLOCK), jnp.float32)

    def kernel(count_ref, block_ref, slot_ref, own_ref, other_ref, *refs):
        tables = (block_ref, slot_ref)
        plane = lax.axis_index("xh")
        part_refs, refs = refs[: len(parts)], refs[len(parts) :]
        if not first:
            (m_in, l_in, a_in), refs = refs[:3], refs[3:]
        m_ref, l_ref, a_ref, q_ref, kv_ref, s_ref, top_ref = refs
        q_ref[pl.ds(plane * NZ, NZ)] = own_ref[...]
        q_ref[pl.ds((1 - plane) * NZ, NZ)] = other_ref[...]
        hold_parts(part_refs, kv_ref)
        count = count_ref[0]
        top_ref[...] = jnp.full(top_ref.shape, LOW, jnp.float32)
        score_tiles(count, tables, q_ref, kv_ref, s_ref, top_ref)
        for block in range(ROWS):
            top = jnp.max(top_ref[block], axis=1, keepdims=True)
            if first:
                m_ref[block] = jnp.broadcast_to(top, (BLOCK, BLOCK))
                l_ref[block] = jnp.zeros((BLOCK, BLOCK), jnp.float32)
                a_ref[block] = jnp.zeros((BLOCK, HEAD_DIM), jnp.float32)
            else:
                new = jnp.maximum(m_in[block], top)
                fade = jnp.exp2((m_in[block] - new) * EXP2_SCALE)
                m_ref[block] = new
                l_ref[block] = l_in[block] * fade
                a_ref[block] = a_in[block] * fade
        mix_tiles(count, tables, kv_ref, s_ref, m_ref, l_ref, a_ref)

    return pl.pallas_call(
        kernel,
        out_shape=(whole, whole, whole),
        in_specs=in_smem(3) + in_vmem(2 + len(parts) + (0 if first else 3)),
        out_specs=tuple(in_vmem(3)),
        scratch_shapes=[
            pltpu.VMEM((ROWS, BLOCK, HEAD_DIM), jnp.bfloat16),
            pltpu.VMEM((slots, 2 * BLOCK, HEAD_DIM), jnp.bfloat16),
            pltpu.VMEM((ROWS * slots, BLOCK, BLOCK), jnp.float32),
            pltpu.VMEM((ROWS, BLOCK, BLOCK), jnp.float32),
        ],
        compiler_params=pltpu.CompilerParams(vmem_limit_bytes=28 * MIB),
        cost_estimate=pl.CostEstimate(
            flops=len(parts) * 40 * 2 * 128**3,
            bytes_accessed=6 * MIB,
            transcendentals=20 * 128 * 128,
        ),
    )(*tables, *query, *parts, *(() if first else state))


def merge_kernel(here_ref, here_stats_ref, there_ref, there_stats_ref, out_ref, rows_ref):
    rows_ref[: 2 * NZ, :] = there_stats_ref[...]
    rows_ref[2 * NZ :, :] = jnp.zeros((BLOCK - 2 * NZ, BLOCK), jnp.float32)
    here, there = here_stats_ref[...], rows_ref[...].T
    for i in range(NZ):
        m0, m1 = here[:, i : i + 1], there[:, i : i + 1]
        l0, l1 = here[:, NZ + i : NZ + i + 1], there[:, NZ + i : NZ + i + 1]
        m = jnp.maximum(m0, m1)
        f0 = jnp.exp2((m0 - m) * EXP2_SCALE)
        f1 = jnp.exp2((m1 - m) * EXP2_SCALE)
        mixed = here_ref[i] * f0 + there_ref[i].astype(jnp.float32) * f1
        out_ref[i] = (mixed / (l0 * f0 + l1 * f1)).astype(jnp.bfloat16)


def merge(here, here_stats, there, there_stats):
    return pl.pallas_call(
        merge_kernel,
        out_shape=jax.ShapeDtypeStruct(here.shape, jnp.bfloat16),
        in_specs=in_vmem(4),
        out_specs=in_vmem(1)[0],
        scratch_shapes=[pltpu.VMEM((BLOCK, BLOCK), jnp.float32)],
        compiler_params=pltpu.CompilerParams(vmem_limit_bytes=4 * MIB),
    )(here, here_stats, there, there_stats)


def project(a, b, w_own, w_other, first, width, dtype):
    deep = w_own.shape[0]
    tiles = width // TILE_N

    def kernel(a_ref, b_ref, w_hbm, w2_hbm, out_ref, rows_ref, w_ref, sems):
        copies = []
        for tile in range(tiles):
            lanes = pl.ds(first + tile * TILE_N, TILE_N)
            for which, source in enumerate((w_hbm, w2_hbm)):
                copies.append(
                    pltpu.make_async_copy(
                        source.at[:, lanes], w_ref.at[which, tile], sems.at[which, tile]
                    )
                )
                copies[-1].start()
        for which, ref in enumerate((a_ref, b_ref)):
            for head in range(HEADS):
                at = (which * HEADS + head) * HEAD_DIM
                rows_ref[:, at : at + HEAD_DIM] = ref[head]
        for tile in range(tiles):
            copies[2 * tile].wait()
            copies[2 * tile + 1].wait()
            out = jnp.dot(rows_ref[:, :deep], w_ref[0, tile], preferred_element_type=jnp.float32)
            out = out + jnp.dot(
                rows_ref[:, deep:], w_ref[1, tile], preferred_element_type=jnp.float32
            )
            out_ref[:, tile * TILE_N : (tile + 1) * TILE_N] = out.astype(out_ref.dtype)

    anywhere = pl.BlockSpec(memory_space=pl.ANY)
    return pl.pallas_call(
        kernel,
        out_shape=jax.ShapeDtypeStruct((BLOCK, width), dtype),
        in_specs=in_vmem(2) + [anywhere] * 2,
        out_specs=in_vmem(1)[0],
        scratch_shapes=[
            pltpu.VMEM((BLOCK, 2 * deep), jnp.bfloat16),
            pltpu.VMEM((2, tiles, deep, TILE_N), jnp.bfloat16),
            pltpu.SemaphoreType.DMA((2, tiles)),
        ],
        compiler_params=pltpu.CompilerParams(vmem_limit_bytes=12 * MIB),
        cost_estimate=pl.CostEstimate(
            flops=2 * BLOCK * 2 * deep * width, bytes_accessed=4 * MIB, transcendentals=0
        ),
    )(a, b, w_own, w_other)


def add_kernel(near_ref, *refs):
    out_ref = refs[-1]
    at = 0
    for far_ref in refs[:-1]:
        lanes = slice(at, at + far_ref.shape[1])
        out = near_ref[:, lanes] + far_ref[...].astype(jnp.float32)
        out_ref[:, lanes] = out.astype(out_ref.dtype)
        at += far_ref.shape[1]


def add(near, far):
    return pl.pallas_call(
        add_kernel,
        out_shape=jax.ShapeDtypeStruct(near.shape, jnp.bfloat16),
        in_specs=in_vmem(1 + len(far)),
        out_specs=in_vmem(1)[0],
        compiler_params=pltpu.CompilerParams(vmem_limit_bytes=4 * MIB),
    )(near, *far)


GROUPS = (((0,), None), ((1, 3), None), ((2,), 1), ((2,), 0))


def tiles_kernel(mask_ref, *refs):
    y, plane = lax.axis_index("y"), lax.axis_index("xh")
    for group, (columns, on) in enumerate(GROUPS):
        count_ref, block_ref, slot_ref = refs[3 * group : 3 * group + 3]
        first_block = 0 if on is None else ((plane + on) & (XH - 1)) * NZ

        def one_query_block(
            block, at, columns=columns, refs=(block_ref, slot_ref), first_block=first_block
        ):
            block_ref, slot_ref = refs
            row = (first_block + block) * NY + y
            for column, back in enumerate(columns):
                first = plane * (NZ * NY) + ((y - back + NY) & (NY - 1))
                for i in range(NZ):
                    block_ref[at] = block
                    slot_ref[at] = column * NZ + i
                    at = at + jnp.where(mask_ref[row, first + i * NY] != 0, 1, 0)
            return at

        total = lax.fori_loop(0, ROWS if on is None else NZ, one_query_block, jnp.int32(0))
        count_ref[0] = total
        for u in range(UNROLL):
            block_ref[total + u] = 0
            slot_ref[total + u] = 0


def live_tiles(frame_mask):
    out_shape = []
    for columns, on in GROUPS:
        most = (ROWS if on is None else NZ) * NZ * len(columns) + 128
        out_shape += [jax.ShapeDtypeStruct((size,), jnp.int32) for size in (1, most, most)]
    flat = pl.pallas_call(
        tiles_kernel,
        out_shape=tuple(out_shape),
        in_specs=in_smem(1),
        out_specs=tuple(in_smem(len(out_shape))),
        compiler_params=pltpu.CompilerParams(vmem_limit_bytes=4 * MIB),
        cost_estimate=pl.CostEstimate(flops=10**6, bytes_accessed=10**5, transcendentals=0),
    )(frame_mask)
    return [tuple(flat[3 * i : 3 * i + 3]) for i in range(len(GROUPS))]


def local(queries, keys, values, frame_mask, w_out):
    xl, c = lax.axis_index("xl"), lax.axis_index("c")

    width = w_out.shape[1] // (XL * NC)

    def w_columns(w, to_xl, to_c):
        return lax.dynamic_slice(w, (0, (to_xl * NC + to_c) * width), (w.shape[0], width))

    slots = split(queries, keys, values)
    slots, w_out = lax.optimization_barrier((slots, w_out))
    w_own = [w_columns(w_out, to_xl, c) for to_xl in (1 - xl, xl)]
    w_sent = [w_columns(w_out, to_xl, 1 - c) for to_xl in (1 - xl, xl)]
    w_own, w_sent, frame_mask = lax.optimization_barrier((w_own, w_sent, frame_mask))
    w_here = [lax.ppermute(w, "c", shift(NC, 1)) for w in w_sent]
    groups = live_tiles(frame_mask)

    slots = lax.all_to_all(slots, "z", 0, 0, tiled=True)
    slots, w_own, groups = lax.optimization_barrier((slots, w_own, groups))
    low, high = slots[: NZ // 2, BLOCK:], slots[NZ // 2 :, BLOCK:]
    slots, low, high = lax.optimization_barrier((slots, low, high))
    before_low = lax.ppermute(low, "y", shift(NY, 1))
    after_high = lax.ppermute(high, "y", shift(NY, -1))
    query = slots[:, :BLOCK]
    query = (query, lax.ppermute(query, "xh", shift(XH, 1)))
    late_low, late_high, w_here = lax.optimization_barrier((low, high, w_here))
    before_high = lax.ppermute(late_high, "y", shift(NY, 1))
    after_low = lax.ppermute(late_low, "y", shift(NY, -1))
    state = attend(groups[0], query, [low, high], None)
    before_low, after_high, state = lax.optimization_barrier((before_low, after_high, state))
    far_low = lax.ppermute(before_low, "y", shift(NY, 1))
    far_high = lax.ppermute(after_high, "y", shift(NY, -1))
    state = attend(groups[1], query, [before_low, before_high, after_low, after_high], state)
    far_parts = [far_low, far_high]
    sent, sent_stats = attend_last(groups[2], query[1], far_parts, state, False)
    sent, sent_stats, state = lax.optimization_barrier((sent, sent_stats, state))
    there = lax.ppermute(sent, "xh", shift(XH, 1))
    there_stats = lax.ppermute(sent_stats, "xh", shift(XH, 1))
    here, here_stats = attend_last(groups[3], query[0], far_parts, state, True)
    heads = merge(here, here_stats, there, there_stats)
    heads = lax.all_to_all(heads, "z", 0, 0, tiled=True)[:HEADS]
    heads_core = lax.ppermute(heads, "c", shift(NC, 1))
    early = width // TILE_N // 2 * TILE_N
    far = [
        lax.ppermute(
            project(heads, heads_core, w_own[0], w_here[0], first, columns, jnp.bfloat16),
            "xl",
            shift(XL, 1),
        )
        for first, columns in ((0, early), (early, width - early))
    ]
    near = project(heads, heads_core, w_own[1], w_here[1], 0, width, jnp.float32)
    return add(near, far)


def solution(mesh):
    fine = Mesh(mesh.devices.reshape(XH, NZ, NY, XL, NC), ("xh", "z", "y", "xl", "c"))
    seq, head = ("xh", "z", "y"), ("xl", "c")
    in_specs = (P(seq, head), P(seq, head), P(seq, head), P(), P(head, None))
    return jax.shard_map(
        local, mesh=fine, in_specs=in_specs, out_specs=P(seq, head), check_vma=False
    )
```

```python
import jax
import jax.numpy as jnp
from jax import lax
from jax.experimental import pallas as pl
from jax.experimental.pallas import tpu as pltpu
from jax.sharding import Mesh
from jax.sharding import PartitionSpec as P

HEAD_DIM = 128
BLOCK = 128
HEADS = 5
XH, NZ, NY, XL, NC = 2, 8, 4, 2, 2
ROWS = XH * NZ
UNROLL = 8
TILE_N = 256
LOW = -1e30
EXP2_SCALE = HEAD_DIM ** (-0.5) * 1.4426950408889634
MIB = 1024 * 1024


def shift(size, by):
    return [(i, (i + by) % size) for i in range(size)]


def in_vmem(count):
    return [pl.BlockSpec(memory_space=pltpu.VMEM)] * count


def in_smem(count):
    return [pl.BlockSpec(memory_space=pltpu.SMEM)] * count


def split_kernel(q_hbm, k_hbm, v_hbm, slots_hbm, whole_ref, out_ref, sems):
    loads = [
        pltpu.make_async_copy(source, whole_ref.at[t], sems.at[t])
        for t, source in enumerate((q_hbm, k_hbm, v_hbm))
    ]
    for load in loads:
        load.start()
    for t, load in enumerate(loads):
        load.wait()
        for head in range(HEADS):
            lanes = slice(head * HEAD_DIM, (head + 1) * HEAD_DIM)
            out_ref[head, t * BLOCK : (t + 1) * BLOCK, :] = whole_ref[t, :, lanes]
    out = pltpu.make_async_copy(out_ref, slots_hbm.at[:HEADS], sems.at[3])
    out.start()
    out.wait()


def split(queries, keys, values):
    anywhere = pl.BlockSpec(memory_space=pl.ANY)
    part = (3 * BLOCK, HEAD_DIM)
    return pl.pallas_call(
        split_kernel,
        out_shape=jax.ShapeDtypeStruct((NZ,) + part, jnp.bfloat16),
        in_specs=[anywhere] * 3,
        out_specs=anywhere,
        scratch_shapes=[
            pltpu.VMEM((3,) + queries.shape, jnp.bfloat16),
            pltpu.VMEM((HEADS,) + part, jnp.bfloat16),
            pltpu.SemaphoreType.DMA((4,)),
        ],
        compiler_params=pltpu.CompilerParams(vmem_limit_bytes=56 * MIB),
    )(queries, keys, values)


def score_tiles(unroll, count, tables, q_ref, kv_ref, s_ref, top_ref):
    block_ref, slot_ref = tables

    def score(step, carry):
        tiles = []
        for u in range(unroll):
            e = step * unroll + u
            s = lax.dot_general(
                q_ref[block_ref[e]],
                kv_ref[slot_ref[e], :BLOCK, :],
                (((1,), (1,)), ((), ())),
                preferred_element_type=jnp.float32,
            )
            s = jnp.where(e < count, s, LOW)
            s_ref[e] = s
            tiles.append(s)
        for u in range(unroll):
            block = block_ref[step * unroll + u]
            top_ref[block] = jnp.maximum(top_ref[block], tiles[u])
        return carry

    lax.fori_loop(0, (count + (unroll - 1)) // unroll, score, 0)


def mix_tiles(unroll, count, tables, kv_ref, s_ref, m_ref, l_ref, a_ref):
    block_ref, slot_ref = tables

    def mix(step, carry):
        weights, products = [], []
        for u in range(unroll):
            e = step * unroll + u
            weight = jnp.exp2((s_ref[e] - m_ref[block_ref[e]]) * EXP2_SCALE)
            weights.append(weight)
            products.append(
                jnp.dot(
                    weight.astype(jnp.bfloat16),
                    kv_ref[slot_ref[e], BLOCK:, :],
                    preferred_element_type=jnp.float32,
                )
            )
        for u in range(unroll):
            block = block_ref[step * unroll + u]
            l_ref[block] = l_ref[block] + weights[u]
            a_ref[block] = a_ref[block] + products[u]
        return carry

    lax.fori_loop(0, (count + (unroll - 1)) // unroll, mix, 0)


def stats_of(m_ref, l_ref):
    lane = lax.broadcasted_iota(jnp.int32, (BLOCK, BLOCK), 1)
    stats = jnp.zeros((BLOCK, BLOCK), jnp.float32)
    for i in range(NZ):
        total = jnp.sum(l_ref[i], axis=1, keepdims=True)
        stats = jnp.where(lane == i, m_ref[i], stats)
        stats = jnp.where(lane == NZ + i, total, stats)
    return stats


def hold_parts(parts, kv_ref):
    at = 0
    for part in parts:
        kv_ref[at : at + part.shape[0]] = part[...]
        at += part.shape[0]


def attend_last(tables, query, parts, state, mine):
    slots = sum(part.shape[0] for part in parts)
    unroll = UNROLL if mine else UNROLL // 2

    def kernel(count_ref, block_ref, slot_ref, q_ref, *refs):
        part_refs, refs = refs[: len(parts)], refs[len(parts) :]
        (m_in, l_in, a_in), refs = refs[:3], refs[3:]
        sums_ref, stats_ref, kv_ref, s_ref, top_ref, m_ref, l_ref, a_ref = refs
        tables = (block_ref, slot_ref)
        plane = lax.axis_index("xh")
        first = (plane if mine else 1 - plane) * NZ
        hold_parts(part_refs, kv_ref)
        count = count_ref[0]
        top_ref[...] = jnp.full(top_ref.shape, LOW, jnp.float32)
        score_tiles(unroll, count, tables, q_ref, kv_ref, s_ref, top_ref)
        for i in range(NZ):
            top = jnp.max(top_ref[i], axis=1, keepdims=True)
            old = m_in[first + i]
            new = jnp.maximum(old, top)
            fade = jnp.exp2((old - new) * EXP2_SCALE)
            m_ref[i] = new
            l_ref[i] = l_in[first + i] * fade
            a_ref[i] = a_in[first + i] * fade
        mix_tiles(unroll, count, tables, kv_ref, s_ref, m_ref, l_ref, a_ref)
        sums_ref[...] = a_ref[...].astype(sums_ref.dtype)
        stats = stats_of(m_ref, l_ref)
        stats_ref[...] = stats if mine else stats.T[: 2 * NZ]

    half = pltpu.VMEM((NZ, BLOCK, BLOCK), jnp.float32)
    return pl.pallas_call(
        kernel,
        out_shape=(
            jax.ShapeDtypeStruct((NZ, BLOCK, HEAD_DIM), jnp.float32 if mine else jnp.bfloat16),
            jax.ShapeDtypeStruct((BLOCK if mine else 2 * NZ, BLOCK), jnp.float32),
        ),
        in_specs=in_smem(3) + in_vmem(1 + len(parts) + 3),
        out_specs=tuple(in_vmem(2)),
        scratch_shapes=[
            pltpu.VMEM((slots, 2 * BLOCK, HEAD_DIM), jnp.bfloat16),
            pltpu.VMEM((NZ * slots, BLOCK, BLOCK), jnp.float32),
            half,
            half,
            half,
            half,
        ],
        compiler_params=pltpu.CompilerParams(vmem_limit_bytes=28 * MIB),
        cost_estimate=pl.CostEstimate(
            flops=20 * 2 * 128**3, bytes_accessed=3 * MIB, transcendentals=10 * 128 * 128
        ),
    )(*tables, query, *parts, *state)


def attend(tables, query, parts, state):
    first = state is None
    slots = sum(part.shape[0] for part in parts)
    whole = jax.ShapeDtypeStruct((ROWS, BLOCK, BLOCK), jnp.float32)

    def kernel(count_ref, block_ref, slot_ref, own_ref, other_ref, *refs):
        tables = (block_ref, slot_ref)
        plane = lax.axis_index("xh")
        part_refs, refs = refs[: len(parts)], refs[len(parts) :]
        if not first:
            (m_in, l_in, a_in), refs = refs[:3], refs[3:]
        m_ref, l_ref, a_ref, q_ref, kv_ref, s_ref, top_ref = refs
        q_ref[pl.ds(plane * NZ, NZ)] = own_ref[...]
        q_ref[pl.ds((1 - plane) * NZ, NZ)] = other_ref[...]
        hold_parts(part_refs, kv_ref)
        count = count_ref[0]
        top_ref[...] = jnp.full(top_ref.shape, LOW, jnp.float32)
        score_tiles(UNROLL, count, tables, q_ref, kv_ref, s_ref, top_ref)
        for block in range(ROWS):
            top = jnp.max(top_ref[block], axis=1, keepdims=True)
            if first:
                m_ref[block] = jnp.broadcast_to(top, (BLOCK, BLOCK))
                l_ref[block] = jnp.zeros((BLOCK, BLOCK), jnp.float32)
                a_ref[block] = jnp.zeros((BLOCK, HEAD_DIM), jnp.float32)
            else:
                new = jnp.maximum(m_in[block], top)
                fade = jnp.exp2((m_in[block] - new) * EXP2_SCALE)
                m_ref[block] = new
                l_ref[block] = l_in[block] * fade
                a_ref[block] = a_in[block] * fade
        mix_tiles(UNROLL, count, tables, kv_ref, s_ref, m_ref, l_ref, a_ref)

    return pl.pallas_call(
        kernel,
        out_shape=(whole, whole, whole),
        in_specs=in_smem(3) + in_vmem(2 + len(parts) + (0 if first else 3)),
        out_specs=tuple(in_vmem(3)),
        scratch_shapes=[
            pltpu.VMEM((ROWS, BLOCK, HEAD_DIM), jnp.bfloat16),
            pltpu.VMEM((slots, 2 * BLOCK, HEAD_DIM), jnp.bfloat16),
            pltpu.VMEM((ROWS * slots, BLOCK, BLOCK), jnp.float32),
            pltpu.VMEM((ROWS, BLOCK, BLOCK), jnp.float32),
        ],
        compiler_params=pltpu.CompilerParams(vmem_limit_bytes=28 * MIB),
        cost_estimate=pl.CostEstimate(
            flops=len(parts) * 40 * 2 * 128**3,
            bytes_accessed=6 * MIB,
            transcendentals=20 * 128 * 128,
        ),
    )(*tables, *query, *parts, *(() if first else state))


def merge_kernel(here_ref, here_stats_ref, there_ref, there_stats_ref, out_ref, rows_ref):
    rows_ref[: 2 * NZ, :] = there_stats_ref[...]
    rows_ref[2 * NZ :, :] = jnp.zeros((BLOCK - 2 * NZ, BLOCK), jnp.float32)
    here, there = here_stats_ref[...], rows_ref[...].T
    for i in range(NZ):
        m0, m1 = here[:, i : i + 1], there[:, i : i + 1]
        l0, l1 = here[:, NZ + i : NZ + i + 1], there[:, NZ + i : NZ + i + 1]
        m = jnp.maximum(m0, m1)
        f0 = jnp.exp2((m0 - m) * EXP2_SCALE)
        f1 = jnp.exp2((m1 - m) * EXP2_SCALE)
        mixed = here_ref[i] * f0 + there_ref[i].astype(jnp.float32) * f1
        out_ref[i] = (mixed / (l0 * f0 + l1 * f1)).astype(jnp.bfloat16)


def merge(here, here_stats, there, there_stats):
    return pl.pallas_call(
        merge_kernel,
        out_shape=jax.ShapeDtypeStruct(here.shape, jnp.bfloat16),
        in_specs=in_vmem(4),
        out_specs=in_vmem(1)[0],
        scratch_shapes=[pltpu.VMEM((BLOCK, BLOCK), jnp.float32)],
        compiler_params=pltpu.CompilerParams(vmem_limit_bytes=4 * MIB),
    )(here, here_stats, there, there_stats)


def project(a, b, w_own, w_other, first, width, dtype):
    deep = w_own.shape[0]
    tiles = width // TILE_N

    def kernel(a_ref, b_ref, w_hbm, w2_hbm, out_ref, rows_ref, w_ref, sems):
        copies = []
        for tile in range(tiles):
            lanes = pl.ds(first + tile * TILE_N, TILE_N)
            for which, source in enumerate((w_hbm, w2_hbm)):
                copies.append(
                    pltpu.make_async_copy(
                        source.at[:, lanes], w_ref.at[which, tile], sems.at[which, tile]
                    )
                )
                copies[-1].start()
        for which, ref in enumerate((a_ref, b_ref)):
            for head in range(HEADS):
                at = (which * HEADS + head) * HEAD_DIM
                rows_ref[:, at : at + HEAD_DIM] = ref[head]
        for tile in range(tiles):
            copies[2 * tile].wait()
            copies[2 * tile + 1].wait()
            out = jnp.dot(rows_ref[:, :deep], w_ref[0, tile], preferred_element_type=jnp.float32)
            out = out + jnp.dot(
                rows_ref[:, deep:], w_ref[1, tile], preferred_element_type=jnp.float32
            )
            out_ref[:, tile * TILE_N : (tile + 1) * TILE_N] = out.astype(out_ref.dtype)

    anywhere = pl.BlockSpec(memory_space=pl.ANY)
    return pl.pallas_call(
        kernel,
        out_shape=jax.ShapeDtypeStruct((BLOCK, width), dtype),
        in_specs=in_vmem(2) + [anywhere] * 2,
        out_specs=in_vmem(1)[0],
        scratch_shapes=[
            pltpu.VMEM((BLOCK, 2 * deep), jnp.bfloat16),
            pltpu.VMEM((2, tiles, deep, TILE_N), jnp.bfloat16),
            pltpu.SemaphoreType.DMA((2, tiles)),
        ],
        compiler_params=pltpu.CompilerParams(vmem_limit_bytes=12 * MIB),
        cost_estimate=pl.CostEstimate(
            flops=2 * BLOCK * 2 * deep * width, bytes_accessed=4 * MIB, transcendentals=0
        ),
    )(a, b, w_own, w_other)


def add_kernel(near_ref, *refs):
    out_ref = refs[-1]
    at = 0
    for far_ref in refs[:-1]:
        lanes = slice(at, at + far_ref.shape[1])
        out = near_ref[:, lanes] + far_ref[...].astype(jnp.float32)
        out_ref[:, lanes] = out.astype(out_ref.dtype)
        at += far_ref.shape[1]


def add(near, far):
    return pl.pallas_call(
        add_kernel,
        out_shape=jax.ShapeDtypeStruct(near.shape, jnp.bfloat16),
        in_specs=in_vmem(1 + len(far)),
        out_specs=in_vmem(1)[0],
        compiler_params=pltpu.CompilerParams(vmem_limit_bytes=4 * MIB),
    )(near, *far)


GROUPS = (((0,), None), ((1, 3), None), ((2,), 1), ((2,), 0))


def tiles_kernel(mask_ref, *refs):
    y, plane = lax.axis_index("y"), lax.axis_index("xh")
    for group, (columns, on) in enumerate(GROUPS):
        count_ref, block_ref, slot_ref = refs[3 * group : 3 * group + 3]
        first_block = 0 if on is None else ((plane + on) & (XH - 1)) * NZ

        def one_query_block(
            block, at, columns=columns, refs=(block_ref, slot_ref), first_block=first_block
        ):
            block_ref, slot_ref = refs
            row = (first_block + block) * NY + y
            for column, back in enumerate(columns):
                first = plane * (NZ * NY) + ((y - back + NY) & (NY - 1))
                for i in range(NZ):
                    block_ref[at] = block
                    slot_ref[at] = column * NZ + i
                    at = at + jnp.where(mask_ref[row, first + i * NY] != 0, 1, 0)
            return at

        total = lax.fori_loop(0, ROWS if on is None else NZ, one_query_block, jnp.int32(0))
        count_ref[0] = total
        for u in range(UNROLL):
            block_ref[total + u] = 0
            slot_ref[total + u] = 0


def live_tiles(frame_mask):
    out_shape = []
    for columns, on in GROUPS:
        most = (ROWS if on is None else NZ) * NZ * len(columns) + 128
        out_shape += [jax.ShapeDtypeStruct((size,), jnp.int32) for size in (1, most, most)]
    flat = pl.pallas_call(
        tiles_kernel,
        out_shape=tuple(out_shape),
        in_specs=in_smem(1),
        out_specs=tuple(in_smem(len(out_shape))),
        compiler_params=pltpu.CompilerParams(vmem_limit_bytes=4 * MIB),
        cost_estimate=pl.CostEstimate(flops=10**6, bytes_accessed=10**5, transcendentals=0),
    )(frame_mask)
    return [tuple(flat[3 * i : 3 * i + 3]) for i in range(len(GROUPS))]


def local(queries, keys, values, frame_mask, w_out):
    xl, c = lax.axis_index("xl"), lax.axis_index("c")

    width = w_out.shape[1] // (XL * NC)

    def w_columns(w, to_xl, to_c):
        return lax.dynamic_slice(w, (0, (to_xl * NC + to_c) * width), (w.shape[0], width))

    slots = split(queries, keys, values)
    slots, w_out = lax.optimization_barrier((slots, w_out))
    w_own = [w_columns(w_out, to_xl, c) for to_xl in (1 - xl, xl)]
    w_sent = [w_columns(w_out, to_xl, 1 - c) for to_xl in (1 - xl, xl)]
    w_own, w_sent, frame_mask = lax.optimization_barrier((w_own, w_sent, frame_mask))
    w_here = [lax.ppermute(w, "c", shift(NC, 1)) for w in w_sent]
    groups = live_tiles(frame_mask)

    slots = lax.all_to_all(slots, "z", 0, 0, tiled=True)
    slots, w_own, groups = lax.optimization_barrier((slots, w_own, groups))
    low, high = slots[: NZ // 2, BLOCK:], slots[NZ // 2 :, BLOCK:]
    slots, low, high = lax.optimization_barrier((slots, low, high))
    before_low = lax.ppermute(low, "y", shift(NY, 1))
    after_high = lax.ppermute(high, "y", shift(NY, -1))
    slots, late_low, late_high, w_here = lax.optimization_barrier((slots, low, high, w_here))
    query = slots[:, :BLOCK]
    query = (query, lax.ppermute(query, "xh", shift(XH, 1)))
    before_high = lax.ppermute(late_high, "y", shift(NY, 1))
    after_low = lax.ppermute(late_low, "y", shift(NY, -1))
    far_low = lax.ppermute(before_low, "y", shift(NY, 1))
    far_high = lax.ppermute(after_high, "y", shift(NY, -1))
    state = attend(groups[0], query, [low, high], None)
    state = attend(groups[1], query, [before_low, before_high, after_low, after_high], state)
    far_parts = [far_low, far_high]
    sent, sent_stats = attend_last(groups[2], query[1], far_parts, state, False)
    sent, sent_stats, state = lax.optimization_barrier((sent, sent_stats, state))
    there = lax.ppermute(sent, "xh", shift(XH, 1))
    there_stats = lax.ppermute(sent_stats, "xh", shift(XH, 1))
    here, here_stats = attend_last(groups[3], query[0], far_parts, state, True)
    heads = merge(here, here_stats, there, there_stats)
    heads = lax.all_to_all(heads, "z", 0, 0, tiled=True)[:HEADS]
    heads_core = lax.ppermute(heads, "c", shift(NC, 1))
    early = width // TILE_N // 2 * TILE_N
    far = [
        lax.ppermute(
            project(heads, heads_core, w_own[0], w_here[0], first, columns, jnp.bfloat16),
            "xl",
            shift(XL, 1),
        )
        for first, columns in ((0, early), (early, width - early))
    ]
    near = project(heads, heads_core, w_own[1], w_here[1], 0, width, jnp.float32)
    return add(near, far)


def solution(mesh):
    fine = Mesh(mesh.devices.reshape(XH, NZ, NY, XL, NC), ("xh", "z", "y", "xl", "c"))
    seq, head = ("xh", "z", "y"), ("xl", "c")
    in_specs = (P(seq, head), P(seq, head), P(seq, head), P(), P(head, None))
    return jax.shard_map(
        local, mesh=fine, in_specs=in_specs, out_specs=P(seq, head), check_vma=False
    )
```

```python
import jax
import jax.numpy as jnp
from jax import lax
from jax.experimental import pallas as pl
from jax.experimental.pallas import tpu as pltpu
from jax.sharding import Mesh
from jax.sharding import PartitionSpec as P

HEAD_DIM = 128
BLOCK = 128
HEADS = 5
XH, NZ, NY, XL, NC = 2, 8, 4, 2, 2
ROWS = XH * NZ
UNROLL = 8
TILE_N = 256
LOW = -1e30
EXP2_SCALE = HEAD_DIM ** (-0.5) * 1.4426950408889634
MIB = 1024 * 1024


def shift(size, by):
    return [(i, (i + by) % size) for i in range(size)]


def in_vmem(count):
    return [pl.BlockSpec(memory_space=pltpu.VMEM)] * count


def in_smem(count):
    return [pl.BlockSpec(memory_space=pltpu.SMEM)] * count


def split_kernel(q_hbm, k_hbm, v_hbm, slots_hbm, whole_ref, out_ref, sems):
    loads = [
        pltpu.make_async_copy(source, whole_ref.at[t], sems.at[t])
        for t, source in enumerate((q_hbm, k_hbm, v_hbm))
    ]
    for load in loads:
        load.start()
    for t, load in enumerate(loads):
        load.wait()
        for head in range(HEADS):
            lanes = slice(head * HEAD_DIM, (head + 1) * HEAD_DIM)
            out_ref[head, t * BLOCK : (t + 1) * BLOCK, :] = whole_ref[t, :, lanes]
    out = pltpu.make_async_copy(out_ref, slots_hbm.at[:HEADS], sems.at[3])
    out.start()
    out.wait()


def split(queries, keys, values):
    anywhere = pl.BlockSpec(memory_space=pl.ANY)
    part = (3 * BLOCK, HEAD_DIM)
    return pl.pallas_call(
        split_kernel,
        out_shape=jax.ShapeDtypeStruct((NZ,) + part, jnp.bfloat16),
        in_specs=[anywhere] * 3,
        out_specs=anywhere,
        scratch_shapes=[
            pltpu.VMEM((3,) + queries.shape, jnp.bfloat16),
            pltpu.VMEM((HEADS,) + part, jnp.bfloat16),
            pltpu.SemaphoreType.DMA((4,)),
        ],
        compiler_params=pltpu.CompilerParams(vmem_limit_bytes=56 * MIB),
    )(queries, keys, values)


def score_tiles(unroll, count, tables, q_ref, kv_ref, s_ref, top_ref):
    block_ref, slot_ref = tables

    def score(step, carry):
        tiles = []
        for u in range(unroll):
            e = step * unroll + u
            s = lax.dot_general(
                q_ref[block_ref[e]],
                kv_ref[slot_ref[e], :BLOCK, :],
                (((1,), (1,)), ((), ())),
                preferred_element_type=jnp.float32,
            )
            s = jnp.where(e < count, s, LOW)
            s_ref[e] = s
            tiles.append(s)
        for u in range(unroll):
            block = block_ref[step * unroll + u]
            top_ref[block] = jnp.maximum(top_ref[block], tiles[u])
        return carry

    lax.fori_loop(0, (count + (unroll - 1)) // unroll, score, 0)


def mix_tiles(unroll, count, tables, kv_ref, s_ref, m_ref, l_ref, a_ref):
    block_ref, slot_ref = tables

    def mix(step, carry):
        weights, products = [], []
        for u in range(unroll):
            e = step * unroll + u
            weight = jnp.exp2((s_ref[e] - m_ref[block_ref[e]]) * EXP2_SCALE)
            weights.append(weight)
            products.append(
                jnp.dot(
                    weight.astype(jnp.bfloat16),
                    kv_ref[slot_ref[e], BLOCK:, :],
                    preferred_element_type=jnp.float32,
                )
            )
        for u in range(unroll):
            block = block_ref[step * unroll + u]
            l_ref[block] = l_ref[block] + weights[u]
            a_ref[block] = a_ref[block] + products[u]
        return carry

    lax.fori_loop(0, (count + (unroll - 1)) // unroll, mix, 0)


def stats_of(m_ref, l_ref):
    lane = lax.broadcasted_iota(jnp.int32, (BLOCK, BLOCK), 1)
    stats = jnp.zeros((BLOCK, BLOCK), jnp.float32)
    for i in range(NZ):
        total = jnp.sum(l_ref[i], axis=1, keepdims=True)
        stats = jnp.where(lane == i, m_ref[i], stats)
        stats = jnp.where(lane == NZ + i, total, stats)
    return stats


def hold_parts(parts, kv_ref):
    at = 0
    for part in parts:
        kv_ref[at : at + part.shape[0]] = part[...]
        at += part.shape[0]


def attend_last(tables, query, parts, state, mine):
    slots = sum(part.shape[0] for part in parts)
    unroll = UNROLL if mine else UNROLL // 2

    def kernel(count_ref, block_ref, slot_ref, q_ref, *refs):
        part_refs, refs = refs[: len(parts)], refs[len(parts) :]
        (m_in, l_in, a_in), refs = refs[:3], refs[3:]
        sums_ref, stats_ref, kv_ref, s_ref, top_ref, m_ref, l_ref, a_ref = refs
        tables = (block_ref, slot_ref)
        plane = lax.axis_index("xh")
        first = (plane if mine else 1 - plane) * NZ
        hold_parts(part_refs, kv_ref)
        count = count_ref[0]
        top_ref[...] = jnp.full(top_ref.shape, LOW, jnp.float32)
        score_tiles(unroll, count, tables, q_ref, kv_ref, s_ref, top_ref)
        for i in range(NZ):
            top = jnp.max(top_ref[i], axis=1, keepdims=True)
            old = m_in[first + i]
            new = jnp.maximum(old, top)
            fade = jnp.exp2((old - new) * EXP2_SCALE)
            m_ref[i] = new
            l_ref[i] = l_in[first + i] * fade
            a_ref[i] = a_in[first + i] * fade
        mix_tiles(unroll, count, tables, kv_ref, s_ref, m_ref, l_ref, a_ref)
        sums_ref[...] = a_ref[...].astype(sums_ref.dtype)
        stats = stats_of(m_ref, l_ref)
        stats_ref[...] = stats if mine else stats.T[: 2 * NZ]

    half = pltpu.VMEM((NZ, BLOCK, BLOCK), jnp.float32)
    return pl.pallas_call(
        kernel,
        out_shape=(
            jax.ShapeDtypeStruct((NZ, BLOCK, HEAD_DIM), jnp.float32 if mine else jnp.bfloat16),
            jax.ShapeDtypeStruct((BLOCK if mine else 2 * NZ, BLOCK), jnp.float32),
        ),
        in_specs=in_smem(3) + in_vmem(1 + len(parts) + 3),
        out_specs=tuple(in_vmem(2)),
        scratch_shapes=[
            pltpu.VMEM((slots, 2 * BLOCK, HEAD_DIM), jnp.bfloat16),
            pltpu.VMEM((NZ * slots, BLOCK, BLOCK), jnp.float32),
            half,
            half,
            half,
            half,
        ],
        compiler_params=pltpu.CompilerParams(vmem_limit_bytes=28 * MIB),
        cost_estimate=pl.CostEstimate(
            flops=20 * 2 * 128**3, bytes_accessed=3 * MIB, transcendentals=10 * 128 * 128
        ),
    )(*tables, query, *parts, *state)


def attend(tables, query, parts, state):
    first = state is None
    slots = sum(part.shape[0] for part in parts)
    whole = jax.ShapeDtypeStruct((ROWS, BLOCK, BLOCK), jnp.float32)

    def kernel(count_ref, block_ref, slot_ref, own_ref, other_ref, *refs):
        tables = (block_ref, slot_ref)
        plane = lax.axis_index("xh")
        part_refs, refs = refs[: len(parts)], refs[len(parts) :]
        if not first:
            (m_in, l_in, a_in), refs = refs[:3], refs[3:]
        m_ref, l_ref, a_ref, q_ref, kv_ref, s_ref, top_ref = refs
        q_ref[pl.ds(plane * NZ, NZ)] = own_ref[...]
        q_ref[pl.ds((1 - plane) * NZ, NZ)] = other_ref[...]
        hold_parts(part_refs, kv_ref)
        count = count_ref[0]
        top_ref[...] = jnp.full(top_ref.shape, LOW, jnp.float32)
        score_tiles(UNROLL, count, tables, q_ref, kv_ref, s_ref, top_ref)
        for block in range(ROWS):
            top = jnp.max(top_ref[block], axis=1, keepdims=True)
            if first:
                m_ref[block] = jnp.broadcast_to(top, (BLOCK, BLOCK))
                l_ref[block] = jnp.zeros((BLOCK, BLOCK), jnp.float32)
                a_ref[block] = jnp.zeros((BLOCK, HEAD_DIM), jnp.float32)
            else:
                new = jnp.maximum(m_in[block], top)
                fade = jnp.exp2((m_in[block] - new) * EXP2_SCALE)
                m_ref[block] = new
                l_ref[block] = l_in[block] * fade
                a_ref[block] = a_in[block] * fade
        mix_tiles(UNROLL, count, tables, kv_ref, s_ref, m_ref, l_ref, a_ref)

    return pl.pallas_call(
        kernel,
        out_shape=(whole, whole, whole),
        in_specs=in_smem(3) + in_vmem(2 + len(parts) + (0 if first else 3)),
        out_specs=tuple(in_vmem(3)),
        scratch_shapes=[
            pltpu.VMEM((ROWS, BLOCK, HEAD_DIM), jnp.bfloat16),
            pltpu.VMEM((slots, 2 * BLOCK, HEAD_DIM), jnp.bfloat16),
            pltpu.VMEM((ROWS * slots, BLOCK, BLOCK), jnp.float32),
            pltpu.VMEM((ROWS, BLOCK, BLOCK), jnp.float32),
        ],
        compiler_params=pltpu.CompilerParams(vmem_limit_bytes=28 * MIB),
        cost_estimate=pl.CostEstimate(
            flops=len(parts) * 40 * 2 * 128**3,
            bytes_accessed=6 * MIB,
            transcendentals=20 * 128 * 128,
        ),
    )(*tables, *query, *parts, *(() if first else state))


def merge_kernel(here_ref, here_stats_ref, there_ref, there_stats_ref, out_ref, rows_ref):
    rows_ref[: 2 * NZ, :] = there_stats_ref[...]
    rows_ref[2 * NZ :, :] = jnp.zeros((BLOCK - 2 * NZ, BLOCK), jnp.float32)
    here, there = here_stats_ref[...], rows_ref[...].T
    for i in range(NZ):
        m0, m1 = here[:, i : i + 1], there[:, i : i + 1]
        l0, l1 = here[:, NZ + i : NZ + i + 1], there[:, NZ + i : NZ + i + 1]
        m = jnp.maximum(m0, m1)
        f0 = jnp.exp2((m0 - m) * EXP2_SCALE)
        f1 = jnp.exp2((m1 - m) * EXP2_SCALE)
        mixed = here_ref[i] * f0 + there_ref[i].astype(jnp.float32) * f1
        out_ref[i] = (mixed / (l0 * f0 + l1 * f1)).astype(jnp.bfloat16)


def merge(here, here_stats, there, there_stats):
    return pl.pallas_call(
        merge_kernel,
        out_shape=jax.ShapeDtypeStruct(here.shape, jnp.bfloat16),
        in_specs=in_vmem(4),
        out_specs=in_vmem(1)[0],
        scratch_shapes=[pltpu.VMEM((BLOCK, BLOCK), jnp.float32)],
        compiler_params=pltpu.CompilerParams(vmem_limit_bytes=4 * MIB),
    )(here, here_stats, there, there_stats)


def project(heads, w, added, first, width, dtype):
    deep = w.shape[0]
    tiles = width // TILE_N

    def kernel(heads_ref, w_hbm, *refs):
        if added is not None:
            added_ref, refs = refs[0], refs[1:]
        out_ref, rows_ref, w_ref, sems = refs
        copies = []
        for tile in range(tiles):
            lanes = pl.ds(first + tile * TILE_N, TILE_N)
            copies.append(
                pltpu.make_async_copy(w_hbm.at[:, lanes], w_ref.at[tile], sems.at[tile])
            )
            copies[-1].start()
        for head in range(HEADS):
            at = head * HEAD_DIM
            rows_ref[:, at : at + HEAD_DIM] = heads_ref[head]
        for tile in range(tiles):
            copies[tile].wait()
            at = tile * TILE_N
            out = jnp.dot(rows_ref[...], w_ref[tile], preferred_element_type=jnp.float32)
            if added is not None:
                out = out + added_ref[:, first + at : first + at + TILE_N]
            out_ref[:, at : at + TILE_N] = out.astype(out_ref.dtype)

    return pl.pallas_call(
        kernel,
        out_shape=jax.ShapeDtypeStruct((BLOCK, width), dtype),
        in_specs=in_vmem(1)
        + [pl.BlockSpec(memory_space=pl.ANY)]
        + in_vmem(0 if added is None else 1),
        out_specs=in_vmem(1)[0],
        scratch_shapes=[
            pltpu.VMEM((BLOCK, deep), jnp.bfloat16),
            pltpu.VMEM((tiles, deep, TILE_N), jnp.bfloat16),
            pltpu.SemaphoreType.DMA((tiles,)),
        ],
        compiler_params=pltpu.CompilerParams(vmem_limit_bytes=8 * MIB),
        cost_estimate=pl.CostEstimate(
            flops=2 * BLOCK * deep * width, bytes_accessed=2 * MIB, transcendentals=0
        ),
    )(heads, w, *(() if added is None else (added,)))


def add_kernel(near_ref, *refs):
    out_ref = refs[-1]
    at = 0
    for far_ref in refs[:-1]:
        lanes = slice(at, at + far_ref.shape[1])
        out = near_ref[:, lanes] + far_ref[...].astype(jnp.float32)
        out_ref[:, lanes] = out.astype(out_ref.dtype)
        at += far_ref.shape[1]


def add(near, far):
    return pl.pallas_call(
        add_kernel,
        out_shape=jax.ShapeDtypeStruct(near.shape, jnp.bfloat16),
        in_specs=in_vmem(1 + len(far)),
        out_specs=in_vmem(1)[0],
        compiler_params=pltpu.CompilerParams(vmem_limit_bytes=4 * MIB),
    )(near, *far)


GROUPS = (((0,), None), ((1, 3), None), ((2,), 1), ((2,), 0))


def tiles_kernel(mask_ref, *refs):
    y, plane = lax.axis_index("y"), lax.axis_index("xh")
    for group, (columns, on) in enumerate(GROUPS):
        count_ref, block_ref, slot_ref = refs[3 * group : 3 * group + 3]
        first_block = 0 if on is None else ((plane + on) & (XH - 1)) * NZ

        def one_query_block(
            block, at, columns=columns, refs=(block_ref, slot_ref), first_block=first_block
        ):
            block_ref, slot_ref = refs
            row = (first_block + block) * NY + y
            for column, back in enumerate(columns):
                first = plane * (NZ * NY) + ((y - back + NY) & (NY - 1))
                for i in range(NZ):
                    block_ref[at] = block
                    slot_ref[at] = column * NZ + i
                    at = at + jnp.where(mask_ref[row, first + i * NY] != 0, 1, 0)
            return at

        total = lax.fori_loop(0, ROWS if on is None else NZ, one_query_block, jnp.int32(0))
        count_ref[0] = total
        for u in range(UNROLL):
            block_ref[total + u] = 0
            slot_ref[total + u] = 0


def live_tiles(frame_mask):
    out_shape = []
    for columns, on in GROUPS:
        most = (ROWS if on is None else NZ) * NZ * len(columns) + 128
        out_shape += [jax.ShapeDtypeStruct((size,), jnp.int32) for size in (1, most, most)]
    flat = pl.pallas_call(
        tiles_kernel,
        out_shape=tuple(out_shape),
        in_specs=in_smem(1),
        out_specs=tuple(in_smem(len(out_shape))),
        compiler_params=pltpu.CompilerParams(vmem_limit_bytes=4 * MIB),
        cost_estimate=pl.CostEstimate(flops=10**6, bytes_accessed=10**5, transcendentals=0),
    )(frame_mask)
    return [tuple(flat[3 * i : 3 * i + 3]) for i in range(len(GROUPS))]


def local(queries, keys, values, frame_mask, w_out):
    xl, c = lax.axis_index("xl"), lax.axis_index("c")

    width = w_out.shape[1] // (XL * NC)

    def w_columns(w, to_xl, to_c):
        return lax.dynamic_slice(w, (0, (to_xl * NC + to_c) * width), (w.shape[0], width))

    slots = split(queries, keys, values)
    slots, w_out = lax.optimization_barrier((slots, w_out))
    w_own = [w_columns(w_out, to_xl, c) for to_xl in (1 - xl, xl)]
    w_sent = [w_columns(w_out, to_xl, 1 - c) for to_xl in (1 - xl, xl)]
    w_own, w_sent, frame_mask = lax.optimization_barrier((w_own, w_sent, frame_mask))
    w_here = [lax.ppermute(w, "c", shift(NC, 1)) for w in w_sent]
    groups = live_tiles(frame_mask)

    slots = lax.all_to_all(slots, "z", 0, 0, tiled=True)
    slots, w_own, groups = lax.optimization_barrier((slots, w_own, groups))
    low, high = slots[: NZ // 2, BLOCK:], slots[NZ // 2 :, BLOCK:]
    slots, low, high = lax.optimization_barrier((slots, low, high))
    before_low = lax.ppermute(low, "y", shift(NY, 1))
    after_high = lax.ppermute(high, "y", shift(NY, -1))
    slots, late_low, late_high, w_here = lax.optimization_barrier((slots, low, high, w_here))
    query = slots[:, :BLOCK]
    query = (query, lax.ppermute(query, "xh", shift(XH, 1)))
    before_high = lax.ppermute(late_high, "y", shift(NY, 1))
    after_low = lax.ppermute(late_low, "y", shift(NY, -1))
    far_low = lax.ppermute(before_low, "y", shift(NY, 1))
    far_high = lax.ppermute(after_high, "y", shift(NY, -1))
    state = attend(groups[0], query, [low, high], None)
    state = attend(groups[1], query, [before_low, before_high, after_low, after_high], state)
    far_parts = [far_low, far_high]
    sent, sent_stats = attend_last(groups[2], query[1], far_parts, state, False)
    sent, sent_stats, state = lax.optimization_barrier((sent, sent_stats, state))
    there = lax.ppermute(sent, "xh", shift(XH, 1))
    there_stats = lax.ppermute(sent_stats, "xh", shift(XH, 1))
    here, here_stats = attend_last(groups[3], query[0], far_parts, state, True)
    heads = merge(here, here_stats, there, there_stats)
    heads = lax.all_to_all(heads, "z", 0, 0, tiled=True)[:HEADS]
    heads_core = lax.ppermute(heads, "c", shift(NC, 1))
    far_own = project(heads, w_own[0], None, 0, width, jnp.float32)
    early = width // TILE_N // 2 * TILE_N
    far = [
        lax.ppermute(
            project(heads_core, w_here[0], far_own, first, columns, jnp.bfloat16),
            "xl",
            shift(XL, 1),
        )
        for first, columns in ((0, early), (early, width - early))
    ]
    near = project(heads, w_own[1], None, 0, width, jnp.float32)
    near = project(heads_core, w_here[1], near, 0, width, jnp.float32)
    return add(near, far)


def solution(mesh):
    fine = Mesh(mesh.devices.reshape(XH, NZ, NY, XL, NC), ("xh", "z", "y", "xl", "c"))
    seq, head = ("xh", "z", "y"), ("xl", "c")
    in_specs = (P(seq, head), P(seq, head), P(seq, head), P(), P(head, None))
    return jax.shard_map(
        local, mesh=fine, in_specs=in_specs, out_specs=P(seq, head), check_vma=False
    )
```

```python
import jax
import jax.numpy as jnp
from jax import lax
from jax.experimental import pallas as pl
from jax.experimental.pallas import tpu as pltpu
from jax.sharding import Mesh
from jax.sharding import PartitionSpec as P

HEAD_DIM = 128
BLOCK = 128
HEADS = 5
XH, NZ, NY, XL, NC = 2, 8, 4, 2, 2
ROWS = XH * NZ
UNROLL = 8
TILE_N = 256
LOW = -1e30
EXP2_SCALE = HEAD_DIM ** (-0.5) * 1.4426950408889634
MIB = 1024 * 1024


def shift(size, by):
    return [(i, (i + by) % size) for i in range(size)]


def in_vmem(count):
    return [pl.BlockSpec(memory_space=pltpu.VMEM)] * count


def in_smem(count):
    return [pl.BlockSpec(memory_space=pltpu.SMEM)] * count


def split_kernel(q_hbm, k_hbm, v_hbm, slots_hbm, whole_ref, out_ref, sems):
    loads = [
        pltpu.make_async_copy(source, whole_ref.at[t], sems.at[t])
        for t, source in enumerate((q_hbm, k_hbm, v_hbm))
    ]
    for load in loads:
        load.start()
    stores = []
    for t, load in enumerate(loads):
        load.wait()
        for head in range(HEADS):
            lanes = slice(head * HEAD_DIM, (head + 1) * HEAD_DIM)
            out_ref[t, head] = whole_ref[t, :, lanes]
        rows = pl.ds(t * BLOCK, BLOCK)
        stores.append(
            pltpu.make_async_copy(out_ref.at[t], slots_hbm.at[:HEADS, rows], sems.at[3 + t])
        )
        stores[-1].start()
    for store in stores:
        store.wait()


def split(queries, keys, values):
    anywhere = pl.BlockSpec(memory_space=pl.ANY)
    part = (3 * BLOCK, HEAD_DIM)
    return pl.pallas_call(
        split_kernel,
        out_shape=jax.ShapeDtypeStruct((NZ,) + part, jnp.bfloat16),
        in_specs=[anywhere] * 3,
        out_specs=anywhere,
        scratch_shapes=[
            pltpu.VMEM((3,) + queries.shape, jnp.bfloat16),
            pltpu.VMEM((3, HEADS, BLOCK, HEAD_DIM), jnp.bfloat16),
            pltpu.SemaphoreType.DMA((6,)),
        ],
        compiler_params=pltpu.CompilerParams(vmem_limit_bytes=56 * MIB),
    )(queries, keys, values)


def score_tiles(unroll, count, tables, q_ref, kv_ref, s_ref, top_ref):
    block_ref, slot_ref = tables

    def score(step, carry):
        tiles = []
        for u in range(unroll):
            e = step * unroll + u
            s = lax.dot_general(
                q_ref[block_ref[e]],
                kv_ref[slot_ref[e], :BLOCK, :],
                (((1,), (1,)), ((), ())),
                preferred_element_type=jnp.float32,
            )
            s = jnp.where(e < count, s, LOW)
            s_ref[e] = s
            tiles.append(s)
        for u in range(unroll):
            block = block_ref[step * unroll + u]
            top_ref[block] = jnp.maximum(top_ref[block], tiles[u])
        return carry

    lax.fori_loop(0, (count + (unroll - 1)) // unroll, score, 0)


def mix_tiles(unroll, count, tables, kv_ref, s_ref, m_ref, l_ref, a_ref):
    block_ref, slot_ref = tables

    def mix(step, carry):
        weights, products = [], []
        for u in range(unroll):
            e = step * unroll + u
            weight = jnp.exp2((s_ref[e] - m_ref[block_ref[e]]) * EXP2_SCALE)
            weights.append(weight)
            products.append(
                jnp.dot(
                    weight.astype(jnp.bfloat16),
                    kv_ref[slot_ref[e], BLOCK:, :],
                    preferred_element_type=jnp.float32,
                )
            )
        for u in range(unroll):
            block = block_ref[step * unroll + u]
            l_ref[block] = l_ref[block] + weights[u]
            a_ref[block] = a_ref[block] + products[u]
        return carry

    lax.fori_loop(0, (count + (unroll - 1)) // unroll, mix, 0)


def stats_of(m_ref, l_ref):
    lane = lax.broadcasted_iota(jnp.int32, (BLOCK, BLOCK), 1)
    stats = jnp.zeros((BLOCK, BLOCK), jnp.float32)
    for i in range(NZ):
        total = jnp.sum(l_ref[i], axis=1, keepdims=True)
        stats = jnp.where(lane == i, m_ref[i], stats)
        stats = jnp.where(lane == NZ + i, total, stats)
    return stats


def hold_parts(parts, kv_ref):
    at = 0
    for part in parts:
        kv_ref[at : at + part.shape[0]] = part[...]
        at += part.shape[0]


def attend_last(tables, query, parts, state, mine):
    slots = sum(part.shape[0] for part in parts)
    unroll = UNROLL if mine else UNROLL // 2

    def kernel(count_ref, block_ref, slot_ref, q_ref, *refs):
        part_refs, refs = refs[: len(parts)], refs[len(parts) :]
        (m_in, l_in, a_in), refs = refs[:3], refs[3:]
        sums_ref, stats_ref, kv_ref, s_ref, top_ref, m_ref, l_ref, a_ref = refs
        tables = (block_ref, slot_ref)
        plane = lax.axis_index("xh")
        first = (plane if mine else 1 - plane) * NZ
        hold_parts(part_refs, kv_ref)
        count = count_ref[0]
        top_ref[...] = jnp.full(top_ref.shape, LOW, jnp.float32)
        score_tiles(unroll, count, tables, q_ref, kv_ref, s_ref, top_ref)
        for i in range(NZ):
            top = jnp.max(top_ref[i], axis=1, keepdims=True)
            old = m_in[first + i]
            new = jnp.maximum(old, top)
            fade = jnp.exp2((old - new) * EXP2_SCALE)
            m_ref[i] = new
            l_ref[i] = l_in[first + i] * fade
            a_ref[i] = a_in[first + i] * fade
        mix_tiles(unroll, count, tables, kv_ref, s_ref, m_ref, l_ref, a_ref)
        sums_ref[...] = a_ref[...].astype(sums_ref.dtype)
        stats = stats_of(m_ref, l_ref)
        stats_ref[...] = stats if mine else stats.T[: 2 * NZ]

    half = pltpu.VMEM((NZ, BLOCK, BLOCK), jnp.float32)
    return pl.pallas_call(
        kernel,
        out_shape=(
            jax.ShapeDtypeStruct((NZ, BLOCK, HEAD_DIM), jnp.float32 if mine else jnp.bfloat16),
            jax.ShapeDtypeStruct((BLOCK if mine else 2 * NZ, BLOCK), jnp.float32),
        ),
        in_specs=in_smem(3) + in_vmem(1 + len(parts) + 3),
        out_specs=tuple(in_vmem(2)),
        scratch_shapes=[
            pltpu.VMEM((slots, 2 * BLOCK, HEAD_DIM), jnp.bfloat16),
            pltpu.VMEM((NZ * slots, BLOCK, BLOCK), jnp.float32),
            half,
            half,
            half,
            half,
        ],
        compiler_params=pltpu.CompilerParams(vmem_limit_bytes=28 * MIB),
        cost_estimate=pl.CostEstimate(
            flops=20 * 2 * 128**3, bytes_accessed=3 * MIB, transcendentals=10 * 128 * 128
        ),
    )(*tables, query, *parts, *state)


def attend(tables, query, parts, state):
    first = state is None
    slots = sum(part.shape[0] for part in parts)
    whole = jax.ShapeDtypeStruct((ROWS, BLOCK, BLOCK), jnp.float32)

    def kernel(count_ref, block_ref, slot_ref, own_ref, other_ref, *refs):
        tables = (block_ref, slot_ref)
        plane = lax.axis_index("xh")
        part_refs, refs = refs[: len(parts)], refs[len(parts) :]
        if not first:
            (m_in, l_in, a_in), refs = refs[:3], refs[3:]
        m_ref, l_ref, a_ref, q_ref, kv_ref, s_ref, top_ref = refs
        q_ref[pl.ds(plane * NZ, NZ)] = own_ref[...]
        q_ref[pl.ds((1 - plane) * NZ, NZ)] = other_ref[...]
        hold_parts(part_refs, kv_ref)
        count = count_ref[0]
        top_ref[...] = jnp.full(top_ref.shape, LOW, jnp.float32)
        score_tiles(UNROLL, count, tables, q_ref, kv_ref, s_ref, top_ref)
        for block in range(ROWS):
            top = jnp.max(top_ref[block], axis=1, keepdims=True)
            if first:
                m_ref[block] = jnp.broadcast_to(top, (BLOCK, BLOCK))
                l_ref[block] = jnp.zeros((BLOCK, BLOCK), jnp.float32)
                a_ref[block] = jnp.zeros((BLOCK, HEAD_DIM), jnp.float32)
            else:
                new = jnp.maximum(m_in[block], top)
                fade = jnp.exp2((m_in[block] - new) * EXP2_SCALE)
                m_ref[block] = new
                l_ref[block] = l_in[block] * fade
                a_ref[block] = a_in[block] * fade
        mix_tiles(UNROLL, count, tables, kv_ref, s_ref, m_ref, l_ref, a_ref)

    return pl.pallas_call(
        kernel,
        out_shape=(whole, whole, whole),
        in_specs=in_smem(3) + in_vmem(2 + len(parts) + (0 if first else 3)),
        out_specs=tuple(in_vmem(3)),
        scratch_shapes=[
            pltpu.VMEM((ROWS, BLOCK, HEAD_DIM), jnp.bfloat16),
            pltpu.VMEM((slots, 2 * BLOCK, HEAD_DIM), jnp.bfloat16),
            pltpu.VMEM((ROWS * slots, BLOCK, BLOCK), jnp.float32),
            pltpu.VMEM((ROWS, BLOCK, BLOCK), jnp.float32),
        ],
        compiler_params=pltpu.CompilerParams(vmem_limit_bytes=28 * MIB),
        cost_estimate=pl.CostEstimate(
            flops=len(parts) * 40 * 2 * 128**3,
            bytes_accessed=6 * MIB,
            transcendentals=20 * 128 * 128,
        ),
    )(*tables, *query, *parts, *(() if first else state))


def merge_kernel(here_ref, here_stats_ref, there_ref, there_stats_ref, out_ref, rows_ref):
    rows_ref[: 2 * NZ, :] = there_stats_ref[...]
    rows_ref[2 * NZ :, :] = jnp.zeros((BLOCK - 2 * NZ, BLOCK), jnp.float32)
    here, there = here_stats_ref[...], rows_ref[...].T
    for i in range(NZ):
        m0, m1 = here[:, i : i + 1], there[:, i : i + 1]
        l0, l1 = here[:, NZ + i : NZ + i + 1], there[:, NZ + i : NZ + i + 1]
        m = jnp.maximum(m0, m1)
        f0 = jnp.exp2((m0 - m) * EXP2_SCALE)
        f1 = jnp.exp2((m1 - m) * EXP2_SCALE)
        mixed = here_ref[i] * f0 + there_ref[i].astype(jnp.float32) * f1
        out_ref[i] = (mixed / (l0 * f0 + l1 * f1)).astype(jnp.bfloat16)


def merge(here, here_stats, there, there_stats):
    return pl.pallas_call(
        merge_kernel,
        out_shape=jax.ShapeDtypeStruct(here.shape, jnp.bfloat16),
        in_specs=in_vmem(4),
        out_specs=in_vmem(1)[0],
        scratch_shapes=[pltpu.VMEM((BLOCK, BLOCK), jnp.float32)],
        compiler_params=pltpu.CompilerParams(vmem_limit_bytes=4 * MIB),
    )(here, here_stats, there, there_stats)


def project(heads, w, added, first, width, dtype):
    deep = w.shape[0]
    tiles = width // TILE_N

    def kernel(heads_ref, w_hbm, *refs):
        if added is not None:
            added_ref, refs = refs[0], refs[1:]
        out_ref, rows_ref, w_ref, sems = refs
        copies = []
        for tile in range(tiles):
            lanes = pl.ds(first + tile * TILE_N, TILE_N)
            copies.append(
                pltpu.make_async_copy(w_hbm.at[:, lanes], w_ref.at[tile], sems.at[tile])
            )
            copies[-1].start()
        for head in range(HEADS):
            at = head * HEAD_DIM
            rows_ref[:, at : at + HEAD_DIM] = heads_ref[head]
        for tile in range(tiles):
            copies[tile].wait()
            at = tile * TILE_N
            out = jnp.dot(rows_ref[...], w_ref[tile], preferred_element_type=jnp.float32)
            if added is not None:
                out = out + added_ref[:, first + at : first + at + TILE_N]
            out_ref[:, at : at + TILE_N] = out.astype(out_ref.dtype)

    return pl.pallas_call(
        kernel,
        out_shape=jax.ShapeDtypeStruct((BLOCK, width), dtype),
        in_specs=in_vmem(1)
        + [pl.BlockSpec(memory_space=pl.ANY)]
        + in_vmem(0 if added is None else 1),
        out_specs=in_vmem(1)[0],
        scratch_shapes=[
            pltpu.VMEM((BLOCK, deep), jnp.bfloat16),
            pltpu.VMEM((tiles, deep, TILE_N), jnp.bfloat16),
            pltpu.SemaphoreType.DMA((tiles,)),
        ],
        compiler_params=pltpu.CompilerParams(vmem_limit_bytes=8 * MIB),
        cost_estimate=pl.CostEstimate(
            flops=2 * BLOCK * deep * width, bytes_accessed=2 * MIB, transcendentals=0
        ),
    )(heads, w, *(() if added is None else (added,)))


def add_kernel(near_ref, *refs):
    out_ref = refs[-1]
    at = 0
    for far_ref in refs[:-1]:
        lanes = slice(at, at + far_ref.shape[1])
        out = near_ref[:, lanes] + far_ref[...].astype(jnp.float32)
        out_ref[:, lanes] = out.astype(out_ref.dtype)
        at += far_ref.shape[1]


def add(near, far):
    return pl.pallas_call(
        add_kernel,
        out_shape=jax.ShapeDtypeStruct(near.shape, jnp.bfloat16),
        in_specs=in_vmem(1 + len(far)),
        out_specs=in_vmem(1)[0],
        compiler_params=pltpu.CompilerParams(vmem_limit_bytes=4 * MIB),
    )(near, *far)


GROUPS = (((0,), None), ((1, 3), None), ((2,), 1), ((2,), 0))


def tiles_kernel(mask_ref, *refs):
    y, plane = lax.axis_index("y"), lax.axis_index("xh")
    for group, (columns, on) in enumerate(GROUPS):
        count_ref, block_ref, slot_ref = refs[3 * group : 3 * group + 3]
        first_block = 0 if on is None else ((plane + on) & (XH - 1)) * NZ

        def one_query_block(
            block, at, columns=columns, refs=(block_ref, slot_ref), first_block=first_block
        ):
            block_ref, slot_ref = refs
            row = (first_block + block) * NY + y
            for column, back in enumerate(columns):
                first = plane * (NZ * NY) + ((y - back + NY) & (NY - 1))
                for i in range(NZ):
                    block_ref[at] = block
                    slot_ref[at] = column * NZ + i
                    at = at + jnp.where(mask_ref[row, first + i * NY] != 0, 1, 0)
            return at

        total = lax.fori_loop(0, ROWS if on is None else NZ, one_query_block, jnp.int32(0))
        count_ref[0] = total
        for u in range(UNROLL):
            block_ref[total + u] = 0
            slot_ref[total + u] = 0


def live_tiles(frame_mask):
    out_shape = []
    for columns, on in GROUPS:
        most = (ROWS if on is None else NZ) * NZ * len(columns) + 128
        out_shape += [jax.ShapeDtypeStruct((size,), jnp.int32) for size in (1, most, most)]
    flat = pl.pallas_call(
        tiles_kernel,
        out_shape=tuple(out_shape),
        in_specs=in_smem(1),
        out_specs=tuple(in_smem(len(out_shape))),
        compiler_params=pltpu.CompilerParams(vmem_limit_bytes=4 * MIB),
        cost_estimate=pl.CostEstimate(flops=10**6, bytes_accessed=10**5, transcendentals=0),
    )(frame_mask)
    return [tuple(flat[3 * i : 3 * i + 3]) for i in range(len(GROUPS))]


def local(queries, keys, values, frame_mask, w_out):
    xl, c = lax.axis_index("xl"), lax.axis_index("c")

    width = w_out.shape[1] // (XL * NC)

    def w_columns(w, to_xl, to_c):
        return lax.dynamic_slice(w, (0, (to_xl * NC + to_c) * width), (w.shape[0], width))

    slots = split(queries, keys, values)
    slots, w_out = lax.optimization_barrier((slots, w_out))
    w_own = [w_columns(w_out, to_xl, c) for to_xl in (1 - xl, xl)]
    w_sent = [w_columns(w_out, to_xl, 1 - c) for to_xl in (1 - xl, xl)]
    w_own, w_sent, frame_mask = lax.optimization_barrier((w_own, w_sent, frame_mask))
    w_here = [lax.ppermute(w, "c", shift(NC, 1)) for w in w_sent]
    groups = live_tiles(frame_mask)

    slots = lax.all_to_all(slots, "z", 0, 0, tiled=True)
    slots, w_own, groups = lax.optimization_barrier((slots, w_own, groups))
    low, high = slots[: NZ // 2, BLOCK:], slots[NZ // 2 :, BLOCK:]
    slots, low, high = lax.optimization_barrier((slots, low, high))
    before_low = lax.ppermute(low, "y", shift(NY, 1))
    after_high = lax.ppermute(high, "y", shift(NY, -1))
    slots, late_low, late_high, w_here = lax.optimization_barrier((slots, low, high, w_here))
    query = slots[:, :BLOCK]
    query = (query, lax.ppermute(query, "xh", shift(XH, 1)))
    before_high = lax.ppermute(late_high, "y", shift(NY, 1))
    after_low = lax.ppermute(late_low, "y", shift(NY, -1))
    far_low = lax.ppermute(before_low, "y", shift(NY, 1))
    far_high = lax.ppermute(after_high, "y", shift(NY, -1))
    state = attend(groups[0], query, [low, high], None)
    state = attend(groups[1], query, [before_low, before_high, after_low, after_high], state)
    far_parts = [far_low, far_high]
    sent, sent_stats = attend_last(groups[2], query[1], far_parts, state, False)
    sent, sent_stats, state = lax.optimization_barrier((sent, sent_stats, state))
    there = lax.ppermute(sent, "xh", shift(XH, 1))
    there_stats = lax.ppermute(sent_stats, "xh", shift(XH, 1))
    here, here_stats = attend_last(groups[3], query[0], far_parts, state, True)
    heads = merge(here, here_stats, there, there_stats)
    heads = lax.all_to_all(heads, "z", 0, 0, tiled=True)[:HEADS]
    heads_core = lax.ppermute(heads, "c", shift(NC, 1))
    far_own = project(heads, w_own[0], None, 0, width, jnp.float32)
    early = width // TILE_N // 2 * TILE_N
    far = [
        lax.ppermute(
            project(heads_core, w_here[0], far_own, first, columns, jnp.bfloat16),
            "xl",
            shift(XL, 1),
        )
        for first, columns in ((0, early), (early, width - early))
    ]
    near = project(heads, w_own[1], None, 0, width, jnp.float32)
    near = project(heads_core, w_here[1], near, 0, width, jnp.float32)
    return add(near, far)


def solution(mesh):
    fine = Mesh(mesh.devices.reshape(XH, NZ, NY, XL, NC), ("xh", "z", "y", "xl", "c"))
    seq, head = ("xh", "z", "y"), ("xl", "c")
    in_specs = (P(seq, head), P(seq, head), P(seq, head), P(), P(head, None))
    return jax.shard_map(
        local, mesh=fine, in_specs=in_specs, out_specs=P(seq, head), check_vma=False
    )
```

```python
import jax
import jax.numpy as jnp
from jax import lax
from jax.experimental import pallas as pl
from jax.experimental.pallas import tpu as pltpu
from jax.sharding import Mesh
from jax.sharding import PartitionSpec as P

HEAD_DIM = 128
BLOCK = 128
HEADS = 5
XH, NZ, NY, XL, NC = 2, 8, 4, 2, 2
ROWS = XH * NZ
UNROLL = 8
TILE_N = 256
LOW = -1e30
EXP2_SCALE = HEAD_DIM ** (-0.5) * 1.4426950408889634
MIB = 1024 * 1024


def shift(size, by):
    return [(i, (i + by) % size) for i in range(size)]


def in_vmem(count):
    return [pl.BlockSpec(memory_space=pltpu.VMEM)] * count


def in_smem(count):
    return [pl.BlockSpec(memory_space=pltpu.SMEM)] * count


def split_kernel(q_hbm, k_hbm, v_hbm, slots_hbm, whole_ref, out_ref, sems):
    loads = [
        pltpu.make_async_copy(source, whole_ref.at[t], sems.at[t])
        for t, source in enumerate((q_hbm, k_hbm, v_hbm))
    ]
    for load in loads:
        load.start()
    for t, load in enumerate(loads):
        load.wait()
        for head in range(HEADS):
            lanes = slice(head * HEAD_DIM, (head + 1) * HEAD_DIM)
            out_ref[head, t * BLOCK : (t + 1) * BLOCK, :] = whole_ref[t, :, lanes]
    out = pltpu.make_async_copy(out_ref, slots_hbm.at[:HEADS], sems.at[3])
    out.start()
    out.wait()


def split(queries, keys, values):
    anywhere = pl.BlockSpec(memory_space=pl.ANY)
    part = (3 * BLOCK, HEAD_DIM)
    return pl.pallas_call(
        split_kernel,
        out_shape=jax.ShapeDtypeStruct((NZ,) + part, jnp.bfloat16),
        in_specs=[anywhere] * 3,
        out_specs=anywhere,
        scratch_shapes=[
            pltpu.VMEM((3,) + queries.shape, jnp.bfloat16),
            pltpu.VMEM((HEADS,) + part, jnp.bfloat16),
            pltpu.SemaphoreType.DMA((4,)),
        ],
        compiler_params=pltpu.CompilerParams(vmem_limit_bytes=56 * MIB),
    )(queries, keys, values)


def score_tiles(unroll, count, tables, q_ref, kv_ref, s_ref, top_ref):
    block_ref, slot_ref = tables

    def score(step, carry):
        tiles = []
        for u in range(unroll):
            e = step * unroll + u
            s = lax.dot_general(
                q_ref[block_ref[e]],
                kv_ref[slot_ref[e], :BLOCK, :],
                (((1,), (1,)), ((), ())),
                preferred_element_type=jnp.float32,
            )
            s = jnp.where(e < count, s, LOW)
            s_ref[e] = s
            tiles.append(s)
        for u in range(unroll):
            block = block_ref[step * unroll + u]
            top_ref[block] = jnp.maximum(top_ref[block], tiles[u])
        return carry

    lax.fori_loop(0, (count + (unroll - 1)) // unroll, score, 0)


def mix_tiles(unroll, count, tables, kv_ref, s_ref, m_ref, l_ref, a_ref):
    block_ref, slot_ref = tables

    def mix(step, carry):
        weights, products = [], []
        for u in range(unroll):
            e = step * unroll + u
            weight = jnp.exp2((s_ref[e] - m_ref[block_ref[e]]) * EXP2_SCALE)
            weights.append(weight)
            products.append(
                jnp.dot(
                    weight.astype(jnp.bfloat16),
                    kv_ref[slot_ref[e], BLOCK:, :],
                    preferred_element_type=jnp.float32,
                )
            )
        for u in range(unroll):
            block = block_ref[step * unroll + u]
            l_ref[block] = l_ref[block] + weights[u]
            a_ref[block] = a_ref[block] + products[u]
        return carry

    lax.fori_loop(0, (count + (unroll - 1)) // unroll, mix, 0)


def stats_of(m_ref, l_ref):
    lane = lax.broadcasted_iota(jnp.int32, (BLOCK, BLOCK), 1)
    stats = jnp.zeros((BLOCK, BLOCK), jnp.float32)
    for i in range(NZ):
        total = jnp.sum(l_ref[i], axis=1, keepdims=True)
        stats = jnp.where(lane == i, m_ref[i], stats)
        stats = jnp.where(lane == NZ + i, total, stats)
    return stats


def hold_parts(parts, kv_ref):
    at = 0
    for part in parts:
        kv_ref[at : at + part.shape[0]] = part[...]
        at += part.shape[0]


def attend_last(tables, query, parts, state, mine):
    slots = sum(part.shape[0] for part in parts)
    unroll = UNROLL if mine else UNROLL // 2

    def kernel(count_ref, block_ref, slot_ref, q_ref, *refs):
        part_refs, refs = refs[: len(parts)], refs[len(parts) :]
        (m_in, l_in, a_in), refs = refs[:3], refs[3:]
        sums_ref, stats_ref, kv_ref, s_ref, top_ref, m_ref, l_ref, a_ref = refs
        tables = (block_ref, slot_ref)
        plane = lax.axis_index("xh")
        first = (plane if mine else 1 - plane) * NZ
        hold_parts(part_refs, kv_ref)
        count = count_ref[0]
        top_ref[...] = jnp.full(top_ref.shape, LOW, jnp.float32)
        score_tiles(unroll, count, tables, q_ref, kv_ref, s_ref, top_ref)
        for i in range(NZ):
            top = jnp.max(top_ref[i], axis=1, keepdims=True)
            old = m_in[first + i]
            new = jnp.maximum(old, top)
            fade = jnp.exp2((old - new) * EXP2_SCALE)
            m_ref[i] = new
            l_ref[i] = l_in[first + i] * fade
            a_ref[i] = a_in[first + i] * fade
        mix_tiles(unroll, count, tables, kv_ref, s_ref, m_ref, l_ref, a_ref)
        sums_ref[...] = a_ref[...].astype(sums_ref.dtype)
        stats = stats_of(m_ref, l_ref)
        stats_ref[...] = stats if mine else stats.T[: 2 * NZ]

    half = pltpu.VMEM((NZ, BLOCK, BLOCK), jnp.float32)
    return pl.pallas_call(
        kernel,
        out_shape=(
            jax.ShapeDtypeStruct((NZ, BLOCK, HEAD_DIM), jnp.float32 if mine else jnp.bfloat16),
            jax.ShapeDtypeStruct((BLOCK if mine else 2 * NZ, BLOCK), jnp.float32),
        ),
        in_specs=in_smem(3) + in_vmem(1 + len(parts) + 3),
        out_specs=tuple(in_vmem(2)),
        scratch_shapes=[
            pltpu.VMEM((slots, 2 * BLOCK, HEAD_DIM), jnp.bfloat16),
            pltpu.VMEM((NZ * slots, BLOCK, BLOCK), jnp.float32),
            half,
            half,
            half,
            half,
        ],
        compiler_params=pltpu.CompilerParams(vmem_limit_bytes=28 * MIB),
        cost_estimate=pl.CostEstimate(
            flops=20 * 2 * 128**3, bytes_accessed=3 * MIB, transcendentals=10 * 128 * 128
        ),
    )(*tables, query, *parts, *state)


def attend(tables, query, parts, state):
    first = state is None
    unroll = UNROLL if first else 2 * UNROLL
    slots = sum(part.shape[0] for part in parts)
    whole = jax.ShapeDtypeStruct((ROWS, BLOCK, BLOCK), jnp.float32)

    def kernel(count_ref, block_ref, slot_ref, own_ref, other_ref, *refs):
        tables = (block_ref, slot_ref)
        plane = lax.axis_index("xh")
        part_refs, refs = refs[: len(parts)], refs[len(parts) :]
        if not first:
            (m_in, l_in, a_in), refs = refs[:3], refs[3:]
        m_ref, l_ref, a_ref, q_ref, kv_ref, s_ref, top_ref = refs
        q_ref[pl.ds(plane * NZ, NZ)] = own_ref[...]
        q_ref[pl.ds((1 - plane) * NZ, NZ)] = other_ref[...]
        hold_parts(part_refs, kv_ref)
        count = count_ref[0]
        top_ref[...] = jnp.full(top_ref.shape, LOW, jnp.float32)
        score_tiles(unroll, count, tables, q_ref, kv_ref, s_ref, top_ref)
        for block in range(ROWS):
            top = jnp.max(top_ref[block], axis=1, keepdims=True)
            if first:
                m_ref[block] = jnp.broadcast_to(top, (BLOCK, BLOCK))
                l_ref[block] = jnp.zeros((BLOCK, BLOCK), jnp.float32)
                a_ref[block] = jnp.zeros((BLOCK, HEAD_DIM), jnp.float32)
            else:
                new = jnp.maximum(m_in[block], top)
                fade = jnp.exp2((m_in[block] - new) * EXP2_SCALE)
                m_ref[block] = new
                l_ref[block] = l_in[block] * fade
                a_ref[block] = a_in[block] * fade
        mix_tiles(unroll, count, tables, kv_ref, s_ref, m_ref, l_ref, a_ref)

    return pl.pallas_call(
        kernel,
        out_shape=(whole, whole, whole),
        in_specs=in_smem(3) + in_vmem(2 + len(parts) + (0 if first else 3)),
        out_specs=tuple(in_vmem(3)),
        scratch_shapes=[
            pltpu.VMEM((ROWS, BLOCK, HEAD_DIM), jnp.bfloat16),
            pltpu.VMEM((slots, 2 * BLOCK, HEAD_DIM), jnp.bfloat16),
            pltpu.VMEM((ROWS * slots, BLOCK, BLOCK), jnp.float32),
            pltpu.VMEM((ROWS, BLOCK, BLOCK), jnp.float32),
        ],
        compiler_params=pltpu.CompilerParams(vmem_limit_bytes=28 * MIB),
        cost_estimate=pl.CostEstimate(
            flops=len(parts) * 40 * 2 * 128**3,
            bytes_accessed=6 * MIB,
            transcendentals=20 * 128 * 128,
        ),
    )(*tables, *query, *parts, *(() if first else state))


def merge_kernel(here_ref, here_stats_ref, there_ref, there_stats_ref, out_ref, rows_ref):
    rows_ref[: 2 * NZ, :] = there_stats_ref[...]
    rows_ref[2 * NZ :, :] = jnp.zeros((BLOCK - 2 * NZ, BLOCK), jnp.float32)
    here, there = here_stats_ref[...], rows_ref[...].T
    for i in range(NZ):
        m0, m1 = here[:, i : i + 1], there[:, i : i + 1]
        l0, l1 = here[:, NZ + i : NZ + i + 1], there[:, NZ + i : NZ + i + 1]
        m = jnp.maximum(m0, m1)
        f0 = jnp.exp2((m0 - m) * EXP2_SCALE)
        f1 = jnp.exp2((m1 - m) * EXP2_SCALE)
        mixed = here_ref[i] * f0 + there_ref[i].astype(jnp.float32) * f1
        out_ref[i] = (mixed / (l0 * f0 + l1 * f1)).astype(jnp.bfloat16)


def merge(here, here_stats, there, there_stats):
    return pl.pallas_call(
        merge_kernel,
        out_shape=jax.ShapeDtypeStruct(here.shape, jnp.bfloat16),
        in_specs=in_vmem(4),
        out_specs=in_vmem(1)[0],
        scratch_shapes=[pltpu.VMEM((BLOCK, BLOCK), jnp.float32)],
        compiler_params=pltpu.CompilerParams(vmem_limit_bytes=4 * MIB),
    )(here, here_stats, there, there_stats)


def project(heads, w, added, first, width, dtype):
    deep = w.shape[0]
    tiles = width // TILE_N

    def kernel(heads_ref, w_hbm, *refs):
        if added is not None:
            added_ref, refs = refs[0], refs[1:]
        out_ref, rows_ref, w_ref, sems = refs
        copies = []
        for tile in range(tiles):
            lanes = pl.ds(first + tile * TILE_N, TILE_N)
            copies.append(
                pltpu.make_async_copy(w_hbm.at[:, lanes], w_ref.at[tile], sems.at[tile])
            )
            copies[-1].start()
        for head in range(HEADS):
            at = head * HEAD_DIM
            rows_ref[:, at : at + HEAD_DIM] = heads_ref[head]
        for tile in range(tiles):
            copies[tile].wait()
            at = tile * TILE_N
            out = jnp.dot(rows_ref[...], w_ref[tile], preferred_element_type=jnp.float32)
            if added is not None:
                out = out + added_ref[:, first + at : first + at + TILE_N]
            out_ref[:, at : at + TILE_N] = out.astype(out_ref.dtype)

    return pl.pallas_call(
        kernel,
        out_shape=jax.ShapeDtypeStruct((BLOCK, width), dtype),
        in_specs=in_vmem(1)
        + [pl.BlockSpec(memory_space=pl.ANY)]
        + in_vmem(0 if added is None else 1),
        out_specs=in_vmem(1)[0],
        scratch_shapes=[
            pltpu.VMEM((BLOCK, deep), jnp.bfloat16),
            pltpu.VMEM((tiles, deep, TILE_N), jnp.bfloat16),
            pltpu.SemaphoreType.DMA((tiles,)),
        ],
        compiler_params=pltpu.CompilerParams(vmem_limit_bytes=8 * MIB),
        cost_estimate=pl.CostEstimate(
            flops=2 * BLOCK * deep * width, bytes_accessed=2 * MIB, transcendentals=0
        ),
    )(heads, w, *(() if added is None else (added,)))


def add_kernel(near_ref, *refs):
    out_ref = refs[-1]
    at = 0
    for far_ref in refs[:-1]:
        lanes = slice(at, at + far_ref.shape[1])
        out = near_ref[:, lanes] + far_ref[...].astype(jnp.float32)
        out_ref[:, lanes] = out.astype(out_ref.dtype)
        at += far_ref.shape[1]


def add(near, far):
    return pl.pallas_call(
        add_kernel,
        out_shape=jax.ShapeDtypeStruct(near.shape, jnp.bfloat16),
        in_specs=in_vmem(1 + len(far)),
        out_specs=in_vmem(1)[0],
        compiler_params=pltpu.CompilerParams(vmem_limit_bytes=4 * MIB),
    )(near, *far)


GROUPS = (((0,), None), ((1, 3), None), ((2,), 1), ((2,), 0))


def tiles_kernel(mask_ref, *refs):
    y, plane = lax.axis_index("y"), lax.axis_index("xh")
    for group, (columns, on) in enumerate(GROUPS):
        count_ref, block_ref, slot_ref = refs[3 * group : 3 * group + 3]
        first_block = 0 if on is None else ((plane + on) & (XH - 1)) * NZ

        def one_query_block(
            block, at, columns=columns, refs=(block_ref, slot_ref), first_block=first_block
        ):
            block_ref, slot_ref = refs
            row = (first_block + block) * NY + y
            for column, back in enumerate(columns):
                first = plane * (NZ * NY) + ((y - back + NY) & (NY - 1))
                for i in range(NZ):
                    block_ref[at] = block
                    slot_ref[at] = column * NZ + i
                    at = at + jnp.where(mask_ref[row, first + i * NY] != 0, 1, 0)
            return at

        total = lax.fori_loop(0, ROWS if on is None else NZ, one_query_block, jnp.int32(0))
        count_ref[0] = total
        for u in range(2 * UNROLL):
            block_ref[total + u] = 0
            slot_ref[total + u] = 0


def live_tiles(frame_mask):
    out_shape = []
    for columns, on in GROUPS:
        most = (ROWS if on is None else NZ) * NZ * len(columns) + 128
        out_shape += [jax.ShapeDtypeStruct((size,), jnp.int32) for size in (1, most, most)]
    flat = pl.pallas_call(
        tiles_kernel,
        out_shape=tuple(out_shape),
        in_specs=in_smem(1),
        out_specs=tuple(in_smem(len(out_shape))),
        compiler_params=pltpu.CompilerParams(vmem_limit_bytes=4 * MIB),
        cost_estimate=pl.CostEstimate(flops=10**6, bytes_accessed=10**5, transcendentals=0),
    )(frame_mask)
    return [tuple(flat[3 * i : 3 * i + 3]) for i in range(len(GROUPS))]


def local(queries, keys, values, frame_mask, w_out):
    xl, c = lax.axis_index("xl"), lax.axis_index("c")

    width = w_out.shape[1] // (XL * NC)

    def w_columns(w, to_xl, to_c):
        return lax.dynamic_slice(w, (0, (to_xl * NC + to_c) * width), (w.shape[0], width))

    slots = split(queries, keys, values)
    slots, w_out = lax.optimization_barrier((slots, w_out))
    w_own = [w_columns(w_out, to_xl, c) for to_xl in (1 - xl, xl)]
    w_sent = [w_columns(w_out, to_xl, 1 - c) for to_xl in (1 - xl, xl)]
    w_own, w_sent, frame_mask = lax.optimization_barrier((w_own, w_sent, frame_mask))
    w_here = [lax.ppermute(w, "c", shift(NC, 1)) for w in w_sent]
    groups = live_tiles(frame_mask)

    slots = lax.all_to_all(slots, "z", 0, 0, tiled=True)
    slots, w_own, groups = lax.optimization_barrier((slots, w_own, groups))
    low, high = slots[: NZ // 2, BLOCK:], slots[NZ // 2 :, BLOCK:]
    slots, low, high = lax.optimization_barrier((slots, low, high))
    before_low = lax.ppermute(low, "y", shift(NY, 1))
    after_high = lax.ppermute(high, "y", shift(NY, -1))
    slots, late_low, late_high, w_here = lax.optimization_barrier((slots, low, high, w_here))
    query = slots[:, :BLOCK]
    query = (query, lax.ppermute(query, "xh", shift(XH, 1)))
    before_high = lax.ppermute(late_high, "y", shift(NY, 1))
    after_low = lax.ppermute(late_low, "y", shift(NY, -1))
    far_low = lax.ppermute(before_low, "y", shift(NY, 1))
    far_high = lax.ppermute(after_high, "y", shift(NY, -1))
    state = attend(groups[0], query, [low, high], None)
    state = attend(groups[1], query, [before_low, before_high, after_low, after_high], state)
    far_parts = [far_low, far_high]
    sent, sent_stats = attend_last(groups[2], query[1], far_parts, state, False)
    sent, sent_stats, state = lax.optimization_barrier((sent, sent_stats, state))
    there = lax.ppermute(sent, "xh", shift(XH, 1))
    there_stats = lax.ppermute(sent_stats, "xh", shift(XH, 1))
    here, here_stats = attend_last(groups[3], query[0], far_parts, state, True)
    heads = merge(here, here_stats, there, there_stats)
    heads = lax.all_to_all(heads, "z", 0, 0, tiled=True)[:HEADS]
    heads_core = lax.ppermute(heads, "c", shift(NC, 1))
    far_own = project(heads, w_own[0], None, 0, width, jnp.float32)
    early = width // TILE_N // 2 * TILE_N
    far = [
        lax.ppermute(
            project(heads_core, w_here[0], far_own, first, columns, jnp.bfloat16),
            "xl",
            shift(XL, 1),
        )
        for first, columns in ((0, early), (early, width - early))
    ]
    near = project(heads, w_own[1], None, 0, width, jnp.float32)
    near = project(heads_core, w_here[1], near, 0, width, jnp.float32)
    return add(near, far)


def solution(mesh):
    fine = Mesh(mesh.devices.reshape(XH, NZ, NY, XL, NC), ("xh", "z", "y", "xl", "c"))
    seq, head = ("xh", "z", "y"), ("xl", "c")
    in_specs = (P(seq, head), P(seq, head), P(seq, head), P(), P(head, None))
    return jax.shard_map(
        local, mesh=fine, in_specs=in_specs, out_specs=P(seq, head), check_vma=False
    )
```
